32 devices in a mesh: dp: 8 (over z, core), tensor: 4 (over y, x).
Axes of the slice: x: 2, y: 2, z: 4, core: 2. Of those that a mesh axis runs over, the one named last changes fastest.
Arguments:
- inputs: float32 [8192, 1024], P(('dp', 'tensor')), may hold values from -6 to 6
- teacher: float32 [8192, 1024], P(('dp', 'tensor')), may hold values from -6 to 6
- valid_mask: int32 [8, 1024], P('dp'), may hold values from 0 to 1, as said below
- documents: int32 [8, 1024], P('dp'), may hold values from 0 to 3, never falling along the last dimension, each value on 1 to 512 neighbouring positions
- picture_starts: int32 [8, 2], P('dp'), may hold values from 0 to 768, as said below
- w_query: bfloat16 [1024, 1024], P('dp', 'tensor'), may hold values from -0.25 to 0.25
- w_key: bfloat16 [1024, 1024], P('dp', 'tensor'), may hold values from -0.25 to 0.25
- w_value: bfloat16 [1024, 1024], P('dp', 'tensor'), may hold values from -0.1875 to 0.1875
- w_out: bfloat16 [1024, 1024], P('tensor', 'dp'), may hold values from -0.75 to 0.75
- w_gate: bfloat16 [1024, 2816], P('dp', 'tensor'), may hold values from -0.1875 to 0.1875
- w_up: bfloat16 [1024, 2816], P('dp', 'tensor'), may hold values from -0.1875 to 0.1875
- w_down: bfloat16 [2816, 1024], P('tensor', 'dp'), may hold values from -0.109375 to 0.109375
Outputs:
- output: float32 [8192, 1024], P(('dp', 'tensor'))
- loss_value: float32 [], replicated
- grad_inputs: float32 [8192, 1024], P(('dp', 'tensor'))
- grad_query: float32 [1024, 1024], P('dp', 'tensor')
- grad_key: float32 [1024, 1024], P('dp', 'tensor')
- grad_value: float32 [1024, 1024], P('dp', 'tensor')
- grad_out: float32 [1024, 1024], P('tensor', 'dp')
- grad_gate: float32 [1024, 2816], P('dp', 'tensor')
- grad_up: float32 [1024, 2816], P('dp', 'tensor')
- grad_down: float32 [2816, 1024], P('tensor', 'dp')
The draws below stay inside these ranges and needn't reach their ends.
Inputs may be any that keep to these rules, and one draw needn't show every extreme that they name: `valid_mask`: position 0 of every sequence is valid. `documents`: ids never fall along a sequence; each document has 1 to 512 tokens. `picture_starts`: piece p of a sequence starts between p * 512 and p * 512 + 1024 / 2 - 256, so the pieces of a sequence never intersect.
All inputs are finite; a program needn't handle non-finite values.
Results may differ from the reference program's by a relative error of at most 0.017.
Values may be sent and summed in bfloat16 or wider, within the bound.
A program may use at most 128 MiB of HBM per device.

```python
import math
import jax
import jax.numpy as jnp
import numpy as np
from jax import lax

D = 1024
HEADS = 16
HD = 64
FF = 2816
LEN = 1024
PIECE = 256
NPIC = 2
DOCS = 4
NSEQ = 8
TOKENS = 8192


def draw_valid_mask(key, part):
    seq_index = jnp.arange(NSEQ, dtype=jnp.int32)[:, None]
    pos_index = jnp.arange(LEN, dtype=jnp.int32)[None, :]
    seq_level = 300 + 700 * seq_index // max(NSEQ - 1, 1)
    pos_level = 350 + 650 * pos_index // max(LEN - 1, 1)
    threshold = seq_level * pos_level // 1000
    rolled = jax.random.randint(key, (NSEQ, LEN), 0, 1000, dtype=jnp.int32)
    return jnp.where((rolled < threshold) | (pos_index == 0), 1, 0).astype(jnp.int32)


def draw_picture_starts(key, part):
    slot_len = LEN // NPIC
    spare = slot_len - PIECE
    offsets = jax.random.randint(key, (NSEQ, NPIC), 0, spare + 1, dtype=jnp.int32)
    seq_index = jnp.arange(NSEQ, dtype=jnp.int32)[:, None]
    pic_index = jnp.arange(NPIC, dtype=jnp.int32)[None, :]
    forced = jnp.where(pic_index == NPIC - 1, spare, 0)
    offsets = jnp.where(seq_index == 0, forced, offsets)
    return (pic_index * slot_len + offsets).astype(jnp.int32)


def block_scale(rng, dims, split, least, largest):
    level = 1.0
    for axis_at, parts in split:
        steps = jax.random.uniform(jax.random.fold_in(jax.random.fold_in(rng, 6), axis_at), (parts,), jnp.float32, least / len(split), largest / len(split))
        level = level * jnp.repeat(jnp.exp(steps), dims[axis_at] // parts).reshape((-1,) + (1,) * (len(dims) - 1 - axis_at))
    return level


def length_profile(count, total, reach, skew):
    weights = [(1 << 20) // math.isqrt(rank ** skew) + 1 for rank in range(2, count + 1)]
    spare, holding = total - reach - (count - 1), [1] * (count - 1)
    while spare > 0:
        candidates = [i for i in range(count - 1) if holding[i] < reach]
        mass, remaining = sum([weights[i] for i in candidates]), spare
        for i in candidates:
            extra = min(reach - holding[i], max(1, remaining * weights[i] // mass), spare)
            holding[i] = holding[i] + extra
            spare = spare - extra
    return np.array([reach] + holding)


def ragged_sizes(key, number_of, total, reach, lean):
    if number_of == 2:
        one = jax.random.randint(key, (), max(1, total - reach), min(reach, total - 1) + 1)
        return jnp.stack([one, total - one])
    lengths = jnp.asarray(length_profile(number_of, total, reach, lean), jnp.int32)
    pairs = (number_of - 1) // 2
    donor, taker = lengths[1:1 + 2 * pairs:2], lengths[2:2 + 2 * pairs:2]
    slack = jnp.minimum(donor - 1, reach - taker)
    shifted = jax.random.randint(jax.random.fold_in(key, 1), (pairs,), 0, 1 << 20) % (slack + 1)
    lengths = lengths.at[1:1 + 2 * pairs:2].set(donor - shifted).at[2:2 + 2 * pairs:2].set(taker + shifted)
    return lengths[jax.random.permutation(jax.random.fold_in(key, 2), number_of)]


def bell_draw(stream_key, dims, spread, limit, shards=(), held_as=jnp.bfloat16):
    entries = spread * jax.random.normal(stream_key, dims, jnp.float32)
    if shards:
        entries = entries * block_scale(stream_key, dims, shards, -0.22, 0.18)
    return jnp.clip(entries, -limit, limit).astype(held_as)


def setup_inputs(seed: int = 0) -> dict:
    keys = jax.random.split(jax.random.key(seed), 13)
    inputs = bell_draw(keys[0], (TOKENS, D), 1.0, 6.0, ((0, 32),), jnp.float32)
    teacher = bell_draw(keys[1], (TOKENS, D), 1.0, 6.0, ((0, 32),), jnp.float32)
    valid_mask = draw_valid_mask(jax.random.fold_in(keys[12], 71), 0)
    documents = jax.vmap(lambda own: jnp.searchsorted(jnp.cumsum(ragged_sizes(own, DOCS, LEN, LEN // 2, 0)), jnp.arange(LEN), side="right"))(jax.random.split(keys[3], NSEQ)).reshape((NSEQ, LEN)).astype(jnp.int32)
    picture_starts = draw_picture_starts(jax.random.fold_in(keys[12], 71), 0)
    w_query = bell_draw(keys[5], (D, D), (D // 2) ** -0.5, 0.25, ((0, 8), (1, 4)))
    w_key = bell_draw(keys[6], (D, D), (D // 2) ** -0.5, 0.25, ((0, 8), (1, 4)))
    w_value = bell_draw(keys[7], (D, D), D ** -0.5, 0.1875, ((0, 8), (1, 4)))
    w_out = bell_draw(keys[8], (D, D), (D // 16) ** -0.5, 0.75, ((0, 4), (1, 8)))
    w_gate = bell_draw(keys[9], (D, FF), D ** -0.5, 0.1875, ((0, 8), (1, 4)))
    w_up = bell_draw(keys[10], (D, FF), D ** -0.5, 0.1875, ((0, 8), (1, 4)))
    w_down = bell_draw(keys[11], (FF, D), FF ** -0.5, 0.109375, ((0, 4), (1, 8)))
    return dict(inputs=inputs, teacher=teacher, valid_mask=valid_mask, documents=documents, picture_starts=picture_starts, w_query=w_query, w_key=w_key, w_value=w_value, w_out=w_out, w_gate=w_gate, w_up=w_up, w_down=w_down)


highest = lax.Precision.HIGHEST
norm_eps = 1e-05
masked_score = -1e+30

@jax.custom_vjp
def low(v):
    return lax.optimization_barrier(v.astype(jnp.bfloat16)).astype(jnp.float32)

@jax.custom_vjp
def low_back(v):
    return v

def low_keep(v):
    return (low(v), None)

def low_pass(kept, grad):
    return (grad,)

def back_keep(v):
    return (v, None)

def back_low(kept, grad):
    return (low(grad),)
low.defvjp(low_keep, low_pass)
low_back.defvjp(back_keep, back_low)

def layer_norm(values):
    centred = values - lax.optimization_barrier(jnp.mean(values, axis=-1, keepdims=True))
    return centred * lax.rsqrt(lax.optimization_barrier(jnp.mean(centred * centred, axis=-1, keepdims=True)) + norm_eps)

def rotary_tables(length, head_width):
    half_width = head_width // 2
    frequency = 10000.0 ** (-2.0 * jnp.arange(half_width, dtype=jnp.float32) / head_width)
    angles = jnp.arange(length, dtype=jnp.float32)[:, None] * frequency[None, :]
    cosine = jnp.cos(angles)
    sine_part = jnp.sin(angles)
    return (jnp.concatenate([cosine, cosine], axis=1), jnp.concatenate([sine_part, sine_part], axis=1))

def rotate(shaped, cosine, sine_part):
    half_width = shaped.shape[-1] // 2
    turned = jnp.concatenate([-shaped[..., half_width:], shaped[..., :half_width]], axis=-1)
    return shaped * cosine[None, :, None, :] + turned * sine_part[None, :, None, :]

def picture_ids(starts, length):
    positions = jnp.arange(length, dtype=jnp.int32)[None, :, None]
    inside = (positions >= starts[:, None, :]) & (positions < starts[:, None, :] + PIECE)
    labels = jnp.arange(1, starts.shape[1] + 1, dtype=jnp.int32)[None, None, :]
    return lax.optimization_barrier(jnp.sum(jnp.where(inside, labels, 0), axis=2)).astype(jnp.int32)

def allowed_block(doc_row, pic_row, valid_row, first_query, block_rows):
    query_pos = first_query + jnp.arange(block_rows, dtype=jnp.int32)
    key_pos = jnp.arange(doc_row.shape[0], dtype=jnp.int32)
    doc_query = lax.dynamic_slice_in_dim(doc_row, first_query, block_rows)
    pic_query = lax.dynamic_slice_in_dim(pic_row, first_query, block_rows)
    same_doc = doc_query[:, None] == doc_row[None, :]
    before = key_pos[None, :] <= query_pos[:, None]
    same_pic = (pic_query[:, None] == pic_row[None, :]) & (pic_query[:, None] > 0)
    itself = key_pos[None, :] == query_pos[:, None]
    usable = (valid_row[None, :] == 1) | itself
    return same_doc & (before | same_pic) & usable

def one_group(group_rows, valid_rows, doc_rows, pic_rows, weights):
    w_query, w_key, w_value, w_out, w_gate, w_up, w_down = weights
    group_seqs, length = doc_rows.shape
    cosine, sine_part = rotary_tables(length, HD)
    normed = low(layer_norm(group_rows))
    query_pre = low_back(jnp.dot(normed, w_query, precision=highest))
    key_pre = low_back(jnp.dot(normed, w_key, precision=highest))
    queries = low(rotate(query_pre.reshape(group_seqs, length, HEADS, HD), cosine, sine_part))
    keys_rot = low(rotate(key_pre.reshape(group_seqs, length, HEADS, HD), cosine, sine_part))
    values = low(low_back(jnp.dot(normed, w_value, precision=highest))).reshape(group_seqs, length, HEADS, HD)
    scores = low_back(HD ** (-0.5) * jnp.einsum('sqhd,skhd->shqk', queries, keys_rot, precision=highest))

    def mask_of(doc_row, pic_row, valid_row):
        return allowed_block(doc_row, pic_row, valid_row, 0, length)
    allowed = jax.vmap(mask_of)(doc_rows, pic_rows, valid_rows)
    masked = jnp.where(allowed[:, None], scores, masked_score)
    row_max = lax.optimization_barrier(jnp.max(masked, axis=3, keepdims=True))
    exponent = jnp.exp(masked - row_max)
    attn_probs = low(exponent / lax.optimization_barrier(jnp.sum(exponent, axis=3, keepdims=True)))
    mixed = jnp.einsum('shqk,skhd->sqhd', attn_probs, values, precision=highest)
    mixed = low(low_back(mixed)).reshape(group_seqs * length, HEADS * HD)
    middle = group_rows + low_back(jnp.dot(mixed, w_out, precision=highest))
    normed_two = low(layer_norm(middle))
    gate_pre = low_back(jnp.dot(normed_two, w_gate, precision=highest))
    up_proj = low_back(jnp.dot(normed_two, w_up, precision=highest))
    hidden = low(jax.nn.silu(gate_pre) * up_proj)
    return middle + low_back(jnp.dot(hidden, w_down, precision=highest))

def reference(inputs, teacher, valid_mask, documents, picture_starts, w_query, w_key, w_value, w_out, w_gate, w_up, w_down):
    weights = tuple([matrix.astype(jnp.float32) for matrix in (w_query, w_key, w_value, w_out, w_gate, w_up, w_down)])
    group_seqs = math.gcd(NSEQ, max(1, 2048 // LEN))
    groups = NSEQ // group_seqs
    pictures = picture_ids(picture_starts, LEN)
    valid_groups = valid_mask.reshape(groups, group_seqs, LEN)
    doc_groups = documents.reshape(groups, group_seqs, LEN)
    pic_groups = pictures.reshape(groups, group_seqs, LEN)

    def step_fn(weights_now, pieces):
        group_rows, valid_rows, doc_rows, pic_rows = pieces
        return (weights_now, one_group(group_rows, valid_rows, doc_rows, pic_rows, weights_now))

    def forward(rows_all, w_one, w_two, w_three, w_four, w_five, w_six, w_seven):
        weights_now = (w_one, w_two, w_three, w_four, w_five, w_six, w_seven)
        final_weights, outputs = lax.scan(jax.checkpoint(step_fn), weights_now, (rows_all.reshape(groups, group_seqs * LEN, D), valid_groups, doc_groups, pic_groups))
        return outputs.reshape(TOKENS, D)
    output, pullback = jax.vjp(forward, inputs, weights[0], weights[1], weights[2], weights[3], weights[4], weights[5], weights[6])
    valid_rows = valid_mask.reshape(TOKENS, 1).astype(jnp.float32)
    deviation = output - teacher
    valid_total = jnp.sum(valid_rows)
    loss_value = jnp.sum(valid_rows * deviation * deviation) / (D * valid_total)
    cotangent = valid_rows * deviation * (TOKENS / valid_total)
    gradients = pullback(cotangent)
    return (output, loss_value, gradients[0], gradients[1], gradients[2], gradients[3], gradients[4], gradients[5], gradients[6], gradients[7])
```

```python
import functools

import jax
import jax.numpy as jnp
import numpy as np
from jax import lax
from jax.experimental import pallas as pl
from jax.experimental.pallas import tpu as pltpu
from jax.sharding import PartitionSpec as P

MESH = pl.DeviceIdType.MESH
HD = 64
PIECE = 256
EPS = 1e-5
MASKED = -1e30
BF = jnp.bfloat16
F32 = jnp.float32
NT = (((1,), (1,)), ((), ()))
NN = (((1,), (0,)), ((), ()))


def dot(a, b, dims=NN):
    return lax.dot_general(a, b, dims, preferred_element_type=F32)


def eye(n):
    return (
        lax.broadcasted_iota(jnp.int32, (n, n), 0) == lax.broadcasted_iota(jnp.int32, (n, n), 1)
    ).astype(F32).astype(BF)


def turned(a):
    return dot(eye(a.shape[1]), a, NT).astype(BF)


def mean_of(v):
    return jnp.sum(v, axis=1, keepdims=True) * (1.0 / v.shape[1])


def normed(v):
    centred = v - mean_of(v)
    inv = lax.rsqrt(mean_of(centred * centred) + EPS)
    return centred * inv, inv


def normed_back(n, inv, g):
    return inv * (g - mean_of(g) - n * mean_of(g * n))


class Geo:
    def __init__(self, n_dp, n_t, tok_rows, d_model, cols, hid):
        self.n_dp, self.n_t, self.R, self.D, self.c, self.f = n_dp, n_t, tok_rows, d_model, cols, hid
        self.C = n_dp // 2
        self.S = tok_rows * n_t
        self.H = cols // HD
        self.Dn = d_model // n_dp
        self.square = n_t == 4

    def place(self):
        self.d = lax.axis_index("dp")
        self.t = lax.axis_index("tensor")
        self.chip = self.d // 2
        self.core = self.d % 2
        if self.square:
            self.tx = self.t + 1 - 2 * (self.t % 2)
            self.ty = (self.t + 2) % 4
            self.td = 3 - self.t
            self.to = [self.tx, self.ty]
            self.arrive = [self.t, self.tx, self.ty, self.td]
            self.leave = [self.td, self.tx, self.ty, self.t]
        else:
            n = self.n_t
            self.to = [(self.t + k) % n for k in range(1, n)]
            self.arrive = [(self.t + n - k) % n for k in range(n)]
            self.leave = [(self.t + k) % n for k in range(1, n)] + [self.t]
        self.sib = self.d + 1 - 2 * self.core
        return self

    def zto(self, k):
        return ((self.chip + k) % self.C) * 2 + self.core

    def zfrom(self, k):
        return ((self.chip + self.C - k) % self.C) * 2 + self.core

    def rows(self, blk, first=0, count=None):
        count = self.R if count is None else count
        return pl.ds(pl.multiple_of(blk * self.R + first, count), count)

    def wrows(self, d):
        return pl.ds(pl.multiple_of(d * self.Dn, self.Dn), self.Dn)

    def greet(self, tensor=True, dp=True):
        bar = pltpu.get_barrier_semaphore()
        out = [(self.d, p) for p in self.to] if tensor else []
        if dp:
            out += [(self.zto(k), self.t) for k in range(1, self.C)] + [(self.sib, self.t)]
        for dev in out:
            pl.semaphore_signal(bar, inc=1, device_id=dev, device_id_type=MESH)
        pl.semaphore_wait(bar, len(out))


class Comm:
    def __init__(self, send_sem, recv_sem, me):
        self.ss, self.rs, self.me = send_sem, recv_sem, me
        self.n = 0
        self.pending = []

    def slots(self, k):
        self.n += k
        return list(range(self.n - k, self.n))

    def _copy(self, slot, src, dst, dev):
        return pltpu.make_async_remote_copy(
            src_ref=src, dst_ref=dst, send_sem=self.ss.at[slot], recv_sem=self.rs.at[slot],
            device_id=dev, device_id_type=MESH,
        )

    def send(self, slot, src, dst, dev):
        copy = self._copy(slot, src, dst, dev)
        copy.start()
        self.pending.append(copy)

    def recv(self, slot, dst, dev):
        self._copy(slot, dst, dst, dev).wait_recv()

    def finish(self):
        for copy in self.pending:
            copy.wait_send()
        self.pending = []


class Gather:
    def __init__(self, geo, comm, buf):
        self.g, self.comm, self.buf = geo, comm, buf
        g = geo
        if g.square:
            self.sx, self.sy = comm.slots(3), comm.slots(3)
            h0, h1 = self.half(g.t, 0), self.half(g.t, 1)
            comm.send(self.sx[0], h0, h0, (g.d, g.tx))
            comm.send(self.sy[1], h1, h1, (g.d, g.ty))
            comm.send(self.sx[1], h1, h1, (g.d, g.tx))
            comm.send(self.sy[0], h0, h0, (g.d, g.ty))
        else:
            self.s = comm.slots(g.n_t - 1)
            own = buf.at[g.rows(g.t)]
            for k, peer in enumerate(g.to):
                comm.send(self.s[k], own, own, (g.d, peer))

    def half(self, blk, i):
        h = self.g.R // 2
        return self.buf.at[self.g.rows(blk, i * h, h)]

    def relay(self):
        g, comm = self.g, self.comm
        if g.square:
            a = self.half(g.tx, 0)
            comm.recv(self.sx[0], a, (g.d, g.tx))
            comm.send(self.sy[2], a, a, (g.d, g.ty))
            b = self.half(g.ty, 1)
            comm.recv(self.sy[1], b, (g.d, g.ty))
            comm.send(self.sx[2], b, b, (g.d, g.tx))

    def wait(self, i):
        g, comm = self.g, self.comm
        if i == 0:
            return
        if not g.square:
            comm.recv(self.s[i - 1], self.buf.at[g.rows(g.arrive[i])], (g.d, g.arrive[i]))
        elif i == 1:
            comm.recv(self.sx[1], self.half(g.tx, 1), (g.d, g.tx))
        elif i == 2:
            comm.recv(self.sy[0], self.half(g.ty, 0), (g.d, g.ty))
        else:
            comm.recv(self.sx[2], self.half(g.td, 1), (g.d, g.tx))
            comm.recv(self.sy[2], self.half(g.td, 0), (g.d, g.ty))


def scatter_scratch(g):
    h = g.R // 2
    if g.square:
        return [pltpu.VMEM((3, 2, h, g.D), BF), pltpu.VMEM((2, h, g.D), BF), pltpu.VMEM((2, h, g.D), BF), pltpu.VMEM((2, 2, h, g.D), BF)]
    return [pltpu.VMEM((g.n_t - 1, 2, h, g.D), BF), pltpu.VMEM((1, 8, 128), BF), pltpu.VMEM((1, 8, 128), BF), pltpu.VMEM((g.n_t - 1, 2, h, g.D), BF)]


class Scatter:
    def __init__(self, geo, comm, bufs):
        self.g, self.comm = geo, comm
        self.part, self.into, self.out, self.fin = bufs
        g = geo
        if g.square:
            self.sx, self.sy = comm.slots(3), comm.slots(3)
        else:
            self.s = comm.slots(g.n_t - 1)

    def give(self, i, value):
        g, comm = self.g, self.comm
        h = g.R // 2
        for j in range(2):
            self.part[i, j] = value[j * h : (j + 1) * h].astype(BF)
        if not g.square:
            comm.send(self.s[i], self.part.at[i], self.fin.at[i], (g.d, g.leave[i]))
        elif i == 0:
            comm.send(self.sx[0], self.part.at[0, 0], self.into.at[0], (g.d, g.tx))
            comm.send(self.sy[0], self.part.at[0, 1], self.into.at[1], (g.d, g.ty))
        elif i == 1:
            comm.send(self.sx[1], self.part.at[1, 0], self.fin.at[0, 0], (g.d, g.tx))
        else:
            comm.send(self.sy[1], self.part.at[2, 1], self.fin.at[1, 1], (g.d, g.ty))

    def relay(self):
        g, comm = self.g, self.comm
        if not g.square:
            return
        comm.recv(self.sx[0], self.into.at[0], (g.d, g.tx))
        self.out[0] = (self.into[0].astype(F32) + self.part[2, 0].astype(F32)).astype(BF)
        comm.send(self.sy[2], self.out.at[0], self.fin.at[1, 0], (g.d, g.ty))
        comm.recv(self.sy[0], self.into.at[1], (g.d, g.ty))
        self.out[1] = (self.into[1].astype(F32) + self.part[1, 1].astype(F32)).astype(BF)
        comm.send(self.sx[2], self.out.at[1], self.fin.at[0, 1], (g.d, g.tx))

    def total(self, own):
        g, comm = self.g, self.comm
        h = g.R // 2
        if g.square:
            comm.recv(self.sx[1], self.fin.at[0, 0], (g.d, g.tx))
            comm.recv(self.sy[1], self.fin.at[1, 1], (g.d, g.ty))
            comm.recv(self.sx[2], self.fin.at[0, 1], (g.d, g.tx))
            comm.recv(self.sy[2], self.fin.at[1, 0], (g.d, g.ty))
            count = 2
        else:
            count = g.n_t - 1
            for k in range(count):
                comm.recv(self.s[k], self.fin.at[k], (g.d, g.arrive[k + 1]))
        halves = []
        for j in range(2):
            v = own[j * h : (j + 1) * h]
            for k in range(count):
                v = v + self.fin[k, j].astype(F32)
            halves.append(v)
        return jnp.concatenate(halves, axis=0)


class WeightGather:
    def __init__(self, geo, comm, buf):
        self.g, self.comm, self.buf = geo, comm, buf
        g = geo
        self.sz, self.sc = comm.slots(g.C - 1), comm.slots(g.C)
        own = self.at(g.d)
        for k in range(1, g.C):
            comm.send(self.sz[k - 1], own, own, (g.zto(k), g.t))
        comm.send(self.sc[0], own, own, (g.sib, g.t))

    def at(self, d):
        return self.buf.at[:, self.g.wrows(d)]

    def wait(self):
        g, comm = self.g, self.comm
        for k in range(1, g.C):
            block = self.at(g.zfrom(k))
            comm.recv(self.sz[k - 1], block, (g.zfrom(k), g.t))
            comm.send(self.sc[k], block, block, (g.sib, g.t))
        for k in range(g.C):
            other = g.zfrom(k) + 1 - 2 * g.core
            comm.recv(self.sc[k], self.at(other), (g.sib, g.t))


def rotated(v, cosine, sine):
    n = v.shape[1]
    lower = lax.broadcasted_iota(jnp.int32, v.shape, 1) % HD < HD // 2
    swapped = jnp.where(lower, pltpu.roll(v, n - HD // 2, 1), pltpu.roll(v, HD // 2, 1))
    return v * cosine + swapped * sine


def head_lanes(v, h):
    lane = lax.broadcasted_iota(jnp.int32, v.shape, 1)
    keep = (lane >= h * HD) & (lane < (h + 1) * HD)
    return jnp.where(keep, v, jnp.zeros_like(v))


def bias_of(qinfo, kinfo, first, size, rows):
    shape = (size, rows)
    doc_q, pic_q = qinfo[0:1, :], qinfo[1:2, :]
    key_doc, pic_k, doc_k = kinfo[:, 0:1], kinfo[:, 1:2], kinfo[:, 2:3]
    key_pos = lax.broadcasted_iota(jnp.int32, shape, 0)
    query_pos = lax.broadcasted_iota(jnp.int32, shape, 1) + first
    before = key_pos <= query_pos
    open_ = (doc_q == key_doc) & (before | (pic_q == pic_k))
    ok = open_ | (key_pos == query_pos)
    return jnp.where(ok, 0.0, MASKED).astype(F32)


def k1_body(g, x, wq, wk, wv, wo, wg, wu, wd, cosine, sine, qinfo, kinfo,
            middle, rows, q, kk, v, mixed, probs, rinv, wa, wm, count,
            cnt, bias, vt, part, into, out, fin, ts, tr, zs, zr):
    g.place()
    R, S, c, H = g.R, g.S, g.c, g.H
    tc, zc = Comm(ts, tr, g), Comm(zs, zr, g)
    mine = g.wrows(g.d)
    wa[0, mine] = wq[...]
    wa[1, mine] = wk[...]
    wa[2, mine] = wv[...]
    wa[3, mine] = turned(wo[...])
    one, _ = normed(x[...])
    rows[g.rows(g.t)] = one.astype(BF)
    g.greet()
    ag = Gather(g, tc, rows)
    za = WeightGather(g, zc, wa)
    wm[0, mine] = wg[...]
    wm[1, mine] = wu[...]
    wm[2, mine] = turned(wd[...])
    zm = WeightGather(g, zc, wm)
    sc, sz = zc.slots(1)[0], zc.slots(g.C - 1)
    valid = jnp.sum(qinfo[2:3, :].astype(F32), axis=1, keepdims=True)
    cnt[0] = jnp.broadcast_to(valid, (8, 128))
    zc.send(sc, cnt.at[0], cnt.at[1], (g.sib, g.t))
    zc.recv(sc, cnt.at[1], (g.sib, g.t))
    cnt[2] = cnt[0] + cnt[1]
    for k in range(1, g.C):
        zc.send(sz[k - 1], cnt.at[2], cnt.at[2 + k], (g.zto(k), g.t))
    ag.relay()
    za.wait()
    for i in range(g.n_t):
        ag.wait(i)
        blk = g.rows(g.arrive[i])
        row = rows[blk]
        cos_b, sin_b = cosine[blk], sine[blk]
        q[blk] = (rotated(dot(row, wa[0]), cos_b, sin_b) * HD**-0.5).astype(BF)
        kk[blk] = rotated(dot(row, wa[1]), cos_b, sin_b).astype(BF)
        v[blk] = dot(row, wa[2]).astype(BF)
    vt[...] = turned(v[...])
    sca = Scatter(g, tc, (part, into, out, fin))
    for i, blk in enumerate(g.leave):
        bias[...] = bias_of(qinfo[:, g.rows(blk)], kinfo[...], blk * R, S, R)
        q_blk = q[g.rows(blk)]
        outs = []
        for h in range(H):
            s = dot(kk[...], head_lanes(q_blk, h), NT) + bias[...]
            e = jnp.exp(s - jnp.max(s, axis=0, keepdims=True))
            inv = 1.0 / jnp.sum(e, axis=0, keepdims=True)
            low = e.astype(BF)
            probs[blk, :, h * R : (h + 1) * R] = low
            rinv[blk, h : h + 1, :] = inv
            outs.append(dot(vt[h * HD : (h + 1) * HD, :], low) * inv)
        mix = jnp.concatenate(outs, axis=0).T.astype(BF)
        mixed[g.rows(blk)] = mix
        partial = dot(mix, wa[3], NT)
        if i < g.n_t - 1:
            sca.give(i, partial)
        else:
            middle[...] = x[...] + partial
    sca.relay()
    zm.wait()
    middle[...] = sca.total(middle[...])
    total = cnt[2]
    for k in range(1, g.C):
        zc.recv(sz[k - 1], cnt.at[2 + k], (g.zfrom(k), g.t))
        total = total + cnt[2 + k]
    count[...] = total
    tc.finish()
    zc.finish()


def vmem(*shape_dtype):
    return jax.ShapeDtypeStruct(*shape_dtype)


def call(body, g, name, outs, scratch, cid, args, sems=(24, 24)):
    whole = pl.BlockSpec(memory_space=pltpu.VMEM)
    return pl.pallas_call(
        functools.partial(body, g),
        name=name,
        out_shape=outs,
        in_specs=[whole] * len(args),
        out_specs=[whole] * len(outs),
        scratch_shapes=list(scratch) + [
            pltpu.SemaphoreType.DMA((sems[0],)), pltpu.SemaphoreType.DMA((sems[0],)),
            pltpu.SemaphoreType.DMA((sems[1],)), pltpu.SemaphoreType.DMA((sems[1],)),
        ],
        compiler_params=pltpu.CompilerParams(
            collective_id=cid, has_side_effects=True, vmem_limit_bytes=60 * 2**20
        ),
    )(*args)


def rotary(length, cols):
    half = HD // 2
    frequency = 10000.0 ** (-2.0 * np.arange(half) / HD)
    angle = np.arange(length)[:, None] * frequency[None, :]
    cosine = np.concatenate([np.cos(angle)] * 2, axis=1)
    sine = np.concatenate([-np.sin(angle), np.sin(angle)], axis=1)
    reps = cols // HD
    return (jnp.asarray(np.tile(cosine, (1, reps)), F32), jnp.asarray(np.tile(sine, (1, reps)), F32))


def mask_info(documents, picture_starts, valid_mask):
    length = documents.shape[1]
    at = jnp.arange(length, dtype=jnp.int32)
    starts = picture_starts[0]
    pic = jnp.zeros((length,), jnp.int32)
    for p in range(starts.shape[0]):
        pic = jnp.where((at >= starts[p]) & (at < starts[p] + PIECE), p + 1, pic)
    doc, valid = documents[0], valid_mask[0]
    zero = jnp.zeros_like(doc)
    qinfo = jnp.stack([doc, pic, valid, zero, zero, zero, zero, zero])
    kinfo = jnp.stack([jnp.where(valid == 1, doc, -1), jnp.where(pic > 0, pic, -1), doc], axis=1)
    return qinfo, kinfo


def forward_attention(g, inputs, qinfo, kinfo, tables, weights):
    S, R, D, c, f = g.S, g.R, g.D, g.c, g.f
    sds = jax.ShapeDtypeStruct
    outs = [sds((R, D), F32), sds((S, D), BF), sds((S, c), BF), sds((S, c), BF), sds((S, c), BF), sds((S, c), BF),
            sds((g.n_t, S, g.H * R), BF), sds((g.n_t, 8, R), F32), sds((4, D, c), BF), sds((3, D, f), BF), sds((8, 128), F32)]
    scratch = [pltpu.VMEM((g.C + 2, 8, 128), F32), pltpu.VMEM((S, R), F32), pltpu.VMEM((c, S), BF)] + scatter_scratch(g)
    return call(k1_body, g, "attention_forward", outs, scratch, 1, (inputs, *weights, *tables, qinfo, kinfo))


def gather_rows(block):
    return lax.all_gather(block, "tensor", axis=0, tiled=True)


def scatter_rows(partial_value):
    return lax.psum_scatter(partial_value.astype(BF), "tensor", scatter_dimension=0, tiled=True).astype(F32)


def rotated_back(v, cosine, sine):
    n = v.shape[1]
    lower = lax.broadcasted_iota(jnp.int32, v.shape, 1) % HD < HD // 2
    swapped = jnp.where(lower, jnp.roll(v, -(HD // 2), 1), jnp.roll(v, HD // 2, 1))
    return v * cosine - swapped * sine


def per_device(mesh_shape, inputs, teacher, valid_mask, documents, picture_starts,
               w_query, w_key, w_value, w_out, w_gate, w_up, w_down):
    n_dp, n_t = mesh_shape
    R, D = inputs.shape
    c, f = w_query.shape[1], w_gate.shape[1]
    g = Geo(n_dp, n_t, R, D, c, f)
    length = valid_mask.shape[1]
    tables = rotary(length, c)
    qinfo, kinfo = mask_info(documents, picture_starts, valid_mask)
    weights = (w_query, w_key, w_value, w_out, w_gate, w_up, w_down)
    middle, rows_one, q, kk, v, mixed, probs, rinv, wa, wm, count = forward_attention(g, inputs, qinfo, kinfo, tables, weights)
    tensor_rank = lax.axis_index("tensor")
    row_valid = lax.dynamic_slice_in_dim(valid_mask.reshape(-1), tensor_rank * R, R, 0).astype(F32)[:, None]
    valid_total = count[0, 0]
    one, inv_one = normed(inputs)
    two, inv_two = normed(middle)
    rows_two = gather_rows(two.astype(BF))
    gate_pre, up_proj = dot(rows_two, wm[0]), dot(rows_two, wm[1])
    sg = jax.nn.sigmoid(gate_pre)
    hidden = (gate_pre * sg * up_proj).astype(BF)
    output = middle + scatter_rows(dot(hidden, wm[2], NT))
    deviation = output - teacher
    error = lax.psum(jnp.sum(row_valid * deviation * deviation), ("dp", "tensor"))
    loss_value = error / (D * valid_total)
    cotangent = row_valid * deviation * (length * n_dp / valid_total)
    gm = gather_rows(cotangent.astype(BF))
    down_term = jnp.einsum("gd,gf->df", gm, hidden, preferred_element_type=F32)
    gh = dot(gm, wm[2])
    ggl = (gh * up_proj * sg * (1.0 + gate_pre * (1.0 - sg))).astype(BF)
    gul = (gh * gate_pre * sg).astype(BF)
    gate_term = jnp.einsum("gd,gf->df", rows_two, ggl, preferred_element_type=F32)
    up_term = jnp.einsum("gd,gf->df", rows_two, gul, preferred_element_type=F32)
    gr2 = dot(ggl, wm[0], NT) + dot(gul, wm[1], NT)
    grad_middle = cotangent + normed_back(two, inv_two, scatter_rows(gr2))
    ga = gather_rows(grad_middle.astype(BF))
    out_term = jnp.einsum("gd,gc->dc", ga, mixed, preferred_element_type=F32)
    gmix = dot(ga, wa[3]).astype(BF)
    H, S = g.H, g.S
    pt = (probs.astype(F32).reshape(n_t, S, H, R) * rinv[:, None, :H]).transpose(2, 0, 3, 1).reshape(H, S, S)
    gh_ = gmix.reshape(S, H, HD)
    dp_ = jnp.einsum("qhd,khd->hqk", gh_, v.reshape(S, H, HD), preferred_element_type=F32)
    ds = (pt * (dp_ - jnp.sum(pt * dp_, axis=2, keepdims=True))).astype(BF)
    dq = jnp.einsum("hqk,khd->qhd", ds, kk.reshape(S, H, HD), preferred_element_type=F32).reshape(S, c) * HD**-0.5
    dk = jnp.einsum("hqk,qhd->khd", ds, q.reshape(S, H, HD), preferred_element_type=F32).reshape(S, c)
    dv = jnp.einsum("hqk,qhd->khd", pt.astype(BF), gh_, preferred_element_type=F32).reshape(S, c)
    dq = rotated_back(dq, *tables).astype(BF)
    dk = rotated_back(dk, *tables).astype(BF)
    dv = dv.astype(BF)
    terms = [jnp.einsum("gd,gc->dc", rows_one, t_, preferred_element_type=F32) for t_ in (dq, dk, dv)] + [out_term, gate_term, up_term, down_term]
    gr1 = dot(dq, wa[0], NT) + dot(dk, wa[1], NT) + dot(dv, wa[2], NT)
    grads = [lax.psum_scatter(t_.astype(BF), "dp", scatter_dimension=0, tiled=True).astype(F32) for t_ in terms]
    grad_inputs = grad_middle + normed_back(one, inv_one, scatter_rows(gr1))
    gq, gk, gv, go, gg, gu, gd = grads
    return (output, loss_value, grad_inputs, gq, gk, gv, go.T, gg, gu, gd.T)


def solution(mesh):
    rows, pair = P(("dp", "tensor"), None), P("dp", None)
    cut, across = P("dp", "tensor"), P("tensor", "dp")
    return jax.shard_map(
        functools.partial(per_device, (mesh.shape["dp"], mesh.shape["tensor"])),
        mesh=mesh,
        in_specs=(rows, rows, pair, pair, pair, cut, cut, cut, across, cut, cut, across),
        out_specs=(rows, P(), rows, cut, cut, cut, across, cut, cut, across),
        check_vma=False,
    )
```

```python
import functools

import jax
import jax.numpy as jnp
import numpy as np
from jax import lax
from jax.experimental import pallas as pl
from jax.experimental.pallas import tpu as pltpu
from jax.sharding import PartitionSpec as P

MESH = pl.DeviceIdType.MESH
HD = 64
PIECE = 256
EPS = 1e-5
MASKED = -1e30
BF = jnp.bfloat16
F32 = jnp.float32
NT = (((1,), (1,)), ((), ()))
NN = (((1,), (0,)), ((), ()))


def dot(a, b, dims=NN):
    return lax.dot_general(a, b, dims, preferred_element_type=F32)


def eye(n):
    return (
        lax.broadcasted_iota(jnp.int32, (n, n), 0) == lax.broadcasted_iota(jnp.int32, (n, n), 1)
    ).astype(F32).astype(BF)


def turned(a):
    return dot(eye(a.shape[1]), a, NT).astype(BF)


def mean_of(v):
    return jnp.sum(v, axis=1, keepdims=True) * (1.0 / v.shape[1])


def normed(v):
    centred = v - mean_of(v)
    inv = lax.rsqrt(mean_of(centred * centred) + EPS)
    return centred * inv, inv


def normed_back(n, inv, g):
    return inv * (g - mean_of(g) - n * mean_of(g * n))


class Geo:
    def __init__(self, n_dp, n_t, tok_rows, d_model, cols, hid):
        self.n_dp, self.n_t, self.R, self.D, self.c, self.f = n_dp, n_t, tok_rows, d_model, cols, hid
        self.C = n_dp // 2
        self.S = tok_rows * n_t
        self.H = cols // HD
        self.Dn = d_model // n_dp
        self.square = n_t == 4

    def place(self):
        self.d = lax.axis_index("dp")
        self.t = lax.axis_index("tensor")
        self.chip = self.d // 2
        self.core = self.d % 2
        if self.square:
            self.tx = self.t + 1 - 2 * (self.t % 2)
            self.ty = (self.t + 2) % 4
            self.td = 3 - self.t
            self.to = [self.tx, self.ty]
            self.arrive = [self.t, self.tx, self.ty, self.td]
            self.leave = [self.td, self.tx, self.ty, self.t]
        else:
            n = self.n_t
            self.to = [(self.t + k) % n for k in range(1, n)]
            self.arrive = [(self.t + n - k) % n for k in range(n)]
            self.leave = [(self.t + k) % n for k in range(1, n)] + [self.t]
        self.sib = self.d + 1 - 2 * self.core
        return self

    def zto(self, k):
        return ((self.chip + k) % self.C) * 2 + self.core

    def zfrom(self, k):
        return ((self.chip + self.C - k) % self.C) * 2 + self.core

    def rows(self, blk, first=0, count=None):
        count = self.R if count is None else count
        return pl.ds(pl.multiple_of(blk * self.R + first, count), count)

    def wrows(self, d):
        return pl.ds(pl.multiple_of(d * self.Dn, self.Dn), self.Dn)

    def greet(self, tensor=True, dp=True):
        bar = pltpu.get_barrier_semaphore()
        out = [(self.d, p) for p in self.to] if tensor else []
        if dp:
            out += [(self.zto(k), self.t) for k in range(1, self.C)] + [(self.sib, self.t)]
        for dev in out:
            pl.semaphore_signal(bar, inc=1, device_id=dev, device_id_type=MESH)
        pl.semaphore_wait(bar, len(out))


class Comm:
    def __init__(self, send_sem, recv_sem, me):
        self.ss, self.rs, self.me = send_sem, recv_sem, me
        self.n = 0
        self.pending = []

    def slots(self, k):
        self.n += k
        return list(range(self.n - k, self.n))

    def _copy(self, slot, src, dst, dev):
        return pltpu.make_async_remote_copy(
            src_ref=src, dst_ref=dst, send_sem=self.ss.at[slot], recv_sem=self.rs.at[slot],
            device_id=dev, device_id_type=MESH,
        )

    def send(self, slot, src, dst, dev):
        copy = self._copy(slot, src, dst, dev)
        copy.start()
        self.pending.append(copy)

    def recv(self, slot, dst, dev):
        self._copy(slot, dst, dst, dev).wait_recv()

    def finish(self):
        for copy in self.pending:
            copy.wait_send()
        self.pending = []


class Gather:
    def __init__(self, geo, comm, buf):
        self.g, self.comm, self.buf = geo, comm, buf
        g = geo
        if g.square:
            self.sx, self.sy = comm.slots(3), comm.slots(3)
            h0, h1 = self.half(g.t, 0), self.half(g.t, 1)
            comm.send(self.sx[0], h0, h0, (g.d, g.tx))
            comm.send(self.sy[1], h1, h1, (g.d, g.ty))
            comm.send(self.sx[1], h1, h1, (g.d, g.tx))
            comm.send(self.sy[0], h0, h0, (g.d, g.ty))
        else:
            self.s = comm.slots(g.n_t - 1)
            own = buf.at[g.rows(g.t)]
            for k, peer in enumerate(g.to):
                comm.send(self.s[k], own, own, (g.d, peer))

    def half(self, blk, i):
        h = self.g.R // 2
        return self.buf.at[self.g.rows(blk, i * h, h)]

    def relay(self):
        g, comm = self.g, self.comm
        if g.square:
            a = self.half(g.tx, 0)
            comm.recv(self.sx[0], a, (g.d, g.tx))
            comm.send(self.sy[2], a, a, (g.d, g.ty))
            b = self.half(g.ty, 1)
            comm.recv(self.sy[1], b, (g.d, g.ty))
            comm.send(self.sx[2], b, b, (g.d, g.tx))

    def wait(self, i):
        g, comm = self.g, self.comm
        if i == 0:
            return
        if not g.square:
            comm.recv(self.s[i - 1], self.buf.at[g.rows(g.arrive[i])], (g.d, g.arrive[i]))
        elif i == 1:
            comm.recv(self.sx[1], self.half(g.tx, 1), (g.d, g.tx))
        elif i == 2:
            comm.recv(self.sy[0], self.half(g.ty, 0), (g.d, g.ty))
        else:
            comm.recv(self.sx[2], self.half(g.td, 1), (g.d, g.tx))
            comm.recv(self.sy[2], self.half(g.td, 0), (g.d, g.ty))


def scatter_scratch(g):
    h = g.R // 2
    if g.square:
        return [pltpu.VMEM((3, 2, h, g.D), BF), pltpu.VMEM((2, h, g.D), BF), pltpu.VMEM((2, h, g.D), BF), pltpu.VMEM((2, 2, h, g.D), BF)]
    return [pltpu.VMEM((g.n_t - 1, 2, h, g.D), BF), pltpu.VMEM((1, 8, 128), BF), pltpu.VMEM((1, 8, 128), BF), pltpu.VMEM((g.n_t - 1, 2, h, g.D), BF)]


class Scatter:
    def __init__(self, geo, comm, bufs):
        self.g, self.comm = geo, comm
        self.part, self.into, self.out, self.fin = bufs
        g = geo
        if g.square:
            self.sx, self.sy = comm.slots(3), comm.slots(3)
        else:
            self.s = comm.slots(g.n_t - 1)

    def give(self, i, value):
        g, comm = self.g, self.comm
        h = g.R // 2
        for j in range(2):
            self.part[i, j] = value[j * h : (j + 1) * h].astype(BF)
        if not g.square:
            comm.send(self.s[i], self.part.at[i], self.fin.at[i], (g.d, g.leave[i]))
        elif i == 0:
            comm.send(self.sx[0], self.part.at[0, 0], self.into.at[0], (g.d, g.tx))
            comm.send(self.sy[0], self.part.at[0, 1], self.into.at[1], (g.d, g.ty))
        elif i == 1:
            comm.send(self.sx[1], self.part.at[1, 0], self.fin.at[0, 0], (g.d, g.tx))
        else:
            comm.send(self.sy[1], self.part.at[2, 1], self.fin.at[1, 1], (g.d, g.ty))

    def relay(self):
        g, comm = self.g, self.comm
        if not g.square:
            return
        comm.recv(self.sx[0], self.into.at[0], (g.d, g.tx))
        self.out[0] = (self.into[0].astype(F32) + self.part[2, 0].astype(F32)).astype(BF)
        comm.send(self.sy[2], self.out.at[0], self.fin.at[1, 0], (g.d, g.ty))
        comm.recv(self.sy[0], self.into.at[1], (g.d, g.ty))
        self.out[1] = (self.into[1].astype(F32) + self.part[1, 1].astype(F32)).astype(BF)
        comm.send(self.sx[2], self.out.at[1], self.fin.at[0, 1], (g.d, g.tx))

    def total(self, own):
        g, comm = self.g, self.comm
        h = g.R // 2
        if g.square:
            comm.recv(self.sx[1], self.fin.at[0, 0], (g.d, g.tx))
            comm.recv(self.sy[1], self.fin.at[1, 1], (g.d, g.ty))
            comm.recv(self.sx[2], self.fin.at[0, 1], (g.d, g.tx))
            comm.recv(self.sy[2], self.fin.at[1, 0], (g.d, g.ty))
            count = 2
        else:
            count = g.n_t - 1
            for k in range(count):
                comm.recv(self.s[k], self.fin.at[k], (g.d, g.arrive[k + 1]))
        halves = []
        for j in range(2):
            v = own[j * h : (j + 1) * h]
            for k in range(count):
                v = v + self.fin[k, j].astype(F32)
            halves.append(v)
        return jnp.concatenate(halves, axis=0)


class WeightGather:
    def __init__(self, geo, comm, buf):
        self.g, self.comm, self.buf = geo, comm, buf
        g = geo
        self.sz, self.sc = comm.slots(g.C - 1), comm.slots(g.C)
        own = self.at(g.d)
        for k in range(1, g.C):
            comm.send(self.sz[k - 1], own, own, (g.zto(k), g.t))
        comm.send(self.sc[0], own, own, (g.sib, g.t))

    def at(self, d):
        return self.buf.at[:, self.g.wrows(d)]

    def wait(self):
        g, comm = self.g, self.comm
        for k in range(1, g.C):
            block = self.at(g.zfrom(k))
            comm.recv(self.sz[k - 1], block, (g.zfrom(k), g.t))
            comm.send(self.sc[k], block, block, (g.sib, g.t))
        for k in range(g.C):
            other = g.zfrom(k) + 1 - 2 * g.core
            comm.recv(self.sc[k], self.at(other), (g.sib, g.t))


def rotated(v, cosine, sine):
    n = v.shape[1]
    lower = lax.broadcasted_iota(jnp.int32, v.shape, 1) % HD < HD // 2
    swapped = jnp.where(lower, pltpu.roll(v, n - HD // 2, 1), pltpu.roll(v, HD // 2, 1))
    return v * cosine + swapped * sine


def head_lanes(v, h):
    lane = lax.broadcasted_iota(jnp.int32, v.shape, 1)
    keep = (lane >= h * HD) & (lane < (h + 1) * HD)
    return jnp.where(keep, v, jnp.zeros_like(v))


def bias_of(qinfo, kinfo, first, size, rows):
    shape = (size, rows)
    doc_q, pic_q = qinfo[0:1, :], qinfo[1:2, :]
    key_doc, pic_k, doc_k = kinfo[:, 0:1], kinfo[:, 1:2], kinfo[:, 2:3]
    key_pos = lax.broadcasted_iota(jnp.int32, shape, 0)
    query_pos = lax.broadcasted_iota(jnp.int32, shape, 1) + first
    before = key_pos <= query_pos
    open_ = (doc_q == key_doc) & (before | (pic_q == pic_k))
    ok = open_ | (key_pos == query_pos)
    return jnp.where(ok, 0.0, MASKED).astype(F32)


def k1_body(g, x, wq, wk, wv, wo, wg, wu, wd, cosine, sine, qinfo, kinfo,
            middle, rows, q, kk, v, mixed, mixt, probs, rinv, wa, wm, count,
            cnt, bias, vt, part, into, out, fin, ts, tr, zs, zr):
    g.place()
    R, S, c, H = g.R, g.S, g.c, g.H
    tc, zc = Comm(ts, tr, g), Comm(zs, zr, g)
    mine = g.wrows(g.d)
    wa[0, mine] = wq[...]
    wa[1, mine] = wk[...]
    wa[2, mine] = wv[...]
    wa[3, mine] = turned(wo[...])
    one, _ = normed(x[...])
    rows[g.rows(g.t)] = one.astype(BF)
    g.greet()
    ag = Gather(g, tc, rows)
    za = WeightGather(g, zc, wa)
    wm[0, mine] = wg[...]
    wm[1, mine] = wu[...]
    wm[2, mine] = turned(wd[...])
    zm = WeightGather(g, zc, wm)
    sc, sz = zc.slots(1)[0], zc.slots(g.C - 1)
    valid = jnp.sum(qinfo[2:3, :].astype(F32), axis=1, keepdims=True)
    cnt[0] = jnp.broadcast_to(valid, (8, 128))
    zc.send(sc, cnt.at[0], cnt.at[1], (g.sib, g.t))
    zc.recv(sc, cnt.at[1], (g.sib, g.t))
    cnt[2] = cnt[0] + cnt[1]
    for k in range(1, g.C):
        zc.send(sz[k - 1], cnt.at[2], cnt.at[2 + k], (g.zto(k), g.t))
    ag.relay()
    za.wait()
    for i in range(g.n_t):
        ag.wait(i)
        blk = g.rows(g.arrive[i])
        row = rows[blk]
        cos_b, sin_b = cosine[blk], sine[blk]
        q[blk] = (rotated(dot(row, wa[0]), cos_b, sin_b) * HD**-0.5).astype(BF)
        kk[blk] = rotated(dot(row, wa[1]), cos_b, sin_b).astype(BF)
        v[blk] = dot(row, wa[2]).astype(BF)
    vt[...] = turned(v[...])
    sca = Scatter(g, tc, (part, into, out, fin))
    for i, blk in enumerate(g.leave):
        bias[...] = bias_of(qinfo[:, g.rows(blk)], kinfo[...], blk * R, S, R)
        q_blk = q[g.rows(blk)]
        outs = []
        for h in range(H):
            s = dot(kk[...], head_lanes(q_blk, h), NT) + bias[...]
            e = jnp.exp(s - jnp.max(s, axis=0, keepdims=True))
            inv = 1.0 / jnp.sum(e, axis=0, keepdims=True)
            low = e.astype(BF)
            probs[blk, :, h * R : (h + 1) * R] = low
            rinv[blk, h : h + 1, :] = inv
            outs.append(dot(vt[h * HD : (h + 1) * HD, :], low) * inv)
        both = jnp.concatenate(outs, axis=0)
        mixt[blk] = both.astype(BF)
        mix = both.T.astype(BF)
        mixed[g.rows(blk)] = mix
        partial = dot(mix, wa[3], NT)
        if i < g.n_t - 1:
            sca.give(i, partial)
        else:
            middle[...] = x[...] + partial
    sca.relay()
    zm.wait()
    middle[...] = sca.total(middle[...])
    total = cnt[2]
    for k in range(1, g.C):
        zc.recv(sz[k - 1], cnt.at[2 + k], (g.zfrom(k), g.t))
        total = total + cnt[2 + k]
    count[...] = total
    tc.finish()
    zc.finish()


def vmem(*shape_dtype):
    return jax.ShapeDtypeStruct(*shape_dtype)


def call(body, g, name, outs, scratch, cid, args, sems=(24, 24)):
    whole = pl.BlockSpec(memory_space=pltpu.VMEM)
    return pl.pallas_call(
        functools.partial(body, g),
        name=name,
        out_shape=outs,
        in_specs=[whole] * len(args),
        out_specs=[whole] * len(outs),
        scratch_shapes=list(scratch) + [
            pltpu.SemaphoreType.DMA((sems[0],)), pltpu.SemaphoreType.DMA((sems[0],)),
            pltpu.SemaphoreType.DMA((sems[1],)), pltpu.SemaphoreType.DMA((sems[1],)),
        ],
        compiler_params=pltpu.CompilerParams(
            collective_id=cid, has_side_effects=True, vmem_limit_bytes=60 * 2**20
        ),
    )(*args)


def rotary(length, cols):
    half = HD // 2
    frequency = 10000.0 ** (-2.0 * np.arange(half) / HD)
    angle = np.arange(length)[:, None] * frequency[None, :]
    cosine = np.concatenate([np.cos(angle)] * 2, axis=1)
    sine = np.concatenate([-np.sin(angle), np.sin(angle)], axis=1)
    reps = cols // HD
    return (jnp.asarray(np.tile(cosine, (1, reps)), F32), jnp.asarray(np.tile(sine, (1, reps)), F32))


def mask_info(documents, picture_starts, valid_mask):
    length = documents.shape[1]
    at = jnp.arange(length, dtype=jnp.int32)
    starts = picture_starts[0]
    pic = jnp.zeros((length,), jnp.int32)
    for p in range(starts.shape[0]):
        pic = jnp.where((at >= starts[p]) & (at < starts[p] + PIECE), p + 1, pic)
    doc, valid = documents[0], valid_mask[0]
    zero = jnp.zeros_like(doc)
    qinfo = jnp.stack([doc, pic, valid, zero, zero, zero, zero, zero])
    kinfo = jnp.stack([jnp.where(valid == 1, doc, -1), jnp.where(pic > 0, pic, -1), doc, valid], axis=1)
    return qinfo, kinfo


def forward_attention(g, inputs, qinfo, kinfo, tables, weights):
    S, R, D, c, f = g.S, g.R, g.D, g.c, g.f
    sds = jax.ShapeDtypeStruct
    outs = [sds((R, D), F32), sds((S, D), BF), sds((S, c), BF), sds((S, c), BF), sds((S, c), BF), sds((S, c), BF), sds((g.n_t, c, R), BF),
            sds((g.n_t, S, g.H * R), BF), sds((g.n_t, 8, R), F32), sds((4, D, c), BF), sds((3, D, f), BF), sds((8, 128), F32)]
    scratch = [pltpu.VMEM((g.C + 2, 8, 128), F32), pltpu.VMEM((S, R), F32), pltpu.VMEM((c, S), BF)] + scatter_scratch(g)
    return call(k1_body, g, "attention_forward", outs, scratch, 1, (inputs, *weights, *tables, qinfo, kinfo))


def leave_index(g, i):
    if g.square:
        return (3, 1, 2, 0)[i]
    return (g.n_t - 1 - i) % g.n_t if i else g.n_t - 1


def k2_body(g, middle, teacher, kinfo, count, wm,
            output, grad_middle, dw, error,
            rows, gm, hidden, gate_factor, silu, gl, ul, acc, cot,
            part1, into1, out1, fin1, part2, into2, out2, fin2, ts, tr, zs, zr):
    g.place()
    tc = Comm(ts, tr, g)
    two, inv = normed(middle[...])
    rows[g.rows(g.t)] = two.astype(BF)
    g.greet(dp=False)
    ag = Gather(g, tc, rows)
    sca = Scatter(g, tc, (part1, into1, out1, fin1))
    for i, at in enumerate(g.arrive):
        if i == 1:
            ag.relay()
        ag.wait(i)
        blk = g.rows(at)
        row = rows[blk]
        gate, up = dot(row, wm[0]), dot(row, wm[1])
        sig = jax.nn.sigmoid(gate)
        act = gate * sig
        hid = (act * up).astype(BF)
        hidden[blk] = hid
        silu[blk] = act.astype(BF)
        gate_factor[blk] = (up * sig * (1.0 + gate * (1.0 - sig))).astype(BF)
        partial = dot(hid, wm[2], NT)
        if i:
            sca.give(leave_index(g, i), partial)
        else:
            acc[...] = partial + middle[...]
    sca.relay()
    result = sca.total(acc[...])
    output[...] = result
    valid = kinfo[g.rows(g.t), 3:4].astype(F32)
    dev = result - teacher[...]
    c = valid * dev
    rows_error = jnp.sum(jnp.sum(c * dev, axis=1, keepdims=True), axis=0, keepdims=True)
    error[...] = jnp.broadcast_to(rows_error, (8, 128))
    tokens = 1.0 * g.S * g.n_dp
    c = c * (tokens / count[0:1, 0:1])
    cot[...] = c
    gm[g.rows(g.t)] = c.astype(BF)
    ag = Gather(g, tc, gm)
    sca = Scatter(g, tc, (part2, into2, out2, fin2))
    for i, at in enumerate(g.arrive):
        if i == 1:
            ag.relay()
        ag.wait(i)
        blk = g.rows(at)
        gh = dot(gm[blk], wm[2])
        g_low = (gh * gate_factor[blk].astype(F32)).astype(BF)
        u_low = (gh * silu[blk].astype(F32)).astype(BF)
        gl[blk] = g_low
        ul[blk] = u_low
        partial = dot(g_low, wm[0], NT) + dot(u_low, wm[1], NT)
        if i:
            sca.give(leave_index(g, i), partial)
        else:
            acc[...] = partial
    rows_t = turned(rows[...])
    dw[0] = dot(rows_t, gl[...]).astype(BF)
    sca.relay()
    dw[1] = dot(rows_t, ul[...]).astype(BF)
    dw[2] = dot(turned(gm[...]), hidden[...]).astype(BF)
    back = sca.total(acc[...])
    two, inv = normed(middle[...])
    grad_middle[...] = cot[...] + normed_back(two, inv, back)
    tc.finish()


def feed_forward(g, middle, teacher, kinfo, count, wm):
    S, R, D, f = g.S, g.R, g.D, g.f
    sds = jax.ShapeDtypeStruct
    outs = [sds((R, D), F32), sds((R, D), F32), sds((3, D, f), BF), sds((8, 128), F32)]
    scratch = [pltpu.VMEM((S, D), BF)] * 2 + [pltpu.VMEM((S, f), BF)] * 5 + [pltpu.VMEM((R, D), F32)] * 2
    scratch += scatter_scratch(g) + scatter_scratch(g)
    return call(k2_body, g, "feed_forward", outs, scratch, 2, (middle, teacher, kinfo, count, wm))


class WeightScatter:
    def __init__(self, geo, comm, src, bufs):
        self.g, self.comm, self.src = geo, comm, src
        self.sib_in, self.out, self.fin = bufs
        g = geo
        self.sc, self.sz = comm.slots(g.C), comm.slots(g.C - 1)

    def start(self):
        g, comm = self.g, self.comm
        for j in range(g.C):
            block = self.src.at[:, g.wrows(2 * j + 1 - g.core)]
            comm.send(self.sc[j], block, self.sib_in.at[j], (g.sib, g.t))

    def pass_on(self):
        g, comm = self.g, self.comm
        for j in range(g.C):
            comm.recv(self.sc[j], self.sib_in.at[j], (g.sib, g.t))
        for k in range(1, g.C):
            to = (g.chip + k) % g.C
            mine = self.src[:, g.wrows(2 * to + g.core)].astype(F32)
            self.out[k - 1] = (mine + self.sib_in[to].astype(F32)).astype(BF)
            comm.send(self.sz[k - 1], self.out.at[k - 1], self.fin.at[k - 1], (g.zto(k), g.t))

    def total(self):
        g, comm = self.g, self.comm
        v = self.src[:, g.wrows(g.d)].astype(F32) + self.sib_in[g.chip].astype(F32)
        for k in range(1, g.C):
            comm.recv(self.sz[k - 1], self.fin.at[k - 1], (g.zfrom(k), g.t))
            v = v + self.fin[k - 1].astype(F32)
        return v


def weight_scatter_scratch(g, n, w):
    return [pltpu.VMEM((g.C, n, g.Dn, w), BF), pltpu.VMEM((g.C - 1, n, g.Dn, w), BF), pltpu.VMEM((g.C - 1, n, g.Dn, w), BF)]


def k3_body(g, x, grad_middle, q, kk, v, mixed, mixt, probs, rinv, rows, wa, dw, cosine, sine, error,
            grad_inputs, dmlp, dattn, error_all,
            ga, wo, kt, ds, qm, gom, dk, dv, low, dwa, acc, err,
            msib, mout, mfin, asib, aout, afin, part, into, out, fin, ts, tr, zs, zr):
    g.place()
    R, S, c, H = g.R, g.S, g.c, g.H
    tc, zc = Comm(ts, tr, g), Comm(zs, zr, g)
    ga[g.rows(g.t)] = grad_middle[...].astype(BF)
    g.greet()
    ag = Gather(g, tc, ga)
    mlp = WeightScatter(g, zc, dw, (msib, mout, mfin))
    mlp.start()
    te = tc.slots(g.n_t - 1 if not g.square else 2)
    err[0] = error[...]
    if g.square:
        tc.send(te[0], err.at[0], err.at[1], (g.d, g.tx))
    else:
        for k, peer in enumerate(g.to):
            tc.send(te[k], err.at[0], err.at[1 + k], (g.d, peer))
    wo[...] = turned(wa[3])
    kt[...] = turned(kk[...])
    for i, at in enumerate(g.arrive):
        if i == 1:
            mlp.pass_on()
            ag.relay()
        ag.wait(i)
        blk = g.rows(at)
        go_t = dot(wo[...], ga[blk], NT).astype(BF).astype(F32)
        mix_t = mixt[at].astype(F32)
        rows_out, dots = [], []
        for h in range(H):
            part_h = go_t[h * HD : (h + 1) * HD] * rinv[at, h : h + 1, :]
            rows_out.append(part_h)
            dots.append(jnp.sum(part_h * mix_t[h * HD : (h + 1) * HD], axis=0, keepdims=True))
        go = jnp.concatenate(rows_out, axis=0).T.astype(BF)
        q_blk = q[blk]
        dqs = []
        for h in range(H):
            cols = slice(h * R, (h + 1) * R)
            go_h = head_lanes(go, h)
            gom[cols] = go_h
            qm[cols] = head_lanes(q_blk, h)
            gp = dot(v[...], go_h, NT)
            d_low = (probs[at, :, cols].astype(F32) * (gp - dots[h])).astype(BF)
            ds[:, cols] = d_low
            dqs.append(dot(kt[h * HD : (h + 1) * HD, :], d_low))
        dq_blk = jnp.concatenate(dqs, axis=0).T * HD**-0.5
        low[0, blk] = rotated(dq_blk, cosine[blk], -sine[blk]).astype(BF)
        dk_part, dv_part = dot(ds[...], qm[...]), dot(probs[at], gom[...])
        if i == 0:
            dk[...] = dk_part
            dv[...] = dv_part
        else:
            dk[...] += dk_part
            dv[...] += dv_part
    if g.square:
        tc.recv(te[0], err.at[1], (g.d, g.tx))
        err[2] = err[0] + err[1]
        tc.send(te[1], err.at[2], err.at[3], (g.d, g.ty))
    sca = Scatter(g, tc, (part, into, out, fin))
    for i, at in enumerate(g.leave):
        blk = g.rows(at)
        dk_low = rotated(dk[blk], cosine[blk], -sine[blk]).astype(BF)
        dv_low = dv[blk].astype(BF)
        low[1, blk] = dk_low
        low[2, blk] = dv_low
        partial = dot(low[0, blk], wa[0], NT) + dot(dk_low, wa[1], NT) + dot(dv_low, wa[2], NT)
        if i < g.n_t - 1:
            sca.give(i, partial)
        else:
            acc[...] = partial
    rows_t = turned(rows[...])
    for j in range(3):
        dwa[j] = dot(rows_t, low[j]).astype(BF)
    dwa[3] = dot(turned(ga[...]), mixed[...]).astype(BF)
    att = WeightScatter(g, zc, dwa, (asib, aout, afin))
    att.start()
    sca.relay()
    att.pass_on()
    base = 4 if g.square else g.n_t
    if g.square:
        tc.recv(te[1], err.at[3], (g.d, g.ty))
        err[base] = err[2] + err[3]
    else:
        total = err[0]
        for k in range(1, g.n_t):
            tc.recv(te[k - 1], err.at[k], (g.d, g.arrive[k]))
            total = total + err[k]
        err[base] = total
    ec, ez = zc.slots(1)[0], zc.slots(g.C - 1)
    zc.send(ec, err.at[base], err.at[base + 1], (g.sib, g.t))
    zc.recv(ec, err.at[base + 1], (g.sib, g.t))
    err[base + 2] = err[base] + err[base + 1]
    for k in range(1, g.C):
        zc.send(ez[k - 1], err.at[base + 2], err.at[base + 2 + k], (g.zto(k), g.t))
    dmlp[...] = mlp.total()
    one, inv = normed(x[...])
    grad_inputs[...] = grad_middle[...] + normed_back(one, inv, sca.total(acc[...]))
    dattn[...] = att.total()
    total = err[base + 2]
    for k in range(1, g.C):
        zc.recv(ez[k - 1], err.at[base + 2 + k], (g.zfrom(k), g.t))
        total = total + err[base + 2 + k]
    error_all[...] = total
    tc.finish()
    zc.finish()


def backward_attention(g, args):
    S, R, D, c, f, H = g.S, g.R, g.D, g.c, g.f, g.H
    sds = jax.ShapeDtypeStruct
    outs = [sds((R, D), F32), sds((3, g.Dn, f), F32), sds((4, g.Dn, c), F32), sds((8, 128), F32)]
    base = 4 if g.square else g.n_t
    scratch = [
        pltpu.VMEM((S, D), BF), pltpu.VMEM((c, D), BF), pltpu.VMEM((c, S), BF), pltpu.VMEM((S, H * R), BF),
        pltpu.VMEM((H * R, c), BF), pltpu.VMEM((H * R, c), BF), pltpu.VMEM((S, c), F32), pltpu.VMEM((S, c), F32),
        pltpu.VMEM((3, S, c), BF), pltpu.VMEM((4, D, c), BF), pltpu.VMEM((R, D), F32),
        pltpu.VMEM((base + 2 + g.C, 8, 128), F32),
    ]
    scratch += weight_scatter_scratch(g, 3, f) + weight_scatter_scratch(g, 4, c) + scatter_scratch(g)
    return call(k3_body, g, "attention_backward", outs, scratch, 3, args, sems=(24, 32))


def per_device(mesh_shape, inputs, teacher, valid_mask, documents, picture_starts,
               w_query, w_key, w_value, w_out, w_gate, w_up, w_down):
    n_dp, n_t = mesh_shape
    R, D = inputs.shape
    c, f = w_query.shape[1], w_gate.shape[1]
    g = Geo(n_dp, n_t, R, D, c, f)
    length = valid_mask.shape[1]
    tables = rotary(length, c)
    qinfo, kinfo = mask_info(documents, picture_starts, valid_mask)
    weights = (w_query, w_key, w_value, w_out, w_gate, w_up, w_down)
    middle, rows_one, q, kk, v, mixed, mixt, probs, rinv, wa, wm, count = forward_attention(g, inputs, qinfo, kinfo, tables, weights)
    output, grad_middle, dw, error = feed_forward(g, middle, teacher, kinfo, count, wm)
    grad_inputs, dmlp, dattn, error_all = backward_attention(
        g, (inputs, grad_middle, q, kk, v, mixed, mixt, probs, rinv, rows_one, wa, dw, *tables, error))
    loss_value = error_all[0, 0] / (D * count[0, 0])
    return (output, loss_value, grad_inputs, dattn[0], dattn[1], dattn[2], dattn[3].T, dmlp[0], dmlp[1], dmlp[2].T)


def solution(mesh):
    rows, pair = P(("dp", "tensor"), None), P("dp", None)
    cut, across = P("dp", "tensor"), P("tensor", "dp")
    return jax.shard_map(
        functools.partial(per_device, (mesh.shape["dp"], mesh.shape["tensor"])),
        mesh=mesh,
        in_specs=(rows, rows, pair, pair, pair, cut, cut, cut, across, cut, cut, across),
        out_specs=(rows, P(), rows, cut, cut, cut, across, cut, cut, across),
        check_vma=False,
    )
```

```python
import functools

import jax
import jax.numpy as jnp
import numpy as np
from jax import lax
from jax.experimental import pallas as pl
from jax.experimental.pallas import tpu as pltpu
from jax.sharding import PartitionSpec as P

MESH = pl.DeviceIdType.MESH
HD = 64
PIECE = 256
EPS = 1e-5
MASKED = -1e30
VMEM_BYTES = 60 * 2**20
BF = jnp.bfloat16
F32 = jnp.float32
NT = (((1,), (1,)), ((), ()))
NN = (((1,), (0,)), ((), ()))


def dot(a, b, dims=NN):
    return lax.dot_general(a, b, dims, preferred_element_type=F32)


def eye(n):
    return (
        lax.broadcasted_iota(jnp.int32, (n, n), 0) == lax.broadcasted_iota(jnp.int32, (n, n), 1)
    ).astype(F32).astype(BF)


def turned(a):
    n = a.shape[1]
    step = min(n, 256)
    parts = [dot(eye(step), a[:, k : k + step], NT).astype(BF) for k in range(0, n, step)]
    return parts[0] if len(parts) == 1 else jnp.concatenate(parts, axis=0)


def mean_of(v):
    return jnp.sum(v, axis=1, keepdims=True) * (1.0 / v.shape[1])


def normed(v):
    centred = v - mean_of(v)
    inv = lax.rsqrt(mean_of(centred * centred) + EPS)
    return centred * inv, inv


def normed_back(n, inv, g):
    return inv * (g - mean_of(g) - n * mean_of(g * n))


class Geo:
    def __init__(self, n_dp, n_t, tok_rows, d_model, cols, hid):
        self.n_dp, self.n_t, self.R, self.D, self.c, self.f = n_dp, n_t, tok_rows, d_model, cols, hid
        self.C = n_dp // 2
        self.S = tok_rows * n_t
        self.H = cols // HD
        self.Dn = d_model // n_dp
        self.square = n_t == 4
        self.line = self.C == 4

    def place(self):
        self.d = lax.axis_index("dp")
        self.t = lax.axis_index("tensor")
        self.chip = self.d // 2
        self.core = self.d % 2
        if self.square:
            self.tx = self.t + 1 - 2 * (self.t % 2)
            self.ty = (self.t + 2) % 4
            self.td = 3 - self.t
            self.to = [self.tx, self.ty]
            self.arrive = [self.t, self.tx, self.ty, self.td]
            self.leave = [self.td, self.tx, self.ty, self.t]
        else:
            n = self.n_t
            self.to = [(self.t + k) % n for k in range(1, n)]
            self.arrive = [(self.t + n - k) % n for k in range(n)]
            self.leave = [(self.t + k) % n for k in range(1, n)] + [self.t]
        self.sib = self.d + 1 - 2 * self.core
        return self

    def leave_index(self, i):
        if self.square:
            return (3, 1, 2, 0)[i]
        return self.n_t - 1 - i if i else self.n_t - 1

    def zto(self, k):
        return ((self.chip + k) % self.C) * 2 + self.core

    def zfrom(self, k):
        return ((self.chip + self.C - k) % self.C) * 2 + self.core

    def rows(self, blk, first=0, count=None):
        count = self.R if count is None else count
        return pl.ds(pl.multiple_of(blk * self.R + first, count), count)

    def wrows(self, d):
        return pl.ds(pl.multiple_of(d * self.Dn, self.Dn), self.Dn)

    def greet(self):
        bar = pltpu.get_barrier_semaphore()
        out = [(self.d, p) for p in self.to]
        out += [(self.zto(k), self.t) for k in range(1, self.C)] + [(self.sib, self.t)]
        for dev in out:
            pl.semaphore_signal(bar, inc=1, device_id=dev, device_id_type=MESH)
        self.met = len(out)

    def meet(self):
        pl.semaphore_wait(pltpu.get_barrier_semaphore(), self.met)


class Comm:
    def __init__(self, send_sem, recv_sem):
        self.ss, self.rs = send_sem, recv_sem
        self.n = 0
        self.groups = []

    def group(self):
        self.groups.append([])
        return self.groups[-1]

    def slots(self, k):
        self.n += k
        return list(range(self.n - k, self.n))

    def _copy(self, slot, src, dst, dev, send_slot=None):
        return pltpu.make_async_remote_copy(
            src_ref=src, dst_ref=dst, send_sem=self.ss.at[slot if send_slot is None else send_slot],
            recv_sem=self.rs.at[slot], device_id=dev, device_id_type=MESH,
        )

    def send(self, group, slot, src, dst, dev, when=None, send_slot=None):
        copy = self._copy(slot, src, dst, dev, send_slot)
        if when is None:
            copy.start()
        else:
            pl.when(when)(copy.start)
        group.append((when, copy))

    def recv(self, slot, dst, dev, when=None):
        copy = self._copy(slot, dst, dst, dev)
        if when is None:
            copy.wait_recv()
        else:
            pl.when(when)(copy.wait_recv)

    def sent(self, group):
        for when, copy in group:
            if when is None:
                copy.wait_send()
            else:
                pl.when(when)(copy.wait_send)
        group.clear()

    def finish(self):
        for group in self.groups:
            self.sent(group)


class Gather:
    def __init__(self, geo, comm, buf):
        self.g, self.comm, self.buf = geo, comm, buf
        g = geo
        self.group = comm.group()
        if g.square:
            self.sx, self.sy = comm.slots(3), comm.slots(3)
            h0, h1 = self.half(g.t, 0), self.half(g.t, 1)
            comm.send(self.group, self.sx[0], h0, h0, (g.d, g.tx))
            comm.send(self.group, self.sy[1], h1, h1, (g.d, g.ty))
            comm.send(self.group, self.sx[1], h1, h1, (g.d, g.tx))
            comm.send(self.group, self.sy[0], h0, h0, (g.d, g.ty))
        else:
            self.s = comm.slots(g.n_t - 1)
            own = buf.at[g.rows(g.t)]
            for k, peer in enumerate(g.to):
                comm.send(self.group, self.s[k], own, own, (g.d, peer))

    def half(self, blk, i):
        h = self.g.R // 2
        return self.buf.at[self.g.rows(blk, i * h, h)]

    def relay(self):
        g, comm = self.g, self.comm
        if g.square:
            a = self.half(g.tx, 0)
            comm.recv(self.sx[0], a, (g.d, g.tx))
            comm.send(self.group, self.sy[2], a, a, (g.d, g.ty))
            b = self.half(g.ty, 1)
            comm.recv(self.sy[1], b, (g.d, g.ty))
            comm.send(self.group, self.sx[2], b, b, (g.d, g.tx))

    def wait(self, i):
        g, comm = self.g, self.comm
        if i == 0:
            return
        if not g.square:
            comm.recv(self.s[i - 1], self.buf.at[g.rows(g.arrive[i])], (g.d, g.arrive[i]))
        elif i == 1:
            comm.recv(self.sx[1], self.half(g.tx, 1), (g.d, g.tx))
        elif i == 2:
            comm.recv(self.sy[0], self.half(g.ty, 0), (g.d, g.ty))
        else:
            comm.recv(self.sx[2], self.half(g.td, 1), (g.d, g.tx))
            comm.recv(self.sy[2], self.half(g.td, 0), (g.d, g.ty))


def scatter_scratch(g):
    h = g.R // 2
    if g.square:
        return [pltpu.VMEM((3, 2, h, g.D), BF), pltpu.VMEM((2, h, g.D), BF), pltpu.VMEM((2, h, g.D), BF), pltpu.VMEM((2, 2, h, g.D), BF)]
    return [pltpu.VMEM((g.n_t - 1, 2, h, g.D), BF), pltpu.VMEM((1, 16, 128), BF), pltpu.VMEM((1, 16, 128), BF), pltpu.VMEM((g.n_t - 1, 2, h, g.D), BF)]


class Scatter:
    def __init__(self, geo, comm, bufs):
        self.g, self.comm = geo, comm
        self.part, self.into, self.out, self.fin = bufs
        g = geo
        self.group = comm.group()
        if g.square:
            self.sx, self.sy = comm.slots(3), comm.slots(3)
        else:
            self.s = comm.slots(g.n_t - 1)

    def give(self, i, value):
        g, comm = self.g, self.comm
        h = g.R // 2
        for j in range(2):
            self.part[i, j] = value[j * h : (j + 1) * h].astype(BF)
        if not g.square:
            comm.send(self.group, self.s[i], self.part.at[i], self.fin.at[i], (g.d, g.leave[i]))
        elif i == 0:
            comm.send(self.group, self.sx[0], self.part.at[0, 0], self.into.at[0], (g.d, g.tx))
            comm.send(self.group, self.sy[0], self.part.at[0, 1], self.into.at[1], (g.d, g.ty))
        elif i == 1:
            comm.send(self.group, self.sx[1], self.part.at[1, 0], self.fin.at[0, 0], (g.d, g.tx))
        else:
            comm.send(self.group, self.sy[1], self.part.at[2, 1], self.fin.at[1, 1], (g.d, g.ty))

    def relay(self):
        g, comm = self.g, self.comm
        if not g.square:
            return
        comm.recv(self.sx[0], self.into.at[0], (g.d, g.tx))
        self.out[0] = (self.into[0].astype(F32) + self.part[2, 0].astype(F32)).astype(BF)
        comm.send(self.group, self.sy[2], self.out.at[0], self.fin.at[1, 0], (g.d, g.ty))
        comm.recv(self.sy[0], self.into.at[1], (g.d, g.ty))
        self.out[1] = (self.into[1].astype(F32) + self.part[1, 1].astype(F32)).astype(BF)
        comm.send(self.group, self.sx[2], self.out.at[1], self.fin.at[0, 1], (g.d, g.tx))

    def total(self, own):
        g, comm = self.g, self.comm
        h = g.R // 2
        if g.square:
            comm.recv(self.sx[1], self.fin.at[0, 0], (g.d, g.tx))
            comm.recv(self.sy[1], self.fin.at[1, 1], (g.d, g.ty))
            comm.recv(self.sx[2], self.fin.at[0, 1], (g.d, g.tx))
            comm.recv(self.sy[2], self.fin.at[1, 0], (g.d, g.ty))
            count = 2
        else:
            count = g.n_t - 1
            for k in range(count):
                comm.recv(self.s[k], self.fin.at[k], (g.d, g.arrive[k + 1]))
        halves = []
        for j in range(2):
            v = own[j * h : (j + 1) * h]
            for k in range(count):
                v = v + self.fin[k, j].astype(F32)
            halves.append(v)
        comm.sent(self.group)
        return jnp.concatenate(halves, axis=0)


class WeightGather:
    def __init__(self, geo, comm, buf, first, n):
        self.g, self.comm, self.buf, self.of = geo, comm, buf, pl.ds(first, n)
        g = geo
        self.group = comm.group()
        self.sz, self.sc, self.sr = comm.slots(g.C - 1), comm.slots(g.C), comm.slots(2)
        own = self.at(g.d)
        for k in range(1, g.C):
            near = None
            if g.line and k != 2:
                near = g.chip != (0 if k == 3 else 3)
            comm.send(self.group, self.sz[k - 1], own, own, (g.zto(k), g.t), when=near)
        comm.send(self.group, self.sc[0], own, own, (g.sib, g.t))

    def at(self, d):
        return self.buf.at[self.of, self.g.wrows(d)]

    def _take(self, k):
        g, comm = self.g, self.comm
        block = self.at(g.zfrom(k))
        comm.recv(self.sz[k - 1], block, (g.zfrom(k), g.t))
        comm.send(self.group, self.sc[k], block, block, (g.sib, g.t))

    def relay(self):
        g, comm = self.g, self.comm
        if not g.line:
            return
        self._take(2)
        block = self.at(g.zfrom(2))
        comm.send(self.group, self.sz[2], block, block, (6 + g.core, g.t), when=g.chip == 2, send_slot=self.sr[0])
        comm.send(self.group, self.sz[0], block, block, (g.core, g.t), when=g.chip == 1, send_slot=self.sr[1])

    def wait(self):
        g, comm = self.g, self.comm
        for k in range(1, g.C):
            if not (g.line and k == 2):
                self._take(k)
        for k in range(g.C):
            other = g.zfrom(k) + 1 - 2 * g.core
            comm.recv(self.sc[k], self.at(other), (g.sib, g.t))


class WeightScatter:
    def __init__(self, geo, comm, src, bufs):
        self.g, self.comm, self.src = geo, comm, src
        self.sib_in, self.out, self.fin, self.mid = bufs
        g = geo
        self.group = comm.group()
        self.sc, self.sz, self.sr = comm.slots(g.C), comm.slots(g.C - 1), comm.slots(2)
        for j in range(g.C):
            block = self.src.at[g.wrows(2 * j + 1 - g.core)]
            comm.send(self.group, self.sc[j], block, self.sib_in.at[j], (g.sib, g.t))

    def _sum(self, k):
        g = self.g
        to = (g.chip + k) % g.C
        return self.src[g.wrows(2 * to + g.core)].astype(F32) + self.sib_in[to].astype(F32)

    def _send(self, k, when=None):
        g = self.g
        self.comm.send(self.group, self.sz[k - 1], self.out[k - 1], self.fin.at[k - 1], (g.zto(k), g.t), when=when)

    def pass_on(self):
        g, comm = self.g, self.comm
        for j in range(g.C):
            comm.recv(self.sc[j], self.sib_in.at[j], (g.sib, g.t))
        if not g.line:
            for k in range(1, g.C):
                self.out[k - 1][...] = self._sum(k).astype(BF)
                self._send(k)
            return
        self.out[2][...] = self._sum(3).astype(BF)
        comm.send(self.group, self.sr[0], self.out[2], self.mid, (2 + g.core, g.t), when=g.chip == 0)
        self._send(3, when=g.chip != 0)
        self.out[0][...] = self._sum(1).astype(BF)
        comm.send(self.group, self.sr[0], self.out[0], self.mid, (4 + g.core, g.t), when=g.chip == 3, send_slot=self.sr[1])
        self._send(1, when=g.chip != 3)

        @pl.when((g.chip == 0) | (g.chip == 3))
        def _():
            self.out[1][...] = self._sum(2).astype(BF)

        self._send(2, when=(g.chip == 0) | (g.chip == 3))

    def relay(self):
        g, comm = self.g, self.comm
        if not g.line:
            return
        inner = (g.chip == 1) | (g.chip == 2)

        @pl.when(inner)
        def _():
            comm.recv(self.sr[0], self.mid, (g.sib, g.t))
            self.out[1][...] = (self._sum(2) + self.mid[...].astype(F32)).astype(BF)

        self.comm.send(self.group, self.sz[1], self.out[1], self.fin.at[1], (g.zto(2), g.t), when=inner, send_slot=None)

    def total(self, into):
        g, comm = self.g, self.comm
        into[...] = self.src[g.wrows(g.d)].astype(F32) + self.sib_in[g.chip].astype(F32)
        for k in range(1, g.C):

            def add(k=k):
                comm.recv(self.sz[k - 1], self.fin.at[k - 1], (g.zfrom(k), g.t))
                into[...] += self.fin[k - 1].astype(F32)

            if g.line and k != 2:
                pl.when(g.chip != (3 if k == 3 else 0))(add)
            else:
                add()


def weight_scatter_scratch(g, n, w):
    return [pltpu.VMEM((n, g.C, g.Dn, w), BF), pltpu.VMEM((n, g.C - 1, g.Dn, w), BF),
            pltpu.VMEM((n, g.C - 1, g.Dn, w), BF), pltpu.VMEM((n, g.Dn, w), BF)]


def rotated(v, cosine, sine):
    n = v.shape[1]
    if n > cosine.shape[1]:
        cosine = jnp.concatenate([cosine] * (n // cosine.shape[1]), axis=1)
        sine = jnp.concatenate([sine] * (n // sine.shape[1]), axis=1)
    lower = lax.broadcasted_iota(jnp.int32, v.shape, 1) % HD < HD // 2
    swapped = jnp.where(lower, pltpu.roll(v, n - HD // 2, 1), pltpu.roll(v, HD // 2, 1))
    return v * cosine + swapped * sine


def head_lanes(v, h):
    lane = lax.broadcasted_iota(jnp.int32, v.shape, 1)
    keep = (lane >= h * HD) & (lane < (h + 1) * HD)
    return jnp.where(keep, v, jnp.zeros_like(v))


def bias_of(qinfo, kinfo, first, size, rows):
    shape = (size, rows)
    doc_q, pic_q = qinfo[0:1, :], qinfo[1:2, :]
    key_doc, pic_k = kinfo[:, 0:1], kinfo[:, 1:2]
    key_pos = lax.broadcasted_iota(jnp.int32, shape, 0)
    query_pos = lax.broadcasted_iota(jnp.int32, shape, 1) + first
    before = key_pos <= query_pos
    open_ = (doc_q == key_doc) & (before | (pic_q == pic_k))
    ok = open_ | (key_pos == query_pos)
    return jnp.where(ok, 0.0, MASKED).astype(F32)


def rotary(length, cols):
    half = HD // 2
    frequency = 10000.0 ** (-2.0 * np.arange(half) / HD)
    angle = np.arange(length)[:, None] * frequency[None, :]
    cosine = np.concatenate([np.cos(angle)] * 2, axis=1)
    sine = np.concatenate([-np.sin(angle), np.sin(angle)], axis=1)
    reps = max(1, min(cols, 128) // HD)
    return (jnp.asarray(np.tile(cosine, (1, reps)), F32), jnp.asarray(np.tile(sine, (1, reps)), F32))


def in_slot(g, n_pic, blk):
    per = g.n_t // n_pic

    def run(body):
        for p in range(n_pic):
            pl.when(blk // per == p)(functools.partial(body, p, blk - p * per, (p + 1) * (g.S // n_pic)))

    return run


def layer_body(g, n_pic, x, teacher, valid_mask, documents, starts, wq, wk, wv, wo, wg, wu, wd, cosine, sine,
               output, grad_inputs, dattn, dmlp, stats,
               rows1, rows2, gm, ga, wa, wm, qkv, mixed, mixt, turn, wo_t, probs0, probs1, acc2, qm, gom, mids, middle, cot,
               qinfo, kinfo, rinv, cnt, err,
               part, into, out, fin,
               sib_m, fin_m, mid_m, sib_a, out_a, fin_a, mid_a,
               ts, tr, zs, zr, local):
    g.place()
    g.greet()
    R, S, c, H, C, Dn = g.R, g.S, g.c, g.H, g.C, g.Dn
    tc, zc = Comm(ts, tr), Comm(zs, zr)
    few, zfew = tc.group(), zc.group()
    sums = (part, into, out, fin)
    q, kk, v = qkv.at[0], qkv.at[1], qkv.at[2]
    probs = (probs0, probs1)
    bias, dk, dv = acc2.at[0, :, :R], acc2.at[0, :, :c], acc2.at[1, :, :c]
    get_teacher = pltpu.make_async_copy(teacher, cot, local.at[0])
    get_teacher.start()

    one, _ = normed(x[...])
    rows1[g.rows(g.t)] = one.astype(BF)
    mine = g.wrows(g.d)
    wa[0, mine] = wq[...]
    wa[1, mine] = wk[...]
    wa[2, mine] = wv[...]
    wa[3, mine] = turned(wo[...])
    g.meet()
    ag = ag1 = Gather(g, tc, rows1)
    za = WeightGather(g, zc, wa, 0, 4)
    wm[0, mine] = turned(wg[...])
    wm[1, mine] = turned(wu[...])
    wm[2, mine] = turned(wd[...])

    csib, cz = zc.slots(1)[0], zc.slots(C - 1)
    valid, doc = valid_mask[...], documents[...]
    cnt[0] = jnp.broadcast_to(jnp.sum(valid.astype(F32), axis=1, keepdims=True), (8, 128))
    zc.send(zfew, csib, cnt.at[0], cnt.at[1], (g.sib, g.t))
    at = lax.broadcasted_iota(jnp.int32, (1, S), 1)
    pic = jnp.zeros((1, S), jnp.int32)
    for p in range(n_pic):
        first = starts[0:1, p : p + 1]
        pic = jnp.where((at >= first) & (at < first + PIECE), p + 1, pic)
    qinfo[0:1] = doc
    qinfo[1:2] = pic
    as_keys = [jnp.where(valid == 1, doc, -1), jnp.where(pic > 0, pic, -1), valid]
    as_keys = jnp.concatenate([a.astype(F32) for a in as_keys] + [jnp.zeros((125, S), F32)], axis=0)
    kinfo[...] = as_keys.T.astype(jnp.int32)
    zc.recv(csib, cnt.at[1], (g.sib, g.t))
    cnt[2] = cnt[0] + cnt[1]
    for k in range(1, C):
        zc.send(zfew, cz[k - 1], cnt.at[2], cnt.at[2 + k], (g.zto(k), g.t))

    ag.relay()
    za.relay()
    za.wait()
    zg = WeightGather(g, zc, wm, 0, 2)
    for i, blk in enumerate(g.arrive):
        ag.wait(i)
        at = g.rows(blk)
        row = rows1[at]
        cos_b, sin_b = cosine[at], sine[at]
        q[at] = (rotated(dot(row, wa[0]), cos_b, sin_b) * HD**-0.5).astype(BF)
        kk[at] = rotated(dot(row, wa[1]), cos_b, sin_b).astype(BF)
        v[at] = dot(row, wa[2]).astype(BF)
    turn[...] = turned(v[...])

    rs = Scatter(g, tc, sums)
    for i, blk in enumerate(g.leave):
        at = g.rows(blk)

        @in_slot(g, n_pic, blk)
        def _(p, index, hi, blk=blk, at=at):
            keys = slice(0, hi)
            bias[keys] = bias_of(qinfo[:, at], kinfo[keys], blk * R, hi, R)
            q_blk = q[at]
            outs = []
            for h in range(H):
                s = dot(kk[keys], head_lanes(q_blk, h), NT) + bias[keys]
                e = jnp.exp(s - jnp.max(s, axis=0, keepdims=True))
                inv = 1.0 / jnp.sum(e, axis=0, keepdims=True)
                low = e.astype(BF)
                probs[p][index, :, h * R : (h + 1) * R] = low
                rinv[blk, h : h + 1, :] = inv
                outs.append(dot(turn[h * HD : (h + 1) * HD, keys], low) * inv)
            both = jnp.concatenate(outs, axis=0)
            mixt[blk] = both.astype(BF)
            mixed[at] = both.T.astype(BF)

        mix = mixed[at]
        partial = dot(mix, wa[3], NT)
        if i < g.n_t - 1:
            rs.give(i, partial)
        else:
            middle[...] = x[...] + partial
    rs.relay()
    zg.relay()
    zd = WeightGather(g, zc, wm, 2, 1)
    middle[...] = rs.total(middle[...])

    two, _ = normed(middle[...])
    rows2[g.rows(g.t)] = two.astype(BF)
    ag = ag2 = Gather(g, tc, rows2)
    rs = Scatter(g, tc, sums)
    zg.wait()
    for i, blk in enumerate(g.arrive):
        ag.wait(i)
        at = g.rows(blk)
        row = rows2[at]
        gate, up = dot(row, wm[0]), dot(row, wm[1])
        sig = jax.nn.sigmoid(gate)
        act = gate * sig
        mids[0, at] = (act * up).astype(BF)
        mids[2, at] = act.astype(BF)
        mids[1, at] = (up * sig * (1.0 + gate * (1.0 - sig))).astype(BF)
        if i == 0:
            ag.relay()
            zd.relay()
            continue
        if i == 1:
            zd.wait()
        rs.give(g.leave_index(i), dot(mids[0, at], wm[2], NT))
    own = middle[...] + dot(mids[0, g.rows(g.t)], wm[2], NT)
    wo_t[...] = turned(wa[3])
    rs.relay()
    result = rs.total(own)
    output[...] = result

    get_teacher.wait()
    total = cnt[2]
    for k in range(1, C):
        zc.recv(cz[k - 1], cnt.at[2 + k], (g.zfrom(k), g.t))
        total = total + cnt[2 + k]
    stats[1] = total
    keep = kinfo[g.rows(g.t), 2:3].astype(F32)
    dev = result - cot[...]
    cotangent = keep * dev
    rows_error = jnp.sum(jnp.sum(cotangent * dev, axis=1, keepdims=True), axis=0, keepdims=True)
    err[0] = jnp.broadcast_to(rows_error, (8, 128))
    cotangent = cotangent * (1.0 * S * g.n_dp / total[0:1, 0:1])
    cot[...] = cotangent
    gm[g.rows(g.t)] = cotangent.astype(BF)

    ag = Gather(g, tc, gm)
    rs = Scatter(g, tc, sums)
    te = tc.slots(2 if g.square else g.n_t - 1)
    if g.square:
        tc.send(few, te[0], err.at[0], err.at[1], (g.d, g.tx))
    else:
        for k, peer in enumerate(g.to):
            tc.send(few, te[k], err.at[0], err.at[1 + k], (g.d, peer))
    for i, blk in enumerate(g.arrive):
        ag.wait(i)
        at = g.rows(blk)
        gh = dot(gm[at], wm[2])
        mids[1, at] = (gh * mids[1, at].astype(F32)).astype(BF)
        mids[2, at] = (gh * mids[2, at].astype(F32)).astype(BF)
        if i == 0:
            ag.relay()
            tc.sent(ag2.group)
            rows2[...] = turned(rows2[...])
            turn[...] = turned(kk[...])
            continue
        rs.give(g.leave_index(i), dot(mids[1, at], wm[0], NT) + dot(mids[2, at], wm[1], NT))
    at = g.rows(g.t)
    own = dot(mids[1, at], wm[0], NT) + dot(mids[2, at], wm[1], NT)
    grad_inputs[...] = own
    zc.sent(zg.group)
    zc.sent(zd.group)
    wm[0] = dot(rows2[...], mids[1]).astype(BF)

    zscat = []

    def start_mlp(j, used):
        spare = [mids.at[used, k * Dn : (k + 1) * Dn] for k in range(C - 1)]
        zscat.append(WeightScatter(g, zc, wm.at[j], (sib_m.at[j], spare, fin_m.at[j], mid_m.at[j])))

    start_mlp(0, 1)
    rs.relay()
    wm[1] = dot(rows2[...], mids[2]).astype(BF)
    start_mlp(1, 2)
    zscat[0].pass_on()
    for k in range(0, g.D, 256):
        wm[2, k : k + 256] = dot(turned(gm[:, k : k + 256]), mids[0]).astype(BF)
    start_mlp(2, 0)
    zscat[1].pass_on()
    back = rs.total(grad_inputs[...])
    two, inv = normed(middle[...])
    grad_middle = cot[...] + normed_back(two, inv, back)
    cot[...] = grad_middle
    ga[g.rows(g.t)] = grad_middle.astype(BF)

    ag = Gather(g, tc, ga)
    rs = Scatter(g, tc, sums)
    zscat[2].pass_on()
    if g.square:
        tc.recv(te[0], err.at[1], (g.d, g.tx))
        err[2] = err[0] + err[1]
        tc.send(few, te[1], err.at[2], err.at[3], (g.d, g.ty))
    acc2[...] = jnp.zeros_like(acc2)
    for i, blk in enumerate(g.arrive):
        if i == 1:
            zscat[0].relay()
            tc.sent(ag1.group)
            rows1[...] = turned(rows1[...])
        ag.wait(i)
        at = g.rows(blk)
        go_t = dot(wo_t[...], ga[at], NT).astype(BF).astype(F32)
        mix_t = mixt[blk].astype(F32)
        scaled, dots = [], []
        for h in range(H):
            one_head = go_t[h * HD : (h + 1) * HD] * rinv[blk, h : h + 1, :]
            scaled.append(one_head)
            dots.append(jnp.sum(one_head * mix_t[h * HD : (h + 1) * HD], axis=0, keepdims=True))
        go = jnp.concatenate(scaled, axis=0).T.astype(BF)
        q_blk = q[at]
        for h in range(H):
            gom[h * R : (h + 1) * R] = head_lanes(go, h)
            qm[h * R : (h + 1) * R] = head_lanes(q_blk, h)

        @in_slot(g, n_pic, blk)
        def _(p, index, hi, blk=blk, at=at, dots=dots):
            keys = slice(0, hi)
            dv[keys] += dot(probs[p][index], gom[...])
            dqs = []
            for h in range(H):
                cols = slice(h * R, (h + 1) * R)
                gp = dot(v[keys], gom[cols], NT)
                d_low = (probs[p][index, :, cols].astype(F32) * (gp - dots[h])).astype(BF)
                probs[p][index, :, cols] = d_low
                dqs.append(dot(turn[h * HD : (h + 1) * HD, keys], d_low))
            dq_blk = jnp.concatenate(dqs, axis=0).T * HD**-0.5
            q[at] = rotated(dq_blk, cosine[at], -sine[at]).astype(BF)
            dk[keys] += dot(probs[p][index], qm[...])

        if i == 0:
            ag.relay()
    for i, blk in enumerate(g.leave):
        at = g.rows(blk)
        kk[at] = rotated(dk[at], cosine[at], -sine[at]).astype(BF)
        v[at] = dv[at].astype(BF)
        partial = dot(q[at], wa[0], NT) + dot(kk[at], wa[1], NT) + dot(v[at], wa[2], NT)
        if i < g.n_t - 1:
            rs.give(i, partial)
        else:
            grad_inputs[...] = partial
    zscat[1].relay()

    zc.sent(za.group)
    for j in range(3):
        wa[j] = dot(rows1[...], qkv[j]).astype(BF)
        zscat.append(WeightScatter(g, zc, wa.at[j], (sib_a.at[j], [out_a.at[j, k] for k in range(C - 1)], fin_a.at[j], mid_a.at[j])))
    rs.relay()
    for j in range(3):
        zscat[3 + j].pass_on()
    zscat[2].relay()
    for k in range(0, g.D, 256):
        wa[3, k : k + 256] = dot(turned(ga[:, k : k + 256]), mixed[...]).astype(BF)
    zscat.append(WeightScatter(g, zc, wa.at[3], (sib_a.at[3], [out_a.at[3, k] for k in range(C - 1)], fin_a.at[3], mid_a.at[3])))
    zscat[6].pass_on()

    base = 4 if g.square else g.n_t
    if g.square:
        tc.recv(te[1], err.at[3], (g.d, g.ty))
        err[base] = err[2] + err[3]
    else:
        total = err[0]
        for k in range(1, g.n_t):
            tc.recv(te[k - 1], err.at[k], (g.d, g.arrive[k]))
            total = total + err[k]
        err[base] = total
    ec, ez = zc.slots(1)[0], zc.slots(C - 1)
    zc.send(zfew, ec, err.at[base], err.at[base + 1], (g.sib, g.t))
    zc.recv(ec, err.at[base + 1], (g.sib, g.t))
    err[base + 2] = err[base] + err[base + 1]
    for k in range(1, C):
        zc.send(zfew, ez[k - 1], err.at[base + 2], err.at[base + 2 + k], (g.zto(k), g.t))
    for j in range(3):
        zscat[3 + j].relay()
    zscat[6].relay()
    for j in range(3):
        zscat[j].total(dmlp.at[j])
    one, inv = normed(x[...])
    grad_inputs[...] = cot[...] + normed_back(one, inv, rs.total(grad_inputs[...]))
    for j in range(4):
        zscat[3 + j].total(dattn.at[j])
    total = err[base + 2]
    for k in range(1, C):
        zc.recv(ez[k - 1], err.at[base + 2 + k], (g.zfrom(k), g.t))
        total = total + err[base + 2 + k]
    stats[0] = total * (1.0 / g.D) / stats[1]
    tc.finish()
    zc.finish()


def layer(g, n_pic, args):
    S, R, D, c, f, H, C, Dn = g.S, g.R, g.D, g.c, g.f, g.H, g.C, g.Dn
    sds, V = jax.ShapeDtypeStruct, pltpu.VMEM
    outs = [sds((R, D), F32), sds((R, D), F32), sds((4, Dn, c), F32), sds((3, Dn, f), F32), sds((2, 8, 128), F32)]
    base = 4 if g.square else g.n_t
    scratch = [V((S, D), BF)] * 4 + [
        V((4, D, c), BF), V((3, D, f), BF), V((3, S, c), BF), V((S, c), BF), V((g.n_t, c, R), BF), V((c, S), BF), V((c, D), BF),
        V((g.n_t // 2, S // 2, H * R), BF), V((g.n_t // 2, S, H * R), BF), V((2, S, max(R, c)), F32), V((H * R, c), BF), V((H * R, c), BF), V((3, S, f), BF),
        V((R, D), F32), V((R, D), F32), V((8, S), jnp.int32), V((S, 128), jnp.int32), V((g.n_t, 8, R), F32),
        V((2 + C, 8, 128), F32), V((base + 2 + C, 8, 128), F32),
    ]
    scratch += scatter_scratch(g)
    m = weight_scatter_scratch(g, 3, f)
    scratch += [m[0], m[2], m[3]] + weight_scatter_scratch(g, 4, c)
    nt = 4 * 6 + 4 * 6 + 2 if g.square else 9 * (g.n_t - 1)
    nz = 10 * (2 * C + 1) + 2 * C
    sem = pltpu.SemaphoreType.DMA
    scratch += [sem((nt,)), sem((nt,)), sem((nz,)), sem((nz,)), sem((1,))]
    whole = pl.BlockSpec(memory_space=pltpu.VMEM)
    specs = [whole] * len(args)
    specs[1] = pl.BlockSpec(memory_space=pl.ANY)
    return pl.pallas_call(
        functools.partial(layer_body, g, n_pic),
        name="layer",
        out_shape=outs,
        in_specs=specs,
        out_specs=[whole] * len(outs),
        scratch_shapes=scratch,
        compiler_params=pltpu.CompilerParams(collective_id=1, has_side_effects=True, vmem_limit_bytes=VMEM_BYTES),
    )(*args)


def finish_body(output, grad_inputs, dattn, dmlp, stats, o_out, o_loss, o_in, o_q, o_k, o_v, o_o, o_g, o_u, o_d):
    o_out[...] = output[...]
    o_in[...] = grad_inputs[...]
    o_q[...] = dattn[0]
    o_k[...] = dattn[1]
    o_v[...] = dattn[2]
    o_o[...] = dattn[3].T
    o_g[...] = dmlp[0].T
    o_u[...] = dmlp[1].T
    o_d[...] = dmlp[2].T
    o_loss[0, 0] = stats[0, 0, 0]


def finish(g, parts):
    R, D, c, f, Dn = g.R, g.D, g.c, g.f, g.Dn
    sds = jax.ShapeDtypeStruct
    shapes = [(R, D), (1, 1), (R, D), (Dn, c), (Dn, c), (Dn, c), (c, Dn), (f, Dn), (f, Dn), (f, Dn)]
    whole = pl.BlockSpec(memory_space=pltpu.VMEM)
    specs = [whole] * len(shapes)
    specs[1] = pl.BlockSpec(memory_space=pltpu.SMEM)
    return pl.pallas_call(
        finish_body,
        name="finish",
        out_shape=[sds(s, F32) for s in shapes],
        in_specs=[whole] * len(parts),
        out_specs=specs,
        compiler_params=pltpu.CompilerParams(vmem_limit_bytes=VMEM_BYTES),
    )(*parts)


def per_device(n_dp, n_t, inputs, teacher, valid_mask, documents, picture_starts,
               w_query, w_key, w_value, w_out, w_gate, w_up, w_down):
    R, D = inputs.shape
    c, f = w_query.shape[1], w_gate.shape[1]
    g = Geo(n_dp, n_t, R, D, c, f)
    args = (inputs, teacher, valid_mask, documents, picture_starts, w_query, w_key, w_value, w_out, w_gate.T, w_up.T, w_down)
    parts = layer(g, picture_starts.shape[1], (*args, *rotary(g.S, c)))
    out, loss, *grads, gate, up, down = finish(g, parts)
    return (out, loss.reshape(()), *grads, gate.T, up.T, down)


def solution(mesh):
    rows, pair = P(("dp", "tensor"), None), P("dp", None)
    cut, across = P("dp", "tensor"), P("tensor", "dp")
    return jax.shard_map(
        functools.partial(per_device, mesh.shape["dp"], mesh.shape["tensor"]),
        mesh=mesh,
        in_specs=(rows, rows, pair, pair, pair, cut, cut, cut, across, cut, cut, across),
        out_specs=(rows, P(), rows, cut, cut, cut, across, cut, cut, across),
        check_vma=False,
    )
```

```python
import functools

import jax
import jax.numpy as jnp
import numpy as np
from jax import lax
from jax.experimental import pallas as pl
from jax.experimental.pallas import tpu as pltpu
from jax.sharding import PartitionSpec as P

MESH = pl.DeviceIdType.MESH
HD = 64
PIECE = 256
EPS = 1e-5
MASKED = -1e30
VMEM_BYTES = 60 * 2**20
BF = jnp.bfloat16
F32 = jnp.float32
NT = (((1,), (1,)), ((), ()))
NN = (((1,), (0,)), ((), ()))


def dot(a, b, dims=NN):
    return lax.dot_general(a, b, dims, preferred_element_type=F32)


def eye(n):
    return (
        lax.broadcasted_iota(jnp.int32, (n, n), 0) == lax.broadcasted_iota(jnp.int32, (n, n), 1)
    ).astype(F32).astype(BF)


def turned(a):
    n = a.shape[1]
    step = min(n, 256)
    parts = [dot(eye(step), a[:, k : k + step], NT).astype(BF) for k in range(0, n, step)]
    return parts[0] if len(parts) == 1 else jnp.concatenate(parts, axis=0)


def mean_of(v):
    return jnp.sum(v, axis=1, keepdims=True) * (1.0 / v.shape[1])


def normed(v):
    centred = v - mean_of(v)
    inv = lax.rsqrt(mean_of(centred * centred) + EPS)
    return centred * inv, inv


def normed_back(n, inv, g):
    return inv * (g - mean_of(g) - n * mean_of(g * n))


class Geo:
    def __init__(self, n_dp, n_t, tok_rows, d_model, cols, hid):
        self.n_dp, self.n_t, self.R, self.D, self.c, self.f = n_dp, n_t, tok_rows, d_model, cols, hid
        self.C = n_dp // 2
        self.S = tok_rows * n_t
        self.H = cols // HD
        self.Dn = d_model // n_dp
        self.square = n_t == 4
        self.line = self.C == 4

    def place(self):
        self.d = lax.axis_index("dp")
        self.t = lax.axis_index("tensor")
        self.chip = self.d // 2
        self.core = self.d % 2
        if self.square:
            self.tx = self.t + 1 - 2 * (self.t % 2)
            self.ty = (self.t + 2) % 4
            self.td = 3 - self.t
            self.to = [self.tx, self.ty]
            self.arrive = [self.t, self.tx, self.ty, self.td]
            self.leave = [self.td, self.tx, self.ty, self.t]
        else:
            n = self.n_t
            self.to = [(self.t + k) % n for k in range(1, n)]
            self.arrive = [(self.t + n - k) % n for k in range(n)]
            self.leave = [(self.t + k) % n for k in range(1, n)] + [self.t]
        self.sib = self.d + 1 - 2 * self.core
        return self

    def leave_index(self, i):
        if self.square:
            return (3, 1, 2, 0)[i]
        return self.n_t - 1 - i if i else self.n_t - 1

    def zto(self, k):
        return ((self.chip + k) % self.C) * 2 + self.core

    def zfrom(self, k):
        return ((self.chip + self.C - k) % self.C) * 2 + self.core

    def rows(self, blk, first=0, count=None):
        count = self.R if count is None else count
        return pl.ds(pl.multiple_of(blk * self.R + first, count), count)

    def wrows(self, d):
        return pl.ds(pl.multiple_of(d * self.Dn, self.Dn), self.Dn)

    def greet(self):
        bar = pltpu.get_barrier_semaphore()
        out = [(self.d, p) for p in self.to]
        out += [(self.zto(k), self.t) for k in range(1, self.C)] + [(self.sib, self.t)]
        for dev in out:
            pl.semaphore_signal(bar, inc=1, device_id=dev, device_id_type=MESH)
        self.met = len(out)

    def meet(self):
        pl.semaphore_wait(pltpu.get_barrier_semaphore(), self.met)


class Comm:
    def __init__(self, send_sem, recv_sem):
        self.ss, self.rs = send_sem, recv_sem
        self.n = 0
        self.groups = []

    def group(self):
        self.groups.append([])
        return self.groups[-1]

    def slots(self, k):
        self.n += k
        return list(range(self.n - k, self.n))

    def _copy(self, slot, src, dst, dev, send_slot=None):
        return pltpu.make_async_remote_copy(
            src_ref=src, dst_ref=dst, send_sem=self.ss.at[slot if send_slot is None else send_slot],
            recv_sem=self.rs.at[slot], device_id=dev, device_id_type=MESH,
        )

    def send(self, group, slot, src, dst, dev, when=None, send_slot=None):
        copy = self._copy(slot, src, dst, dev, send_slot)
        if when is None:
            copy.start()
        else:
            pl.when(when)(copy.start)
        group.append((when, copy))

    def recv(self, slot, dst, dev, when=None):
        copy = self._copy(slot, dst, dst, dev)
        if when is None:
            copy.wait_recv()
        else:
            pl.when(when)(copy.wait_recv)

    def sent(self, group):
        for when, copy in group:
            if when is None:
                copy.wait_send()
            else:
                pl.when(when)(copy.wait_send)
        group.clear()

    def finish(self):
        for group in self.groups:
            self.sent(group)


class Gather:
    def __init__(self, geo, comm, buf):
        self.g, self.comm, self.buf = geo, comm, buf
        g = geo
        self.group = comm.group()
        if g.square:
            self.sx, self.sy = comm.slots(3), comm.slots(3)
            h0, h1 = self.half(g.t, 0), self.half(g.t, 1)
            comm.send(self.group, self.sx[0], h0, h0, (g.d, g.tx))
            comm.send(self.group, self.sy[1], h1, h1, (g.d, g.ty))
            comm.send(self.group, self.sx[1], h1, h1, (g.d, g.tx))
            comm.send(self.group, self.sy[0], h0, h0, (g.d, g.ty))
        else:
            self.s = comm.slots(g.n_t - 1)
            own = buf.at[g.rows(g.t)]
            for k, peer in enumerate(g.to):
                comm.send(self.group, self.s[k], own, own, (g.d, peer))

    def half(self, blk, i):
        h = self.g.R // 2
        return self.buf.at[self.g.rows(blk, i * h, h)]

    def relay(self):
        g, comm = self.g, self.comm
        if g.square:
            a = self.half(g.tx, 0)
            comm.recv(self.sx[0], a, (g.d, g.tx))
            comm.send(self.group, self.sy[2], a, a, (g.d, g.ty))
            b = self.half(g.ty, 1)
            comm.recv(self.sy[1], b, (g.d, g.ty))
            comm.send(self.group, self.sx[2], b, b, (g.d, g.tx))

    def wait(self, i):
        g, comm = self.g, self.comm
        if i == 0:
            return
        if not g.square:
            comm.recv(self.s[i - 1], self.buf.at[g.rows(g.arrive[i])], (g.d, g.arrive[i]))
        elif i == 1:
            comm.recv(self.sx[1], self.half(g.tx, 1), (g.d, g.tx))
        elif i == 2:
            comm.recv(self.sy[0], self.half(g.ty, 0), (g.d, g.ty))
        else:
            comm.recv(self.sx[2], self.half(g.td, 1), (g.d, g.tx))
            comm.recv(self.sy[2], self.half(g.td, 0), (g.d, g.ty))


def scatter_scratch(g):
    h = g.R // 2
    if g.square:
        return [pltpu.VMEM((3, 2, h, g.D), BF), pltpu.VMEM((2, h, g.D), BF), pltpu.VMEM((2, h, g.D), BF), pltpu.VMEM((2, 2, h, g.D), BF)]
    return [pltpu.VMEM((g.n_t - 1, 2, h, g.D), BF), pltpu.VMEM((1, 16, 128), BF), pltpu.VMEM((1, 16, 128), BF), pltpu.VMEM((g.n_t - 1, 2, h, g.D), BF)]


class Scatter:
    def __init__(self, geo, comm, bufs):
        self.g, self.comm = geo, comm
        self.part, self.into, self.out, self.fin = bufs
        g = geo
        self.group = comm.group()
        if g.square:
            self.sx, self.sy = comm.slots(3), comm.slots(3)
        else:
            self.s = comm.slots(g.n_t - 1)

    def give(self, i, value):
        g, comm = self.g, self.comm
        h = g.R // 2
        for j in range(2):
            self.part[i, j] = value[j * h : (j + 1) * h].astype(BF)
        if not g.square:
            comm.send(self.group, self.s[i], self.part.at[i], self.fin.at[i], (g.d, g.leave[i]))
        elif i == 0:
            comm.send(self.group, self.sx[0], self.part.at[0, 0], self.into.at[0], (g.d, g.tx))
            comm.send(self.group, self.sy[0], self.part.at[0, 1], self.into.at[1], (g.d, g.ty))
        elif i == 1:
            comm.send(self.group, self.sx[1], self.part.at[1, 0], self.fin.at[0, 0], (g.d, g.tx))
        else:
            comm.send(self.group, self.sy[1], self.part.at[2, 1], self.fin.at[1, 1], (g.d, g.ty))

    def relay(self):
        g, comm = self.g, self.comm
        if not g.square:
            return
        comm.recv(self.sx[0], self.into.at[0], (g.d, g.tx))
        self.out[0] = (self.into[0].astype(F32) + self.part[2, 0].astype(F32)).astype(BF)
        comm.send(self.group, self.sy[2], self.out.at[0], self.fin.at[1, 0], (g.d, g.ty))
        comm.recv(self.sy[0], self.into.at[1], (g.d, g.ty))
        self.out[1] = (self.into[1].astype(F32) + self.part[1, 1].astype(F32)).astype(BF)
        comm.send(self.group, self.sx[2], self.out.at[1], self.fin.at[0, 1], (g.d, g.tx))

    def total(self, own):
        g, comm = self.g, self.comm
        h = g.R // 2
        if g.square:
            comm.recv(self.sx[1], self.fin.at[0, 0], (g.d, g.tx))
            comm.recv(self.sy[1], self.fin.at[1, 1], (g.d, g.ty))
            comm.recv(self.sx[2], self.fin.at[0, 1], (g.d, g.tx))
            comm.recv(self.sy[2], self.fin.at[1, 0], (g.d, g.ty))
            count = 2
        else:
            count = g.n_t - 1
            for k in range(count):
                comm.recv(self.s[k], self.fin.at[k], (g.d, g.arrive[k + 1]))
        halves = []
        for j in range(2):
            v = own[j * h : (j + 1) * h]
            for k in range(count):
                v = v + self.fin[k, j].astype(F32)
            halves.append(v)
        comm.sent(self.group)
        return jnp.concatenate(halves, axis=0)


class WeightGather:
    def __init__(self, geo, comm, buf, first, n):
        self.g, self.comm, self.buf, self.of = geo, comm, buf, pl.ds(first, n)
        g = geo
        self.group = comm.group()
        self.inner = (g.chip == 1) | (g.chip == 2)
        self.sz, self.sc, self.sr = comm.slots(g.C - 1), comm.slots(g.C), comm.slots(2)

    def at(self, d):
        return self.buf.at[self.of, self.g.wrows(d)]

    def far(self):
        g, comm = self.g, self.comm
        if g.line:
            comm.send(self.group, self.sz[1], self.at(g.d), self.at(g.d), (g.zto(2), g.t))

    def near(self):
        g, comm = self.g, self.comm
        own = self.at(g.d)
        for k in range(1, g.C):
            if g.line and k == 2:
                continue
            near = g.chip != (0 if k == 3 else 3) if g.line else None
            comm.send(self.group, self.sz[k - 1], own, own, (g.zto(k), g.t), when=near)
        comm.send(self.group, self.sc[0], own, own, (g.sib, g.t))

    def _take(self, k, when=None):
        g, comm = self.g, self.comm
        block = self.at(g.zfrom(k))
        comm.recv(self.sz[k - 1], block, (g.zfrom(k), g.t), when=when)
        comm.send(self.group, self.sc[k], block, block, (g.sib, g.t), when=when)

    def relay(self):
        g, comm = self.g, self.comm
        if not g.line:
            return
        self._take(2, self.inner)
        block = self.at(g.zfrom(2))
        comm.send(self.group, self.sz[2], block, block, (6 + g.core, g.t), when=g.chip == 2, send_slot=self.sr[0])
        comm.send(self.group, self.sz[0], block, block, (g.core, g.t), when=g.chip == 1, send_slot=self.sr[1])

    def pass_on(self):
        g = self.g
        for k in range(1, g.C):
            self._take(k, jnp.logical_not(self.inner) if g.line and k == 2 else None)

    def wait(self):
        g, comm = self.g, self.comm
        for k in range(g.C):
            other = g.zfrom(k) + 1 - 2 * g.core
            comm.recv(self.sc[k], self.at(other), (g.sib, g.t))


class WeightScatter:
    def __init__(self, geo, comm, src, bufs):
        self.g, self.comm, self.src = geo, comm, src
        self.sib_in, self.out, self.fin, self.mid = bufs
        g = geo
        self.group = comm.group()
        self.sc, self.sz, self.sr = comm.slots(g.C), comm.slots(g.C - 1), comm.slots(2)
        for j in range(g.C):
            block = self.src.at[g.wrows(2 * j + 1 - g.core)]
            comm.send(self.group, self.sc[j], block, self.sib_in.at[j], (g.sib, g.t))

    def _sum(self, k):
        g = self.g
        to = (g.chip + k) % g.C
        return self.src[g.wrows(2 * to + g.core)].astype(F32) + self.sib_in[to].astype(F32)

    def _send(self, k, when=None):
        g = self.g
        self.comm.send(self.group, self.sz[k - 1], self.out[k - 1], self.fin.at[k - 1], (g.zto(k), g.t), when=when)

    def pass_on(self):
        g, comm = self.g, self.comm
        for j in range(g.C):
            comm.recv(self.sc[j], self.sib_in.at[j], (g.sib, g.t))
        if not g.line:
            for k in range(1, g.C):
                self.out[k - 1][...] = self._sum(k).astype(BF)
                self._send(k)
            return
        self.out[2][...] = self._sum(3).astype(BF)
        comm.send(self.group, self.sr[0], self.out[2], self.mid, (2 + g.core, g.t), when=g.chip == 0)
        self._send(3, when=g.chip != 0)
        self.out[0][...] = self._sum(1).astype(BF)
        comm.send(self.group, self.sr[0], self.out[0], self.mid, (4 + g.core, g.t), when=g.chip == 3, send_slot=self.sr[1])
        self._send(1, when=g.chip != 3)

        @pl.when((g.chip == 0) | (g.chip == 3))
        def _():
            self.out[1][...] = self._sum(2).astype(BF)

        self._send(2, when=(g.chip == 0) | (g.chip == 3))

    def relay(self):
        g, comm = self.g, self.comm
        if not g.line:
            return
        inner = (g.chip == 1) | (g.chip == 2)

        @pl.when(inner)
        def _():
            comm.recv(self.sr[0], self.mid, (g.sib, g.t))
            self.out[1][...] = (self._sum(2) + self.mid[...].astype(F32)).astype(BF)

        self.comm.send(self.group, self.sz[1], self.out[1], self.fin.at[1], (g.zto(2), g.t), when=inner, send_slot=None)

    def total(self, into):
        g, comm = self.g, self.comm
        into[...] = self.src[g.wrows(g.d)].astype(F32) + self.sib_in[g.chip].astype(F32)
        for k in range(1, g.C):

            def add(k=k):
                comm.recv(self.sz[k - 1], self.fin.at[k - 1], (g.zfrom(k), g.t))
                into[...] += self.fin[k - 1].astype(F32)

            if g.line and k != 2:
                pl.when(g.chip != (3 if k == 3 else 0))(add)
            else:
                add()


def weight_scatter_scratch(g, n, w):
    return [pltpu.VMEM((n, g.C, g.Dn, w), BF), pltpu.VMEM((n, g.C - 1, g.Dn, w), BF),
            pltpu.VMEM((n, g.C - 1, g.Dn, w), BF), pltpu.VMEM((n, g.Dn, w), BF)]


def rotated(v, cosine, sine):
    n = v.shape[1]
    if n > cosine.shape[1]:
        cosine = jnp.concatenate([cosine] * (n // cosine.shape[1]), axis=1)
        sine = jnp.concatenate([sine] * (n // sine.shape[1]), axis=1)
    lower = lax.broadcasted_iota(jnp.int32, v.shape, 1) % HD < HD // 2
    swapped = jnp.where(lower, pltpu.roll(v, n - HD // 2, 1), pltpu.roll(v, HD // 2, 1))
    return v * cosine + swapped * sine


def head_lanes(v, h):
    lane = lax.broadcasted_iota(jnp.int32, v.shape, 1)
    keep = (lane >= h * HD) & (lane < (h + 1) * HD)
    return jnp.where(keep, v, jnp.zeros_like(v))


def bias_of(qinfo, kinfo, first, size, rows):
    shape = (size, rows)
    doc_q, pic_q = qinfo[0:1, :], qinfo[1:2, :]
    key_doc, pic_k = kinfo[:, 0:1], kinfo[:, 1:2]
    key_pos = lax.broadcasted_iota(jnp.int32, shape, 0)
    query_pos = lax.broadcasted_iota(jnp.int32, shape, 1) + first
    before = key_pos <= query_pos
    open_ = (doc_q == key_doc) & (before | (pic_q == pic_k))
    ok = open_ | (key_pos == query_pos)
    return jnp.where(ok, 0.0, MASKED).astype(F32)


def rotary(length, cols):
    half = HD // 2
    frequency = 10000.0 ** (-2.0 * np.arange(half) / HD)
    angle = np.arange(length)[:, None] * frequency[None, :]
    cosine = np.concatenate([np.cos(angle)] * 2, axis=1)
    sine = np.concatenate([-np.sin(angle), np.sin(angle)], axis=1)
    reps = max(1, min(cols, 128) // HD)
    return (jnp.asarray(np.tile(cosine, (1, reps)), F32), jnp.asarray(np.tile(sine, (1, reps)), F32))


def in_slot(g, n_pic, blk):
    per = g.n_t // n_pic

    def run(body):
        for p in range(n_pic):
            pl.when(blk // per == p)(functools.partial(body, p, blk - p * per, (p + 1) * (g.S // n_pic)))

    return run


def layer_body(g, n_pic, x, teacher, valid_mask, documents, starts, wq, wk, wv, wo, wg, wu, wd, cosine, sine,
               output, grad_inputs, dattn, dmlp, stats,
               rows1, rows2, gm, ga, wa, wm, qkv, mixed, mixt, turn, wo_t, probs0, probs1, acc2, qm, gom, mids, middle, cot,
               qinfo, kinfo, rinv, cnt, err,
               part, into, out, fin,
               sib_m, fin_m, mid_m, sib_a, out_a, fin_a, mid_a,
               ts, tr, zs, zr, local):
    g.place()
    g.greet()
    R, S, c, H, C, Dn = g.R, g.S, g.c, g.H, g.C, g.Dn
    tc, zc = Comm(ts, tr), Comm(zs, zr)
    few, zfew = tc.group(), zc.group()
    sums = (part, into, out, fin)
    q, kk, v = qkv.at[0], qkv.at[1], qkv.at[2]
    probs = (probs0, probs1)
    bias, dk, dv = acc2.at[0, :, :R], acc2.at[0, :, :c], acc2.at[1, :, :c]
    get_teacher = pltpu.make_async_copy(teacher, cot, local.at[0])
    get_teacher.start()

    one, _ = normed(x[...])
    rows1[g.rows(g.t)] = one.astype(BF)
    mine = g.wrows(g.d)
    wa[0, mine] = wq[...]
    wa[1, mine] = wk[...]
    wa[2, mine] = wv[...]
    g.meet()
    ag = ag1 = Gather(g, tc, rows1)
    za, zo = WeightGather(g, zc, wa, 0, 3), WeightGather(g, zc, wa, 3, 1)
    zg, zd = WeightGather(g, zc, wm, 0, 2), WeightGather(g, zc, wm, 2, 1)
    za.far()
    wa[3, mine] = turned(wo[...])
    zo.far()
    za.near()
    wm[0, mine] = turned(wg[...])
    wm[1, mine] = turned(wu[...])
    wm[2, mine] = turned(wd[...])

    csib, cz = zc.slots(1)[0], zc.slots(C - 1)
    valid, doc = valid_mask[...], documents[...]
    cnt[0] = jnp.broadcast_to(jnp.sum(valid.astype(F32), axis=1, keepdims=True), (8, 128))
    zc.send(zfew, csib, cnt.at[0], cnt.at[1], (g.sib, g.t))
    at = lax.broadcasted_iota(jnp.int32, (1, S), 1)
    pic = jnp.zeros((1, S), jnp.int32)
    for p in range(n_pic):
        first = starts[0:1, p : p + 1]
        pic = jnp.where((at >= first) & (at < first + PIECE), p + 1, pic)
    qinfo[0:1] = doc
    qinfo[1:2] = pic
    as_keys = [jnp.where(valid == 1, doc, -1), jnp.where(pic > 0, pic, -1), valid]
    as_keys = jnp.concatenate([a.astype(F32) for a in as_keys] + [jnp.zeros((125, S), F32)], axis=0)
    kinfo[...] = as_keys.T.astype(jnp.int32)
    zc.recv(csib, cnt.at[1], (g.sib, g.t))
    cnt[2] = cnt[0] + cnt[1]
    for k in range(1, C):
        zc.send(zfew, cz[k - 1], cnt.at[2], cnt.at[2 + k], (g.zto(k), g.t))

    ag.relay()
    za.relay()
    zo.relay()
    zo.near()
    za.pass_on()
    za.wait()
    zg.far()
    zg.near()
    for i, blk in enumerate(g.arrive):
        ag.wait(i)
        at = g.rows(blk)
        row = rows1[at]
        cos_b, sin_b = cosine[at], sine[at]
        q[at] = (rotated(dot(row, wa[0]), cos_b, sin_b) * HD**-0.5).astype(BF)
        kk[at] = rotated(dot(row, wa[1]), cos_b, sin_b).astype(BF)
        v[at] = dot(row, wa[2]).astype(BF)
    zo.pass_on()
    turn[...] = turned(v[...])

    rs = Scatter(g, tc, sums)
    for i, blk in enumerate(g.leave):
        at = g.rows(blk)

        @in_slot(g, n_pic, blk)
        def _(p, index, hi, blk=blk, at=at):
            keys = slice(0, hi)
            bias[keys] = bias_of(qinfo[:, at], kinfo[keys], blk * R, hi, R)
            q_blk = q[at]
            outs = []
            for h in range(H):
                s = dot(kk[keys], head_lanes(q_blk, h), NT) + bias[keys]
                e = jnp.exp(s - jnp.max(s, axis=0, keepdims=True))
                inv = 1.0 / jnp.sum(e, axis=0, keepdims=True)
                low = e.astype(BF)
                probs[p][index, :, h * R : (h + 1) * R] = low
                rinv[blk, h : h + 1, :] = inv
                outs.append(dot(turn[h * HD : (h + 1) * HD, keys], low) * inv)
            both = jnp.concatenate(outs, axis=0)
            mixt[blk] = both.astype(BF)
            mixed[at] = both.T.astype(BF)

        if i == 0:
            zo.wait()
        if i == 2:
            zg.relay()
            zd.far()
            zd.near()
        partial = dot(mixed[at], wa[3], NT)
        if i < g.n_t - 1:
            rs.give(i, partial)
        else:
            middle[...] = x[...] + partial
    rs.relay()
    middle[...] = rs.total(middle[...])

    two, _ = normed(middle[...])
    rows2[g.rows(g.t)] = two.astype(BF)
    ag = ag2 = Gather(g, tc, rows2)
    rs = Scatter(g, tc, sums)
    zg.pass_on()
    zd.relay()
    zg.wait()
    for i, blk in enumerate(g.arrive):
        ag.wait(i)
        at = g.rows(blk)
        row = rows2[at]
        gate, up = dot(row, wm[0]), dot(row, wm[1])
        sig = jax.nn.sigmoid(gate)
        act = gate * sig
        mids[0, at] = (act * up).astype(BF)
        mids[2, at] = act.astype(BF)
        mids[1, at] = (up * sig * (1.0 + gate * (1.0 - sig))).astype(BF)
        if i == 0:
            ag.relay()
            continue
        if i == 1:
            zd.pass_on()
            zd.wait()
        rs.give(g.leave_index(i), dot(mids[0, at], wm[2], NT))
    own = middle[...] + dot(mids[0, g.rows(g.t)], wm[2], NT)
    wo_t[...] = turned(wa[3])
    rs.relay()
    result = rs.total(own)
    output[...] = result

    get_teacher.wait()
    total = cnt[2]
    for k in range(1, C):
        zc.recv(cz[k - 1], cnt.at[2 + k], (g.zfrom(k), g.t))
        total = total + cnt[2 + k]
    stats[1] = total
    keep = kinfo[g.rows(g.t), 2:3].astype(F32)
    dev = result - cot[...]
    cotangent = keep * dev
    rows_error = jnp.sum(jnp.sum(cotangent * dev, axis=1, keepdims=True), axis=0, keepdims=True)
    err[0] = jnp.broadcast_to(rows_error, (8, 128))
    cotangent = cotangent * (1.0 * S * g.n_dp / total[0:1, 0:1])
    cot[...] = cotangent
    gm[g.rows(g.t)] = cotangent.astype(BF)

    ag = Gather(g, tc, gm)
    rs = Scatter(g, tc, sums)
    te = tc.slots(2 if g.square else g.n_t - 1)
    if g.square:
        tc.send(few, te[0], err.at[0], err.at[1], (g.d, g.tx))
    else:
        for k, peer in enumerate(g.to):
            tc.send(few, te[k], err.at[0], err.at[1 + k], (g.d, peer))
    for i, blk in enumerate(g.arrive):
        ag.wait(i)
        at = g.rows(blk)
        gh = dot(gm[at], wm[2])
        mids[1, at] = (gh * mids[1, at].astype(F32)).astype(BF)
        mids[2, at] = (gh * mids[2, at].astype(F32)).astype(BF)
        if i == 0:
            ag.relay()
            tc.sent(ag2.group)
            rows2[...] = turned(rows2[...])
            turn[...] = turned(kk[...])
            continue
        rs.give(g.leave_index(i), dot(mids[1, at], wm[0], NT) + dot(mids[2, at], wm[1], NT))
    at = g.rows(g.t)
    own = dot(mids[1, at], wm[0], NT) + dot(mids[2, at], wm[1], NT)
    grad_inputs[...] = own
    zc.sent(zg.group)
    zc.sent(zd.group)
    wm[0] = dot(rows2[...], mids[1]).astype(BF)

    zscat = []

    def start_mlp(j, used):
        spare = [mids.at[used, k * Dn : (k + 1) * Dn] for k in range(C - 1)]
        zscat.append(WeightScatter(g, zc, wm.at[j], (sib_m.at[j], spare, fin_m.at[j], mid_m.at[j])))

    start_mlp(0, 1)
    wm[1] = dot(rows2[...], mids[2]).astype(BF)
    start_mlp(1, 2)
    zscat[0].pass_on()
    zscat[1].pass_on()
    rs.relay()
    for k in range(0, g.D, 256):
        wm[2, k : k + 256] = dot(turned(gm[:, k : k + 256]), mids[0]).astype(BF)
    start_mlp(2, 0)
    zscat[0].relay()
    zscat[2].pass_on()
    back = rs.total(grad_inputs[...])
    two, inv = normed(middle[...])
    grad_middle = cot[...] + normed_back(two, inv, back)
    cot[...] = grad_middle
    ga[g.rows(g.t)] = grad_middle.astype(BF)

    def start_attention(j):
        spare = [out_a.at[j, k] for k in range(C - 1)]
        zscat.append(WeightScatter(g, zc, wa.at[j], (sib_a.at[j], spare, fin_a.at[j], mid_a.at[j])))

    ag = Gather(g, tc, ga)
    rs = Scatter(g, tc, sums)
    if g.square:
        tc.recv(te[0], err.at[1], (g.d, g.tx))
        err[2] = err[0] + err[1]
        tc.send(few, te[1], err.at[2], err.at[3], (g.d, g.ty))
    acc2[...] = jnp.zeros_like(acc2)
    for i, blk in enumerate(g.arrive):
        if i == 1:
            zscat[1].relay()
            tc.sent(ag1.group)
            rows1[...] = turned(rows1[...])
        ag.wait(i)
        at = g.rows(blk)
        if i == g.n_t - 1:
            d_out = dot(mixt[0], ga[0 : g.R])
            for k in range(1, g.n_t):
                d_out += dot(mixt[k], ga[k * g.R : (k + 1) * g.R])
            zc.sent(zo.group)
            wa[3] = turned(d_out.astype(BF))
            start_attention(3)
        go_t = dot(wo_t[...], ga[at], NT).astype(BF).astype(F32)
        mix_t = mixt[blk].astype(F32)
        scaled, dots = [], []
        for h in range(H):
            one_head = go_t[h * HD : (h + 1) * HD] * rinv[blk, h : h + 1, :]
            scaled.append(one_head)
            dots.append(jnp.sum(one_head * mix_t[h * HD : (h + 1) * HD], axis=0, keepdims=True))
        go = jnp.concatenate(scaled, axis=0).T.astype(BF)
        q_blk = q[at]
        for h in range(H):
            gom[h * R : (h + 1) * R] = head_lanes(go, h)
            qm[h * R : (h + 1) * R] = head_lanes(q_blk, h)

        @in_slot(g, n_pic, blk)
        def _(p, index, hi, blk=blk, at=at, dots=dots):
            keys = slice(0, hi)
            dv[keys] += dot(probs[p][index], gom[...])
            dqs = []
            for h in range(H):
                cols = slice(h * R, (h + 1) * R)
                gp = dot(v[keys], gom[cols], NT)
                d_low = (probs[p][index, :, cols].astype(F32) * (gp - dots[h])).astype(BF)
                probs[p][index, :, cols] = d_low
                dqs.append(dot(turn[h * HD : (h + 1) * HD, keys], d_low))
            dq_blk = jnp.concatenate(dqs, axis=0).T * HD**-0.5
            q[at] = rotated(dq_blk, cosine[at], -sine[at]).astype(BF)
            dk[keys] += dot(probs[p][index], qm[...])

        if i == 0:
            ag.relay()
        if i == 2:
            zscat[2].relay()
    for i, blk in enumerate(g.leave):
        at = g.rows(blk)
        kk[at] = rotated(dk[at], cosine[at], -sine[at]).astype(BF)
        v[at] = dv[at].astype(BF)
        partial = dot(q[at], wa[0], NT) + dot(kk[at], wa[1], NT) + dot(v[at], wa[2], NT)
        if i < g.n_t - 1:
            rs.give(i, partial)
        else:
            grad_inputs[...] = partial

    zc.sent(za.group)
    for j in range(3):
        wa[j] = dot(rows1[...], qkv[j]).astype(BF)
        start_attention(j)
        zscat[3 + j].pass_on()
    zscat[6].pass_on()
    rs.relay()
    for j in range(3):
        zscat[3 + j].relay()

    base = 4 if g.square else g.n_t
    if g.square:
        tc.recv(te[1], err.at[3], (g.d, g.ty))
        err[base] = err[2] + err[3]
    else:
        total = err[0]
        for k in range(1, g.n_t):
            tc.recv(te[k - 1], err.at[k], (g.d, g.arrive[k]))
            total = total + err[k]
        err[base] = total
    ec, ez = zc.slots(1)[0], zc.slots(C - 1)
    zc.send(zfew, ec, err.at[base], err.at[base + 1], (g.sib, g.t))
    zc.recv(ec, err.at[base + 1], (g.sib, g.t))
    err[base + 2] = err[base] + err[base + 1]
    for k in range(1, C):
        zc.send(zfew, ez[k - 1], err.at[base + 2], err.at[base + 2 + k], (g.zto(k), g.t))
    for j in range(3):
        zscat[j].total(dmlp.at[j])
    zscat[6].relay()
    one, inv = normed(x[...])
    grad_inputs[...] = cot[...] + normed_back(one, inv, rs.total(grad_inputs[...]))
    for j in range(4):
        zscat[3 + j].total(dattn.at[(3, 0, 1, 2)[j]])
    total = err[base + 2]
    for k in range(1, C):
        zc.recv(ez[k - 1], err.at[base + 2 + k], (g.zfrom(k), g.t))
        total = total + err[base + 2 + k]
    stats[0] = total * (1.0 / g.D) / stats[1]
    tc.finish()
    zc.finish()
    assert tc.n <= ts.shape[0] and zc.n <= zs.shape[0]


def layer(g, n_pic, args):
    S, R, D, c, f, H, C, Dn = g.S, g.R, g.D, g.c, g.f, g.H, g.C, g.Dn
    sds, V = jax.ShapeDtypeStruct, pltpu.VMEM
    outs = [sds((R, D), F32), sds((R, D), F32), sds((4, Dn, c), F32), sds((3, Dn, f), F32), sds((2, 8, 128), F32)]
    base = 4 if g.square else g.n_t
    scratch = [V((S, D), BF)] * 4 + [
        V((4, D, c), BF), V((3, D, f), BF), V((3, S, c), BF), V((S, c), BF), V((g.n_t, c, R), BF), V((c, S), BF), V((c, D), BF),
        V((g.n_t // 2, S // 2, H * R), BF), V((g.n_t // 2, S, H * R), BF), V((2, S, max(R, c)), F32), V((H * R, c), BF), V((H * R, c), BF), V((3, S, f), BF),
        V((R, D), F32), V((R, D), F32), V((8, S), jnp.int32), V((S, 128), jnp.int32), V((g.n_t, 8, R), F32),
        V((2 + C, 8, 128), F32), V((base + 2 + C, 8, 128), F32),
    ]
    scratch += scatter_scratch(g)
    m = weight_scatter_scratch(g, 3, f)
    scratch += [m[0], m[2], m[3]] + weight_scatter_scratch(g, 4, c)
    nt = 4 * 6 + 4 * 6 + 2 if g.square else 9 * (g.n_t - 1)
    nz = 11 * (2 * C + 1) + 2 * C
    sem = pltpu.SemaphoreType.DMA
    scratch += [sem((nt,)), sem((nt,)), sem((nz,)), sem((nz,)), sem((1,))]
    whole = pl.BlockSpec(memory_space=pltpu.VMEM)
    specs = [whole] * len(args)
    specs[1] = pl.BlockSpec(memory_space=pl.ANY)
    return pl.pallas_call(
        functools.partial(layer_body, g, n_pic),
        name="layer",
        out_shape=outs,
        in_specs=specs,
        out_specs=[whole] * len(outs),
        scratch_shapes=scratch,
        compiler_params=pltpu.CompilerParams(collective_id=1, has_side_effects=True, vmem_limit_bytes=VMEM_BYTES),
    )(*args)


def finish_body(output, grad_inputs, dattn, dmlp, stats, o_out, o_loss, o_in, o_q, o_k, o_v, o_o, o_g, o_u, o_d):
    o_out[...] = output[...]
    o_in[...] = grad_inputs[...]
    o_q[...] = dattn[0]
    o_k[...] = dattn[1]
    o_v[...] = dattn[2]
    o_o[...] = dattn[3].T
    o_g[...] = dmlp[0].T
    o_u[...] = dmlp[1].T
    o_d[...] = dmlp[2].T
    o_loss[0, 0] = stats[0, 0, 0]


def finish(g, parts):
    R, D, c, f, Dn = g.R, g.D, g.c, g.f, g.Dn
    sds = jax.ShapeDtypeStruct
    shapes = [(R, D), (1, 1), (R, D), (Dn, c), (Dn, c), (Dn, c), (c, Dn), (f, Dn), (f, Dn), (f, Dn)]
    whole = pl.BlockSpec(memory_space=pltpu.VMEM)
    specs = [whole] * len(shapes)
    specs[1] = pl.BlockSpec(memory_space=pltpu.SMEM)
    return pl.pallas_call(
        finish_body,
        name="finish",
        out_shape=[sds(s, F32) for s in shapes],
        in_specs=[whole] * len(parts),
        out_specs=specs,
        compiler_params=pltpu.CompilerParams(vmem_limit_bytes=VMEM_BYTES),
    )(*parts)


def per_device(n_dp, n_t, inputs, teacher, valid_mask, documents, picture_starts,
               w_query, w_key, w_value, w_out, w_gate, w_up, w_down):
    R, D = inputs.shape
    c, f = w_query.shape[1], w_gate.shape[1]
    g = Geo(n_dp, n_t, R, D, c, f)
    args = (inputs, teacher, valid_mask, documents, picture_starts, w_query, w_key, w_value, w_out, w_gate.T, w_up.T, w_down)
    parts = layer(g, picture_starts.shape[1], (*args, *rotary(g.S, c)))
    out, loss, *grads, gate, up, down = finish(g, parts)
    return (out, loss.reshape(()), *grads, gate.T, up.T, down)


def solution(mesh):
    rows, pair = P(("dp", "tensor"), None), P("dp", None)
    cut, across = P("dp", "tensor"), P("tensor", "dp")
    return jax.shard_map(
        functools.partial(per_device, mesh.shape["dp"], mesh.shape["tensor"]),
        mesh=mesh,
        in_specs=(rows, rows, pair, pair, pair, cut, cut, cut, across, cut, cut, across),
        out_specs=(rows, P(), rows, cut, cut, cut, across, cut, cut, across),
        check_vma=False,
    )
```

```python
import functools

import jax
import jax.numpy as jnp
import numpy as np
from jax import lax
from jax.experimental import pallas as pl
from jax.experimental.pallas import tpu as pltpu
from jax.sharding import PartitionSpec as P

MESH = pl.DeviceIdType.MESH
HD = 64
PIECE = 256
EPS = 1e-5
MASKED = -1e30
VMEM_BYTES = 60 * 2**20
BF = jnp.bfloat16
F32 = jnp.float32
NT = (((1,), (1,)), ((), ()))
NN = (((1,), (0,)), ((), ()))


def dot(a, b, dims=NN):
    return lax.dot_general(a, b, dims, preferred_element_type=F32)


def eye(n):
    return (
        lax.broadcasted_iota(jnp.int32, (n, n), 0) == lax.broadcasted_iota(jnp.int32, (n, n), 1)
    ).astype(F32).astype(BF)


def turned(a):
    n = a.shape[1]
    step = min(n, 256)
    parts = [dot(eye(step), a[:, k : k + step], NT).astype(BF) for k in range(0, n, step)]
    return parts[0] if len(parts) == 1 else jnp.concatenate(parts, axis=0)


def mean_of(v):
    return jnp.sum(v, axis=1, keepdims=True) * (1.0 / v.shape[1])


def normed(v):
    centred = v - mean_of(v)
    inv = lax.rsqrt(mean_of(centred * centred) + EPS)
    return centred * inv, inv


def normed_back(n, inv, g):
    return inv * (g - mean_of(g) - n * mean_of(g * n))


class Geo:
    def __init__(self, n_dp, n_t, tok_rows, d_model, cols, hid):
        self.n_dp, self.n_t, self.R, self.D, self.c, self.f = n_dp, n_t, tok_rows, d_model, cols, hid
        self.C = n_dp // 2
        self.S = tok_rows * n_t
        self.H = cols // HD
        self.Dn = d_model // n_dp
        self.square = n_t == 4
        self.line = self.C == 4

    def place(self):
        self.d = lax.axis_index("dp")
        self.t = lax.axis_index("tensor")
        self.chip = self.d // 2
        self.core = self.d % 2
        if self.square:
            self.tx = self.t + 1 - 2 * (self.t % 2)
            self.ty = (self.t + 2) % 4
            self.td = 3 - self.t
            self.to = [self.tx, self.ty]
            self.leave = [self.td, self.tx, self.ty, self.t]
        else:
            n = self.n_t
            self.to = [(self.t + k) % n for k in range(1, n)]
            self.leave = [(self.t + k) % n for k in range(1, n)] + [self.t]
        self.sib = self.d + 1 - 2 * self.core
        return self

    def zto(self, k):
        return ((self.chip + k) % self.C) * 2 + self.core

    def zfrom(self, k):
        return ((self.chip + self.C - k) % self.C) * 2 + self.core

    def rows(self, blk, first=0, count=None):
        count = self.R if count is None else count
        return pl.ds(pl.multiple_of(blk * self.R + first, count), count)

    def wrows(self, d):
        return pl.ds(pl.multiple_of(d * self.Dn, self.Dn), self.Dn)

    def greet(self):
        bar = pltpu.get_barrier_semaphore()
        out = [(self.d, p) for p in self.to]
        out += [(self.zto(k), self.t) for k in range(1, self.C)] + [(self.sib, self.t)]
        for dev in out:
            pl.semaphore_signal(bar, inc=1, device_id=dev, device_id_type=MESH)
        self.met = len(out)

    def meet(self):
        pl.semaphore_wait(pltpu.get_barrier_semaphore(), self.met)


class Comm:
    def __init__(self, send_sem, recv_sem):
        self.ss, self.rs = send_sem, recv_sem
        self.n = self.groups = 0

    def slots(self, k):
        self.n += k
        return list(range(self.n - k, self.n))

    def group(self):
        self.groups += 1
        return self.groups - 1

    def _copy(self, group, slot, src, dst, dev):
        return pltpu.make_async_remote_copy(
            src_ref=src, dst_ref=dst, send_sem=self.ss.at[group], recv_sem=self.rs.at[slot], device_id=dev, device_id_type=MESH
        )

    def send(self, group, slot, src, dst, dev, when=None):
        copy = self._copy(group, slot, src, dst, dev)
        if when is None:
            copy.start()
        else:
            pl.when(when)(copy.start)

    def recv(self, slot, dst, dev, when=None):
        copy = self._copy(0, slot, dst, dst, dev)
        if when is None:
            copy.wait_recv()
        else:
            pl.when(when)(copy.wait_recv)

    def sent(self, group, like, dev, when=None):
        copy = self._copy(group, 0, like, like, dev)
        if when is None:
            copy.wait_send()
        else:
            pl.when(when)(copy.wait_send)


class Gather:
    def __init__(self, geo, comm, slots, group, buf, far_first=False):
        self.g, self.comm, self.buf, self.group = geo, comm, buf, group
        g = geo
        self.far_first = far_first and g.square
        if not g.square:
            self.s = slots
            self.order = [(g.t + g.n_t - k) % g.n_t for k in range(g.n_t)]
            self.lead = [g.n_t - 1] + [g.n_t - 1 - k for k in range(1, g.n_t)]
            return
        self.sx, self.sy = slots[:5], slots[5:]
        if self.far_first:
            self.order, self.lead = [g.t, g.td, g.tx, g.ty], [3, 0, 1, 2]
        else:
            self.order, self.lead = [g.t, g.tx, g.ty, g.td], [3, 1, 2, 0]

    def begin(self, i):
        g, comm = self.g, self.comm
        if g.square:
            self._give(self.sx[i], g.t, i, 1, g.tx)
            self._give(self.sy[i], g.t, 2 + i, 1, g.ty)
            if i == 1 and not self.far_first:
                self._rest()
        elif i == 1:
            own = self.buf.at[g.rows(g.t)]
            for k, peer in enumerate(g.to):
                comm.send(self.group, self.s[k], own, own, (g.d, peer))

    def sent(self):
        self.comm.sent(self.group, self.buf.at[0 : (self.g.n_t - 1) * self.g.R], (self.g.d, self.g.to[0]))

    def piece(self, blk, first, count):
        q = self.g.R // 4
        rows = pl.ds(pl.multiple_of(blk * self.g.R + first * q, q), count * q)
        return self.buf.at[rows]

    def _give(self, slot, blk, first, count, to):
        part = self.piece(blk, first, count)
        self.comm.send(self.group, slot, part, part, (self.g.d, to))

    def _rest(self):
        g = self.g
        self._give(self.sx[4], g.t, 2, 2, g.tx)
        self._give(self.sy[4], g.t, 0, 2, g.ty)

    def relay(self):
        g, comm = self.g, self.comm
        if not g.square:
            return
        for i in range(2):
            comm.recv(self.sx[i], self.piece(g.tx, i, 1), (g.d, g.tx))
            self._give(self.sy[2 + i], g.tx, i, 1, g.ty)
            comm.recv(self.sy[i], self.piece(g.ty, 2 + i, 1), (g.d, g.ty))
            self._give(self.sx[2 + i], g.ty, 2 + i, 1, g.tx)
        if self.far_first:
            self._rest()

    def wait(self, i):
        g, comm = self.g, self.comm
        if i == 0:
            return
        if not g.square:
            comm.recv(self.s[i - 1], self.buf.at[g.rows(self.order[i])], (g.d, self.order[i]))
            return
        which = "dxy"[i - 1] if self.far_first else "xyd"[i - 1]
        if which == "x":
            comm.recv(self.sx[4], self.piece(g.tx, 2, 2), (g.d, g.tx))
        elif which == "y":
            comm.recv(self.sy[4], self.piece(g.ty, 0, 2), (g.d, g.ty))
        else:
            for k in range(2):
                comm.recv(self.sx[2 + k], self.piece(g.td, 2 + k, 1), (g.d, g.tx))
                comm.recv(self.sy[2 + k], self.piece(g.td, k, 1), (g.d, g.ty))


def scatter_scratch(g):
    h = g.R // 2
    if g.square:
        return [pltpu.VMEM((3, 2, h, g.D), BF), pltpu.VMEM((2, h, g.D), BF), pltpu.VMEM((2, h, g.D), BF), pltpu.VMEM((2, 2, h, g.D), BF)]
    return [pltpu.VMEM((g.n_t - 1, 2, h, g.D), BF), pltpu.VMEM((1, 16, 128), BF), pltpu.VMEM((1, 16, 128), BF), pltpu.VMEM((g.n_t - 1, 2, h, g.D), BF)]


class Scatter:
    def __init__(self, geo, comm, slots, group, bufs):
        self.g, self.comm, self.group = geo, comm, group
        self.part, self.into, self.out, self.fin = bufs
        g = geo
        if g.square:
            self.sx, self.sy = slots[:4], slots[4:]
        else:
            self.s = slots

    def give(self, i, value):
        g, comm = self.g, self.comm
        h = g.R // 2
        for j in range(2):
            self.part[i, j] = value[j * h : (j + 1) * h].astype(BF)
        if not g.square:
            comm.send(self.group, self.s[i], self.part.at[i], self.fin.at[i], (g.d, g.leave[i]))
        elif i == 0:
            comm.send(self.group, self.sx[0], self.part.at[0, 0], self.into.at[0], (g.d, g.tx))
            comm.send(self.group, self.sy[0], self.part.at[0, 1], self.into.at[1], (g.d, g.ty))
        elif i == 1:
            comm.send(self.group, self.sx[1], self.part.at[1, 0], self.fin.at[0, 0], (g.d, g.tx))
        else:
            comm.send(self.group, self.sy[1], self.part.at[2, 1], self.fin.at[1, 1], (g.d, g.ty))

    def relay(self):
        g, comm = self.g, self.comm
        if not g.square:
            return
        q = g.R // 4
        comm.recv(self.sx[0], self.into.at[0], (g.d, g.tx))
        comm.recv(self.sy[0], self.into.at[1], (g.d, g.ty))
        for k in range(2):
            rows = slice(k * q, (k + 1) * q)
            for a, mine, slots, to in ((0, (2, 0), self.sy, g.ty), (1, (1, 1), self.sx, g.tx)):
                self.out[a, rows] = (self.into[a, rows].astype(F32) + self.part[(*mine, rows)].astype(F32)).astype(BF)
                comm.send(self.group, slots[2 + k], self.out.at[a, rows], self.fin.at[1 - a, a, rows], (g.d, to))

    def take(self, i, own):
        g, comm = self.g, self.comm
        q = g.R // 4
        count = 2 if g.square else g.n_t - 1
        inner = slice(i * q, (i + 1) * q)
        if g.square:
            if i == 0:
                comm.recv(self.sx[1], self.fin.at[0, 0], (g.d, g.tx))
                comm.recv(self.sy[1], self.fin.at[1, 1], (g.d, g.ty))
            comm.recv(self.sx[2 + i], self.fin.at[0, 1, inner], (g.d, g.tx))
            comm.recv(self.sy[2 + i], self.fin.at[1, 0, inner], (g.d, g.ty))
        elif i == 0:
            for k in range(count):
                comm.recv(self.s[k], self.fin.at[k], (g.d, (g.t + g.n_t - k - 1) % g.n_t))
        pairs = []
        for j in range(2):
            rows = slice(2 * j * q + i * q, 2 * j * q + (i + 1) * q)
            v = own[rows]
            for k in range(count):
                v = v + self.fin[k, j, inner].astype(F32)
            pairs.append((rows, v))
        if i == 1:
            comm.sent(self.group, self.part, (g.d, g.to[0]))
        return pairs


class WeightGather:
    def __init__(self, geo, comm, buf, first, n):
        self.g, self.comm, self.buf, self.of = geo, comm, buf, pl.ds(first, n)
        g = geo
        self.group = comm.group()
        self.inner = (g.chip == 1) | (g.chip == 2)
        self.sz, self.sc = comm.slots(g.C - 1), comm.slots(g.C)

    def at(self, d):
        return self.buf.at[self.of, self.g.wrows(d)]

    def far(self):
        g, comm = self.g, self.comm
        if g.line:
            comm.send(self.group, self.sz[1], self.at(g.d), self.at(g.d), (g.zto(2), g.t))

    def near(self):
        g, comm = self.g, self.comm
        own = self.at(g.d)
        for k in range(1, g.C):
            if g.line and k == 2:
                continue
            near = g.chip != (0 if k == 3 else 3) if g.line else None
            comm.send(self.group, self.sz[k - 1], own, own, (g.zto(k), g.t), when=near)
        comm.send(self.group, self.sc[0], own, own, (g.sib, g.t))

    def _take(self, k, when=None):
        g, comm = self.g, self.comm
        block = self.at(g.zfrom(k))
        comm.recv(self.sz[k - 1], block, (g.zfrom(k), g.t), when=when)
        comm.send(self.group, self.sc[k], block, block, (g.sib, g.t), when=when)

    def relay(self):
        g, comm = self.g, self.comm
        if not g.line:
            return
        self._take(2, self.inner)
        block = self.at(g.zfrom(2))
        comm.send(self.group, self.sz[2], block, block, (6 + g.core, g.t), when=g.chip == 2)
        comm.send(self.group, self.sz[0], block, block, (g.core, g.t), when=g.chip == 1)

    def pass_on(self):
        g = self.g
        for k in range(1, g.C):
            self._take(k, jnp.logical_not(self.inner) if g.line and k == 2 else None)

    def wait(self):
        g, comm = self.g, self.comm
        for k in range(g.C):
            other = g.zfrom(k) + 1 - 2 * g.core
            comm.recv(self.sc[k], self.at(other), (g.sib, g.t))

    def sent(self):
        g, comm = self.g, self.comm

        def some(n, when=None):
            comm.sent(self.group, self.buf.at[self.of, 0 : n * g.Dn], (g.sib, g.t), when)

        if g.line:
            some(8, self.inner)
            some(6, jnp.logical_not(self.inner))
        else:
            some(2 * g.C - 1)


class WeightScatter:
    def __init__(self, geo, comm, src, bufs):
        self.g, self.comm, self.src = geo, comm, src
        self.sib_in, self.out, self.fin = bufs
        g = geo
        self.group = comm.group()
        self.sc, self.sz = comm.slots(1)[0], comm.slots(5 if g.line else g.C - 1)
        half = g.chip // 2
        self.near, self.inner, self.other, self.opposite = 3 * half, 1 + half, 2 - half, 3 - 3 * half
        self.end = (g.chip == 0) | (g.chip == 3)
        for j in range(g.C):
            block = self.src.at[g.wrows(2 * j + 1 - g.core)]
            comm.send(self.group, self.sc, block, self.sib_in.at[j], (g.sib, g.t))

    def _sum(self, chip):
        return self.src[self.g.wrows(2 * chip + self.g.core)].astype(F32) + self.sib_in[chip].astype(F32)

    def meet(self):
        g, comm = self.g, self.comm
        comm.recv(self.sc, self.sib_in, (g.sib, g.t))

    def part(self, b):
        g, comm = self.g, self.comm
        if not g.line:
            for k in range(1, g.C) if b == 0 else ():
                self.out[k - 1][...] = self._sum((g.chip + k) % g.C).astype(BF)
                comm.send(self.group, self.sz[k - 1], self.out[k - 1], self.fin.at[k - 1], (g.zto(k), g.t))
            return

        @pl.when(self.end)
        def _():
            self.out[b][...] = self._sum((self.opposite, self.other, self.inner)[b]).astype(BF)

        to = (self.inner * 2 + g.core, g.t)
        comm.send(self.group, self.sz[b], self.out[b], self.fin.at[b], to, when=self.end)

    def pass_on(self):
        self.meet()
        for b in range(3):
            self.part(b)

    def relay(self, b):
        g, comm = self.g, self.comm
        if not g.line:
            return
        middle = jnp.logical_not(self.end)
        came = (0, 1, 3)[b]

        @pl.when(middle)
        def _():
            comm.recv(self.sz[came], self.fin.at[came], (g.sib, g.t))
            mine = self._sum((self.opposite, self.other, self.near)[b])
            self.out[b][...] = (mine + self.fin[came].astype(F32)).astype(BF)

        goes = (3, 4, 0)[b]
        to = ((self.other, self.other, self.near)[b] * 2 + g.core, g.t)
        comm.send(self.group, self.sz[goes], self.out[b], self.fin.at[goes], to, when=middle)

    def sent(self):
        g = self.g
        self.comm.sent(self.group, self.src.at[0 : (2 * g.C - 1) * g.Dn], (g.sib, g.t))

    def total(self):
        g, comm = self.g, self.comm
        mine = self.src[g.wrows(g.d)].astype(F32) + self.sib_in[g.chip].astype(F32)
        if not g.line:
            for k in range(1, g.C):
                comm.recv(self.sz[k - 1], self.fin.at[k - 1], (g.zfrom(k), g.t))
                mine = mine + self.fin[k - 1].astype(F32)
            return mine
        middle = jnp.logical_not(self.end)
        comm.recv(self.sz[0], self.fin.at[0], (g.sib, g.t), when=self.end)
        comm.recv(self.sz[2], self.fin.at[2], (g.sib, g.t), when=middle)
        comm.recv(self.sz[4], self.fin.at[4], (g.sib, g.t), when=middle)
        at_end = self.fin[0].astype(F32)
        between = self.fin[2].astype(F32) + self.fin[4].astype(F32)
        return mine + jnp.where(self.end, at_end, between)


def weight_scatter_scratch(g, n, w):
    steps = 5 if g.line else g.C - 1
    return [pltpu.VMEM((n, g.C, g.Dn, w), BF), pltpu.VMEM((n, g.C - 1, g.Dn, w), BF), pltpu.VMEM((n, steps, g.Dn, w), BF)]


def rotated(v, cosine, sine):
    n = v.shape[1]
    if n > cosine.shape[1]:
        cosine = jnp.concatenate([cosine] * (n // cosine.shape[1]), axis=1)
        sine = jnp.concatenate([sine] * (n // sine.shape[1]), axis=1)
    lower = lax.broadcasted_iota(jnp.int32, v.shape, 1) % HD < HD // 2
    swapped = jnp.where(lower, pltpu.roll(v, n - HD // 2, 1), pltpu.roll(v, HD // 2, 1))
    return v * cosine + swapped * sine


def head_lanes(v, h):
    lane = lax.broadcasted_iota(jnp.int32, v.shape, 1)
    keep = (lane >= h * HD) & (lane < (h + 1) * HD)
    return jnp.where(keep, v, jnp.zeros_like(v))


def attend(g, hi, q_blk, keys_rot, values_t, bias, probs, inverse):
    H, R = g.H, g.R
    step = min(512, hi)
    spans = [slice(k, k + step) for k in range(0, hi, step)]
    scores, top, sums, mix = {}, [None] * H, [None] * H, [None] * H

    def fold(v, op):
        return op(v.reshape(v.shape[0] // 8, 8, v.shape[1]), axis=0)

    def first(h, span):
        s = dot(keys_rot[span], head_lanes(q_blk, h), NT) + bias[span]
        scores[h, span.start] = s
        most = fold(s, jnp.max)
        top[h] = most if top[h] is None else jnp.maximum(top[h], most)

    def second(h, span):
        if span.start == 0:
            top[h] = jnp.max(top[h], axis=0, keepdims=True)
        e = jnp.exp(scores.pop((h, span.start)) - top[h])
        some = fold(e, jnp.sum)
        sums[h] = some if sums[h] is None else sums[h] + some
        low = e.astype(BF)
        probs[span, h * R : (h + 1) * R] = low
        out = dot(values_t[h * HD : (h + 1) * HD, span], low)
        mix[h] = out if mix[h] is None else mix[h] + out

    for h in range(H + 1):
        for span in spans:
            if h < H:
                first(h, span)
            if h > 0:
                second(h - 1, span)
    for h in range(H):
        inv = 1.0 / jnp.sum(sums[h], axis=0, keepdims=True)
        inverse[h : h + 1, :] = inv
        mix[h] = mix[h] * inv
    return jnp.concatenate(mix, axis=0)


def attend_back(g, hi, values, keys_t, probs, go, qm, dots, dk, dv):
    H, R = g.H, g.R
    step = 256 if hi < g.S else hi
    grads = [None] * H
    for k in range(0, hi + step, step):
        now, past = slice(k, k + step), slice(k - step, k)
        if k < hi:
            if step < hi:
                dv[now] += dot(probs[now], go[...])
            ahead = [dot(values[now], go[0:R], NT)]
            for h in range(H):
                cols = slice(h * R, (h + 1) * R)
                if h + 1 < H:
                    ahead.append(dot(values[now], go[(h + 1) * R : (h + 2) * R], NT))
                low = (probs[now, cols].astype(F32) * (ahead[h] - dots[h])).astype(BF)
                if h == 0 and step == hi:
                    dv[now] += dot(probs[now], go[...])
                probs[now, cols] = low
                out = dot(keys_t[h * HD : (h + 1) * HD, now], low)
                grads[h] = out if grads[h] is None else grads[h] + out
        if k > 0:
            dk[past] += dot(probs[past], qm[...])
    return jnp.concatenate(grads, axis=0)


def bias_of(qinfo, kinfo, first, size, rows):
    shape = (size, rows)
    doc_q, pic_q = qinfo[0:1, :], qinfo[1:2, :]
    key_doc, pic_k = kinfo[:, 0:1], kinfo[:, 1:2]
    key_pos = lax.broadcasted_iota(jnp.int32, shape, 0)
    query_pos = lax.broadcasted_iota(jnp.int32, shape, 1) + first
    before = key_pos <= query_pos
    open_ = (doc_q == key_doc) & (before | (pic_q == pic_k))
    ok = open_ | (key_pos == query_pos)
    return jnp.where(ok, 0.0, MASKED).astype(F32)


def rotary(length, cols):
    half = HD // 2
    frequency = 10000.0 ** (-2.0 * np.arange(half) / HD)
    angle = np.arange(length)[:, None] * frequency[None, :]
    cosine = np.concatenate([np.cos(angle)] * 2, axis=1)
    sine = np.concatenate([-np.sin(angle), np.sin(angle)], axis=1)
    reps = max(1, min(cols, 128) // HD)
    return (jnp.asarray(np.tile(cosine, (1, reps)), F32), jnp.asarray(np.tile(sine, (1, reps)), F32))


def in_slot(g, n_pic, blk):
    per = g.n_t // n_pic

    def run(body):
        for p in range(n_pic):
            pl.when(blk // per == p)(functools.partial(body, p, blk - p * per, (p + 1) * (g.S // n_pic)))

    return run


def layer_body(g, n_pic, x, teacher, valid_mask, documents, starts, wq, wk, wv, wo, wg, wu, wd, cosine, sine,
               o_out, o_in, o_q, o_k, o_v, o_o, o_g, o_u, o_d, o_loss,
               rows1, rows2, gm, ga, wa, wm, qkv, mixed, mixt, turn, wo_t, probs0, probs1, acc2, qm, gom, mids, middle, cot,
               qinfo, kinfo, rinv, cnt, err,
               part, into, out, fin,
               sib_m, fin_m, sib_a, out_a, fin_a, output, grad_inputs, dattn, dout, dmlp, stats,
               ts, tr, zs, zr, local):
    g.place()
    g.greet()
    R, S, c, H, C, Dn = g.R, g.S, g.c, g.H, g.C, g.Dn
    tc, zc = Comm(ts, tr), Comm(zs, zr)
    sums = (part, into, out, fin)
    few, ag_group, rs_group = tc.group(), tc.group(), tc.group()
    ag_slots = tc.slots(10 if g.square else g.n_t - 1)
    rs_slots = tc.slots(8 if g.square else g.n_t - 1)
    te = tc.slots(2 if g.square else g.n_t - 1)
    gather = functools.partial(Gather, g, tc, ag_slots, ag_group)
    scatter = functools.partial(Scatter, g, tc, rs_slots, rs_group, sums)
    q, kk, v = qkv.at[0], qkv.at[1], qkv.at[2]
    probs = (probs0, probs1)
    bias, dk, dv = acc2.at[:, :, :R], acc2.at[0, :, :c], acc2.at[1, :, :c]
    stores = []

    def store(buf, to):
        copy = pltpu.make_async_copy(buf, to, local.at[1 + len(stores)])
        copy.start()
        stores.append(copy)

    get_teacher = pltpu.make_async_copy(teacher, cot, local.at[0])
    get_teacher.start()

    one, _ = normed(x[...])
    rows1[g.rows(g.t)] = one.astype(BF)
    block = g.wrows(g.d)
    wa[0, block] = wq[...]
    wa[1, block] = wk[...]
    wa[2, block] = wv[...]
    g.meet()
    ag = gather(rows1)
    ag.begin(0)
    ag.begin(1)
    za, zo = WeightGather(g, zc, wa, 0, 3), WeightGather(g, zc, wa, 3, 1)
    zg, zd = WeightGather(g, zc, wm, 0, 2), WeightGather(g, zc, wm, 2, 1)
    za.far()
    wa[3, block] = turned(wo[...])
    zo.far()
    za.near()
    wm[0, block] = turned(wg[...])
    wm[1, block] = turned(wu[...])
    wm[2, block] = turned(wd[...])

    csib, cz = zc.slots(1)[0], zc.slots(C - 1)
    gsib, gz = zc.group(), zc.group()
    valid, doc = valid_mask[...], documents[...]
    cnt[0] = jnp.broadcast_to(jnp.sum(valid.astype(F32), axis=1, keepdims=True), (8, 128))
    zc.send(gsib, csib, cnt.at[0], cnt.at[1], (g.sib, g.t))
    at = lax.broadcasted_iota(jnp.int32, (1, S), 1)
    pic = jnp.zeros((1, S), jnp.int32)
    for p in range(n_pic):
        first = starts[0:1, p : p + 1]
        pic = jnp.where((at >= first) & (at < first + PIECE), p + 1, pic)
    qinfo[0:1] = doc
    qinfo[1:2] = pic
    as_keys = [jnp.where(valid == 1, doc, -1), jnp.where(pic > 0, pic, -1), valid]
    as_keys = jnp.concatenate([a.astype(F32) for a in as_keys] + [jnp.zeros((125, S), F32)], axis=0)
    kinfo[...] = as_keys.T.astype(jnp.int32)
    zc.recv(csib, cnt.at[1], (g.sib, g.t))
    cnt[2] = cnt[0] + cnt[1]
    for k in range(1, C):
        zc.send(gz, cz[k - 1], cnt.at[2], cnt.at[2 + k], (g.zto(k), g.t))

    def set_bias(i, blk):
        @in_slot(g, n_pic, blk)
        def _(p, index, hi):
            bias[i % 2, 0:hi] = bias_of(qinfo[:, g.rows(blk)], kinfo[0:hi], blk * R, hi, R)

    set_bias(0, g.leave[0])

    ag.relay()
    za.relay()
    zo.relay()
    zo.near()
    za.pass_on()
    za.wait()
    zg.far()
    zg.near()
    for i, blk in enumerate(ag.order):
        ag.wait(i)
        at = g.rows(blk)
        row = rows1[at]
        cos_b, sin_b = cosine[at], sine[at]
        q[at] = (rotated(dot(row, wa[0]), cos_b, sin_b) * HD**-0.5).astype(BF)
        kk[at] = rotated(dot(row, wa[1]), cos_b, sin_b).astype(BF)
        v[at] = dot(row, wa[2]).astype(BF)
    zo.pass_on()
    turn[...] = turned(v[...])

    rs = scatter()
    for i, blk in enumerate(g.leave):
        at = g.rows(blk)

        if i:
            set_bias(i, blk)

        @in_slot(g, n_pic, blk)
        def _(p, index, hi, blk=blk, at=at, i=i):
            both = attend(g, hi, q[at], kk, turn, bias.at[i % 2], probs[p].at[index], rinv.at[blk])
            mixt[blk] = both.astype(BF)
            mixed[at] = both.T.astype(BF)

        if i == 0:
            zo.wait()
        if i == 2:
            zg.relay()
            zd.far()
            zd.near()
        partial = dot(mixed[at], wa[3], NT)
        if i < g.n_t - 1:
            rs.give(i, partial)
        else:
            middle[0:R] = x[...] + partial
    rs.relay()
    ag.sent()
    ag = gather(rows2, far_first=True)

    for i in range(2):
        for rows, summed in rs.take(i, middle):
            middle[rows] = summed
            two, _ = normed(summed)
            rows2[g.rows(g.t, rows.start, R // 4)] = two.astype(BF)
        ag.begin(i)
    rs = scatter()
    zg.pass_on()
    zd.relay()
    zg.wait()
    for i, blk in enumerate(ag.order):
        ag.wait(i)
        at = g.rows(blk)
        row = rows2[at]
        gate, up = dot(row, wm[0]), dot(row, wm[1])
        sig = jax.nn.sigmoid(gate)
        act = gate * sig
        mids[0, at] = (act * up).astype(BF)
        mids[2, at] = act.astype(BF)
        mids[1, at] = (up * sig * (1.0 + gate * (1.0 - sig))).astype(BF)
        if i == 0:
            ag.relay()
            continue
        if i == 1:
            zd.pass_on()
            zd.wait()
        rs.give(ag.lead[i], dot(mids[0, at], wm[2], NT))
    output[...] = middle[0:R] + dot(mids[0, g.rows(g.t)], wm[2], NT)
    wo_t[...] = turned(wa[3])
    rs.relay()

    get_teacher.wait()
    tokens = cnt[2]
    for k in range(1, C):
        zc.recv(cz[k - 1], cnt.at[2 + k], (g.zfrom(k), g.t))
        tokens = tokens + cnt[2 + k]
    share = 1.0 * S * g.n_dp / tokens[0:1, 0:1]
    ag.sent()
    ag = gather(gm, far_first=True)
    errors = jnp.zeros((R // 4, 1), F32)
    for i in range(2):
        for rows, summed in rs.take(i, output):
            output[rows] = summed
            dev = summed - cot[rows]
            kept = kinfo[g.rows(g.t, rows.start, R // 4), 2:3].astype(F32) * dev
            cotangent = kept * share
            cot[rows] = cotangent
            gm[g.rows(g.t, rows.start, R // 4)] = cotangent.astype(BF)
            errors += jnp.sum(kept * dev, axis=1, keepdims=True)
        ag.begin(i)
    store(output, o_out)
    err[0] = jnp.broadcast_to(jnp.sum(errors, axis=0, keepdims=True), (8, 128))

    rs = scatter()
    if g.square:
        tc.send(few, te[0], err.at[0], err.at[1], (g.d, g.tx))
    else:
        for k, peer in enumerate(g.to):
            tc.send(few, te[k], err.at[0], err.at[1 + k], (g.d, peer))
    for i, blk in enumerate(ag.order):
        ag.wait(i)
        at = g.rows(blk)
        gh = dot(gm[at], wm[2])
        mids[1, at] = (gh * mids[1, at].astype(F32)).astype(BF)
        mids[2, at] = (gh * mids[2, at].astype(F32)).astype(BF)
        if i == 0:
            ag.relay()
            rows2[...] = turned(rows2[...])
            turn[...] = turned(kk[...])
            continue
        rs.give(ag.lead[i], dot(mids[1, at], wm[0], NT) + dot(mids[2, at], wm[1], NT))
    at = g.rows(g.t)
    own = dot(mids[1, at], wm[0], NT) + dot(mids[2, at], wm[1], NT)
    grad_inputs[...] = own
    zg.sent()
    zd.sent()
    wm[0] = dot(rows2[...], mids[1]).astype(BF)

    zscat = []

    def start_mlp(j, used):
        spare = [mids.at[used, k * Dn : (k + 1) * Dn] for k in range(C - 1)]
        zscat.append(WeightScatter(g, zc, wm.at[j], (sib_m.at[j], spare, fin_m.at[j])))

    start_mlp(0, 1)
    rs.relay()
    zscat[0].pass_on()
    wm[1] = dot(rows2[...], mids[2]).astype(BF)
    start_mlp(1, 2)
    for k in range(0, g.D, 256):
        wm[2, k : k + 256] = dot(turned(gm[:, k : k + 256]), mids[0]).astype(BF)
    start_mlp(2, 0)
    zscat[1].pass_on()
    two, inv = normed(middle[0:R])
    ag.sent()
    ag = gather(ga)
    for i in range(2):
        for rows, back in rs.take(i, grad_inputs):
            grad_middle = cot[rows] + normed_back(two[rows], inv[rows], back)
            cot[rows] = grad_middle
            ga[g.rows(g.t, rows.start, R // 4)] = grad_middle.astype(BF)
        ag.begin(i)

    def start_attention(j):
        spare = [out_a.at[j, k] for k in range(C - 1)]
        zscat.append(WeightScatter(g, zc, wa.at[j], (sib_a.at[j], spare, fin_a.at[j])))

    rs = scatter()
    zscat[2].pass_on()
    zscat[0].relay(0)
    zscat[0].relay(1)
    base = 4 if g.square else g.n_t
    ec, ez = zc.slots(1)[0], zc.slots(C - 1)
    gec, gez = zc.group(), zc.group()
    if g.square:
        tc.recv(te[0], err.at[1], (g.d, g.tx))
        err[2] = err[0] + err[1]
        tc.send(few, te[1], err.at[2], err.at[3], (g.d, g.ty))
    acc2[...] = jnp.zeros_like(acc2)
    for i, blk in enumerate(ag.order):
        if i == 1:
            zscat[0].relay(2)
            rows1[...] = turned(rows1[...])
        ag.wait(i)
        at = g.rows(blk)
        d_out = dot(mixt[blk], ga[at])
        if i:
            d_out += middle[0:c]
        if i < g.n_t - 1:
            middle[0:c] = d_out
        else:
            zo.sent()
            wa[3] = turned(d_out.astype(BF))
            start_attention(3)
        go_t = dot(wo_t[...], ga[at], NT).astype(BF).astype(F32)
        mix_t = mixt[blk].astype(F32)
        scaled, dots = [], []
        for h in range(H):
            one_head = go_t[h * HD : (h + 1) * HD] * rinv[blk, h : h + 1, :]
            scaled.append(one_head)
            dots.append(jnp.sum(one_head * mix_t[h * HD : (h + 1) * HD], axis=0, keepdims=True))
        go = jnp.concatenate(scaled, axis=0).T.astype(BF)
        q_blk = q[at]
        for h in range(H):
            gom[h * R : (h + 1) * R] = head_lanes(go, h)
            qm[h * R : (h + 1) * R] = head_lanes(q_blk, h)

        @in_slot(g, n_pic, blk)
        def _(p, index, hi, blk=blk, at=at, dots=dots):
            dq = attend_back(g, hi, v, turn, probs[p].at[index], gom, qm, dots, dk, dv).T * HD**-0.5
            q[at] = rotated(dq, cosine[at], -sine[at]).astype(BF)

        if i == 0:
            ag.relay()
        if i == 1:
            if g.square:
                tc.recv(te[1], err.at[3], (g.d, g.ty))
                err[base] = err[2] + err[3]
            else:
                total = err[0]
                for k in range(1, g.n_t):
                    tc.recv(te[k - 1], err.at[k], (g.d, (g.t + g.n_t - k) % g.n_t))
                    total = total + err[k]
                err[base] = total
            zc.send(gec, ec, err.at[base], err.at[base + 1], (g.sib, g.t))
        if i == 2:
            zc.recv(ec, err.at[base + 1], (g.sib, g.t))
            err[base + 2] = err[base] + err[base + 1]
            for k in range(1, C):
                zc.send(gez, ez[k - 1], err.at[base + 2], err.at[base + 2 + k], (g.zto(k), g.t))
            zscat[1].relay(0)
            zscat[1].relay(1)
    for i, blk in enumerate(g.leave):
        at = g.rows(blk)
        kk[at] = rotated(dk[at], cosine[at], -sine[at]).astype(BF)
        v[at] = dv[at].astype(BF)
        partial = dot(q[at], wa[0], NT) + dot(kk[at], wa[1], NT) + dot(v[at], wa[2], NT)
        if i < g.n_t - 1:
            rs.give(i, partial)
        else:
            grad_inputs[...] = partial

    zscat[3].pass_on()
    zscat[1].relay(2)
    zscat[2].relay(0)
    zscat[2].relay(1)
    za.sent()
    for j in range(3):
        wa[j] = dot(rows1[...], qkv[j]).astype(BF)
        start_attention(j)
    for j in (4, 5, 6):
        zscat[j].meet()
        zscat[j].part(0)
    rs.relay()
    for k in (1, 2):
        for j in (4, 5, 6):
            zscat[j].part(k)
    zscat[2].relay(2)
    zscat[3].relay(0)
    zscat[3].relay(1)
    one, inv = normed(x[...])

    for j, to in enumerate((o_g, o_u, o_d)):
        dmlp[j] = zscat[j].total().T
        store(dmlp.at[j], to)
    for j in (4, 5, 6):
        zscat[j].relay(0)
    zscat[3].relay(2)
    for i in range(2):
        for rows, back in rs.take(i, grad_inputs):
            grad_inputs[rows] = cot[rows] + normed_back(one[rows], inv[rows], back)
    store(grad_inputs, o_in)
    for k in (1, 2):
        for j in (4, 5, 6):
            zscat[j].relay(k)
    dout[...] = zscat[3].total().T
    store(dout, o_o)
    total = err[base + 2]
    for k in range(1, C):
        zc.recv(ez[k - 1], err.at[base + 2 + k], (g.zfrom(k), g.t))
        total = total + err[base + 2 + k]
    stats[0] = total * (1.0 / g.D) / tokens
    store(stats.at[0], o_loss)
    for j, to in enumerate((o_q, o_k, o_v)):
        dattn[j] = zscat[4 + j].total()
        store(dattn.at[j], to)
    for copy in stores:
        copy.wait()
    ag.sent()
    for scat in zscat:
        scat.sent()
    tc.sent(few, err.at[0 : len(te)], (g.sib, g.t))
    for group, n in ((gsib, 1), (gz, C - 1), (gec, 1), (gez, C - 1)):
        zc.sent(group, cnt.at[0:n], (g.sib, g.t))
    assert tc.n <= tr.shape[0] and zc.n <= zr.shape[0] and tc.groups <= ts.shape[0] and zc.groups <= zs.shape[0]


def layer(g, n_pic, args):
    S, R, D, c, f, H, C, Dn = g.S, g.R, g.D, g.c, g.f, g.H, g.C, g.Dn
    sds, V = jax.ShapeDtypeStruct, pltpu.VMEM
    shapes = [(R, D), (R, D), (Dn, c), (Dn, c), (Dn, c), (c, Dn), (f, Dn), (f, Dn), (f, Dn), (8, 128)]
    outs = [sds(s, F32) for s in shapes]
    base = 4 if g.square else g.n_t
    scratch = [V((S, D), BF)] * 4 + [
        V((4, D, c), BF), V((3, D, f), BF), V((3, S, c), BF), V((S, c), BF), V((g.n_t, c, R), BF), V((c, S), BF), V((c, D), BF),
        V((g.n_t // 2, S // 2, H * R), BF), V((g.n_t // 2, S, H * R), BF), V((2, S, max(R, c)), F32), V((H * R, c), BF), V((H * R, c), BF), V((3, S, f), BF),
        V((max(R, c), D), F32), V((R, D), F32), V((8, S), jnp.int32), V((S, 128), jnp.int32), V((g.n_t, 8, R), F32),
        V((2 + C, 8, 128), F32), V((base + 2 + C, 8, 128), F32),
    ]
    scratch += scatter_scratch(g)
    m = weight_scatter_scratch(g, 3, f)
    scratch += [m[0], m[2]] + weight_scatter_scratch(g, 4, c)
    scratch += [V((R, D), F32), V((R, D), F32), V((3, Dn, c), F32), V((c, Dn), F32), V((3, f, Dn), F32), V((1, 8, 128), F32)]
    nt = 20 if g.square else 3 * (g.n_t - 1)
    nz = 4 * (2 * C - 1) + 7 * (6 if g.line else C) + 2 * C
    sem = pltpu.SemaphoreType.DMA
    scratch += [sem((3,)), sem((nt,)), sem((15,)), sem((nz,)), sem((11,))]
    whole = pl.BlockSpec(memory_space=pltpu.VMEM)
    specs = [whole] * len(args)
    specs[1] = pl.BlockSpec(memory_space=pl.ANY)
    return pl.pallas_call(
        functools.partial(layer_body, g, n_pic),
        name="layer",
        out_shape=outs,
        in_specs=specs,
        out_specs=[pl.BlockSpec(memory_space=pl.ANY)] * len(outs),
        scratch_shapes=scratch,
        compiler_params=pltpu.CompilerParams(collective_id=1, has_side_effects=True, vmem_limit_bytes=VMEM_BYTES),
    )(*args)


def finish_body(n, *refs):
    stats, parts, outs, loss = refs[0], refs[1 : n + 1], refs[n + 1 : 2 * n + 1], refs[2 * n + 1]
    bufs, come, go = refs[2 * n + 2 : 3 * n + 2], refs[3 * n + 2], refs[3 * n + 3]
    loads = [pltpu.make_async_copy(a, b, come.at[k]) for k, (a, b) in enumerate(zip(parts, bufs))]
    stores = [pltpu.make_async_copy(a, b, go.at[k]) for k, (a, b) in enumerate(zip(bufs, outs))]
    for copy in loads:
        copy.start()
    loss[0, 0] = stats[0, 0]
    for load, store in zip(loads, stores):
        load.wait()
        store.start()
    for copy in stores:
        copy.wait()


def finish(parts, stats):
    sds = jax.ShapeDtypeStruct
    anywhere, n = pl.BlockSpec(memory_space=pl.ANY), len(parts)
    return pl.pallas_call(
        functools.partial(finish_body, n),
        name="finish",
        out_shape=[sds(p.shape, F32) for p in parts] + [sds((1, 1), F32)],
        in_specs=[pl.BlockSpec(memory_space=pltpu.VMEM)] + [anywhere] * n,
        out_specs=[anywhere] * n + [pl.BlockSpec(memory_space=pltpu.SMEM)],
        scratch_shapes=[pltpu.VMEM(p.shape, F32) for p in parts] + [pltpu.SemaphoreType.DMA((n,))] * 2,
    )(stats, *parts)


def per_device(n_dp, n_t, inputs, teacher, valid_mask, documents, picture_starts,
               w_query, w_key, w_value, w_out, w_gate, w_up, w_down):
    R, D = inputs.shape
    c, f = w_query.shape[1], w_gate.shape[1]
    g = Geo(n_dp, n_t, R, D, c, f)
    args = (inputs, teacher, valid_mask, documents, picture_starts, w_query, w_key, w_value, w_out, w_gate.T, w_up.T, w_down)
    *parts, stats = layer(g, picture_starts.shape[1], (*args, *rotary(g.S, c)))
    out, *grads, gate, up, down, loss = finish(parts, stats)
    return (out, loss.reshape(()), *grads, gate.T, up.T, down)


def solution(mesh):
    rows, pair = P(("dp", "tensor"), None), P("dp", None)
    cut, across = P("dp", "tensor"), P("tensor", "dp")
    return jax.shard_map(
        functools.partial(per_device, mesh.shape["dp"], mesh.shape["tensor"]),
        mesh=mesh,
        in_specs=(rows, rows, pair, pair, pair, cut, cut, cut, across, cut, cut, across),
        out_specs=(rows, P(), rows, cut, cut, cut, across, cut, cut, across),
        check_vma=False,
    )
```

```python
import functools

import jax
import jax.numpy as jnp
import numpy as np
from jax import lax
from jax.experimental import pallas as pl
from jax.experimental.pallas import tpu as pltpu
from jax.sharding import PartitionSpec as P

MESH = pl.DeviceIdType.MESH
HD = 64
PIECE = 256
EPS = 1e-5
MASKED = -1e30
VMEM_BYTES = 60 * 2**20
BF = jnp.bfloat16
F32 = jnp.float32
NT = (((1,), (1,)), ((), ()))
NN = (((1,), (0,)), ((), ()))


def dot(a, b, dims=NN):
    return lax.dot_general(a, b, dims, preferred_element_type=F32)


def eye(n):
    return (
        lax.broadcasted_iota(jnp.int32, (n, n), 0) == lax.broadcasted_iota(jnp.int32, (n, n), 1)
    ).astype(F32).astype(BF)


def turned(a):
    n = a.shape[1]
    step = min(n, 256)
    parts = [dot(eye(step), a[:, k : k + step], NT).astype(BF) for k in range(0, n, step)]
    return parts[0] if len(parts) == 1 else jnp.concatenate(parts, axis=0)


def mean_of(v):
    return jnp.sum(v, axis=1, keepdims=True) * (1.0 / v.shape[1])


def normed(v):
    centred = v - mean_of(v)
    inv = lax.rsqrt(mean_of(centred * centred) + EPS)
    return centred * inv, inv


def normed_back(n, inv, g):
    return inv * (g - mean_of(g) - n * mean_of(g * n))


class Geo:
    def __init__(self, n_dp, n_t, tok_rows, d_model, cols, hid):
        self.n_dp, self.n_t, self.R, self.D, self.c, self.f = n_dp, n_t, tok_rows, d_model, cols, hid
        self.C = n_dp // 2
        self.S = tok_rows * n_t
        self.H = cols // HD
        self.Dn = d_model // n_dp
        self.square = n_t == 4
        self.line = self.C == 4

    def place(self):
        self.d = lax.axis_index("dp")
        self.t = lax.axis_index("tensor")
        self.chip = self.d // 2
        self.core = self.d % 2
        if self.square:
            self.tx = self.t + 1 - 2 * (self.t % 2)
            self.ty = (self.t + 2) % 4
            self.td = 3 - self.t
            self.to = [self.tx, self.ty]
            self.leave = [self.td, self.tx, self.ty, self.t]
        else:
            n = self.n_t
            self.to = [(self.t + k) % n for k in range(1, n)]
            self.leave = [(self.t + k) % n for k in range(1, n)] + [self.t]
        self.sib = self.d + 1 - 2 * self.core
        return self

    def leave_at(self, i):
        if self.square:
            return 2 * ((self.t // 2 + i + 1) % 2) + (self.t % 2 + 1 - i // 2) % 2
        return (self.t + 1 + i) % self.n_t

    def arrive_at(self, i):
        if self.square:
            return 2 * ((self.t // 2 + i // 2) % 2) + (self.t % 2 + i % 2) % 2
        return (self.t + self.n_t - i) % self.n_t

    def far_at(self, i):
        if self.square:
            return 2 * ((self.t // 2 + i % 2) % 2) + (self.t % 2 + (i + 1) // 2) % 2
        return (self.t + self.n_t - i) % self.n_t

    def far_lead(self, i):
        return i - 1 if self.square else self.n_t - 1 - i

    def zto(self, k):
        return ((self.chip + k) % self.C) * 2 + self.core

    def zfrom(self, k):
        return ((self.chip + self.C - k) % self.C) * 2 + self.core

    def rows(self, blk, first=0, count=None):
        count = self.R if count is None else count
        return pl.ds(pl.multiple_of(blk * self.R + first, count), count)

    def wrows(self, d):
        return pl.ds(pl.multiple_of(d * self.Dn, self.Dn), self.Dn)

    def greet(self):
        bar = pltpu.get_barrier_semaphore()
        out = [(self.d, p) for p in self.to]
        out += [(self.zto(k), self.t) for k in range(1, self.C)] + [(self.sib, self.t)]
        for dev in out:
            pl.semaphore_signal(bar, inc=1, device_id=dev, device_id_type=MESH)
        self.met = len(out)

    def meet(self):
        pl.semaphore_wait(pltpu.get_barrier_semaphore(), self.met)


class Comm:
    def __init__(self, send_sem, recv_sem):
        self.ss, self.rs = send_sem, recv_sem
        self.n = self.groups = 0

    def slots(self, k):
        self.n += k
        return list(range(self.n - k, self.n))

    def group(self):
        self.groups += 1
        return self.groups - 1

    def _copy(self, group, slot, src, dst, dev):
        return pltpu.make_async_remote_copy(
            src_ref=src, dst_ref=dst, send_sem=self.ss.at[group], recv_sem=self.rs.at[slot], device_id=dev, device_id_type=MESH
        )

    def send(self, group, slot, src, dst, dev, when=None):
        copy = self._copy(group, slot, src, dst, dev)
        if when is None:
            copy.start()
        else:
            pl.when(when)(copy.start)

    def recv(self, slot, dst, dev, when=None):
        copy = self._copy(0, slot, dst, dst, dev)
        if when is None:
            copy.wait_recv()
        else:
            pl.when(when)(copy.wait_recv)

    def sent(self, group, like, dev, when=None):
        copy = self._copy(group, 0, like, like, dev)
        if when is None:
            copy.wait_send()
        else:
            pl.when(when)(copy.wait_send)


class Gather:
    def __init__(self, geo, comm, slots, group, buf, far_first=False):
        self.g, self.comm, self.buf, self.group = geo, comm, buf, group
        g = geo
        self.far_first = far_first and g.square
        if not g.square:
            self.s = slots
            self.order = [(g.t + g.n_t - k) % g.n_t for k in range(g.n_t)]
            self.lead = [g.n_t - 1] + [g.n_t - 1 - k for k in range(1, g.n_t)]
            return
        self.sx, self.sy = slots[:5], slots[5:]
        if self.far_first:
            self.order, self.lead = [g.t, g.td, g.tx, g.ty], [3, 0, 1, 2]
        else:
            self.order, self.lead = [g.t, g.tx, g.ty, g.td], [3, 1, 2, 0]

    def begin(self, i):
        g, comm = self.g, self.comm
        if g.square:
            self._give(self.sx[i], g.t, i, 1, g.tx)
            self._give(self.sy[i], g.t, 2 + i, 1, g.ty)
            if i == 1 and not self.far_first:
                self._rest()
        elif i == 1:
            own = self.buf.at[g.rows(g.t)]
            for k, peer in enumerate(g.to):
                comm.send(self.group, self.s[k], own, own, (g.d, peer))

    def sent(self):
        self.comm.sent(self.group, self.buf.at[0 : (self.g.n_t - 1) * self.g.R], (self.g.d, self.g.to[0]))

    def piece(self, blk, first, count):
        q = self.g.R // 4
        rows = pl.ds(pl.multiple_of(blk * self.g.R + first * q, q), count * q)
        return self.buf.at[rows]

    def _give(self, slot, blk, first, count, to):
        part = self.piece(blk, first, count)
        self.comm.send(self.group, slot, part, part, (self.g.d, to))

    def _rest(self):
        g = self.g
        self._give(self.sx[4], g.t, 2, 2, g.tx)
        self._give(self.sy[4], g.t, 0, 2, g.ty)

    def relay(self):
        g, comm = self.g, self.comm
        if not g.square:
            return
        for i in range(2):
            comm.recv(self.sx[i], self.piece(g.tx, i, 1), (g.d, g.tx))
            self._give(self.sy[2 + i], g.tx, i, 1, g.ty)
            comm.recv(self.sy[i], self.piece(g.ty, 2 + i, 1), (g.d, g.ty))
            self._give(self.sx[2 + i], g.ty, 2 + i, 1, g.tx)
        if self.far_first:
            self._rest()

    def wait(self, i):
        g, comm = self.g, self.comm
        if i == 0:
            return
        if not g.square:
            comm.recv(self.s[i - 1], self.buf.at[g.rows(self.order[i])], (g.d, self.order[i]))
            return
        which = "dxy"[i - 1] if self.far_first else "xyd"[i - 1]
        if which == "x":
            comm.recv(self.sx[4], self.piece(g.tx, 2, 2), (g.d, g.tx))
        elif which == "y":
            comm.recv(self.sy[4], self.piece(g.ty, 0, 2), (g.d, g.ty))
        else:
            for k in range(2):
                comm.recv(self.sx[2 + k], self.piece(g.td, 2 + k, 1), (g.d, g.tx))
                comm.recv(self.sy[2 + k], self.piece(g.td, k, 1), (g.d, g.ty))


def scatter_scratch(g):
    h = g.R // 2
    if g.square:
        return [pltpu.VMEM((3, 2, h, g.D), BF), pltpu.VMEM((2, h, g.D), BF), pltpu.VMEM((2, h, g.D), BF), pltpu.VMEM((2, 2, h, g.D), BF)]
    return [pltpu.VMEM((g.n_t - 1, 2, h, g.D), BF), pltpu.VMEM((1, 16, 128), BF), pltpu.VMEM((1, 16, 128), BF), pltpu.VMEM((g.n_t - 1, 2, h, g.D), BF)]


class Scatter:
    def __init__(self, geo, comm, slots, group, bufs):
        self.g, self.comm, self.group = geo, comm, group
        self.part, self.into, self.out, self.fin = bufs
        g = geo
        if g.square:
            self.sx, self.sy = slots[:4], slots[4:]
        else:
            self.s = slots

    def give(self, i, value):
        h = self.g.R // 2
        for j in range(2):
            self.part[i, j] = value[j * h : (j + 1) * h].astype(BF)
        if isinstance(i, int):
            self.send(i)
        else:
            for k in range(self.g.n_t - 1):
                pl.when(i == k)(functools.partial(self.send, k))

    def send(self, i):
        g, comm = self.g, self.comm
        if not g.square:
            comm.send(self.group, self.s[i], self.part.at[i], self.fin.at[i], (g.d, g.leave[i]))
        elif i == 0:
            comm.send(self.group, self.sx[0], self.part.at[0, 0], self.into.at[0], (g.d, g.tx))
            comm.send(self.group, self.sy[0], self.part.at[0, 1], self.into.at[1], (g.d, g.ty))
        elif i == 1:
            comm.send(self.group, self.sx[1], self.part.at[1, 0], self.fin.at[0, 0], (g.d, g.tx))
        else:
            comm.send(self.group, self.sy[1], self.part.at[2, 1], self.fin.at[1, 1], (g.d, g.ty))

    def relay(self):
        g, comm = self.g, self.comm
        if not g.square:
            return
        q = g.R // 4
        comm.recv(self.sx[0], self.into.at[0], (g.d, g.tx))
        comm.recv(self.sy[0], self.into.at[1], (g.d, g.ty))
        for k in range(2):
            rows = slice(k * q, (k + 1) * q)
            for a, mine, slots, to in ((0, (2, 0), self.sy, g.ty), (1, (1, 1), self.sx, g.tx)):
                self.out[a, rows] = (self.into[a, rows].astype(F32) + self.part[(*mine, rows)].astype(F32)).astype(BF)
                comm.send(self.group, slots[2 + k], self.out.at[a, rows], self.fin.at[1 - a, a, rows], (g.d, to))

    def take(self, i, own):
        g, comm = self.g, self.comm
        q = g.R // 4
        count = 2 if g.square else g.n_t - 1
        inner = slice(i * q, (i + 1) * q)
        if g.square:
            if i == 0:
                comm.recv(self.sx[1], self.fin.at[0, 0], (g.d, g.tx))
                comm.recv(self.sy[1], self.fin.at[1, 1], (g.d, g.ty))
            comm.recv(self.sx[2 + i], self.fin.at[0, 1, inner], (g.d, g.tx))
            comm.recv(self.sy[2 + i], self.fin.at[1, 0, inner], (g.d, g.ty))
        elif i == 0:
            for k in range(count):
                comm.recv(self.s[k], self.fin.at[k], (g.d, (g.t + g.n_t - k - 1) % g.n_t))
        pairs = []
        for j in range(2):
            rows = slice(2 * j * q + i * q, 2 * j * q + (i + 1) * q)
            v = own[rows]
            for k in range(count):
                v = v + self.fin[k, j, inner].astype(F32)
            pairs.append((rows, v))
        if i == 1:
            comm.sent(self.group, self.part, (g.d, g.to[0]))
        return pairs


class WeightGather:
    def __init__(self, geo, comm, buf, first, n):
        self.g, self.comm, self.buf, self.of = geo, comm, buf, pl.ds(first, n)
        g = geo
        self.group = comm.group()
        self.inner = (g.chip == 1) | (g.chip == 2)
        self.sz, self.sc = comm.slots(g.C - 1), comm.slots(g.C)

    def at(self, d):
        return self.buf.at[self.of, self.g.wrows(d)]

    def far(self):
        g, comm = self.g, self.comm
        if g.line:
            comm.send(self.group, self.sz[1], self.at(g.d), self.at(g.d), (g.zto(2), g.t))

    def near(self):
        g, comm = self.g, self.comm
        own = self.at(g.d)
        for k in range(1, g.C):
            if g.line and k == 2:
                continue
            near = g.chip != (0 if k == 3 else 3) if g.line else None
            comm.send(self.group, self.sz[k - 1], own, own, (g.zto(k), g.t), when=near)
        comm.send(self.group, self.sc[0], own, own, (g.sib, g.t))

    def _take(self, k, when=None):
        g, comm = self.g, self.comm
        block = self.at(g.zfrom(k))
        comm.recv(self.sz[k - 1], block, (g.zfrom(k), g.t), when=when)
        comm.send(self.group, self.sc[k], block, block, (g.sib, g.t), when=when)

    def relay(self):
        g, comm = self.g, self.comm
        if not g.line:
            return
        self._take(2, self.inner)
        block = self.at(g.zfrom(2))
        comm.send(self.group, self.sz[2], block, block, (6 + g.core, g.t), when=g.chip == 2)
        comm.send(self.group, self.sz[0], block, block, (g.core, g.t), when=g.chip == 1)

    def pass_on(self):
        g = self.g
        for k in range(1, g.C):
            self._take(k, jnp.logical_not(self.inner) if g.line and k == 2 else None)

    def wait(self):
        g, comm = self.g, self.comm
        for k in range(g.C):
            other = g.zfrom(k) + 1 - 2 * g.core
            comm.recv(self.sc[k], self.at(other), (g.sib, g.t))

    def sent(self):
        g, comm = self.g, self.comm

        def some(n, when=None):
            comm.sent(self.group, self.buf.at[self.of, 0 : n * g.Dn], (g.sib, g.t), when)

        if g.line:
            some(8, self.inner)
            some(6, jnp.logical_not(self.inner))
        else:
            some(2 * g.C - 1)


class WeightScatter:
    def __init__(self, geo, comm, src, bufs):
        self.g, self.comm, self.src = geo, comm, src
        self.sib_in, self.out, self.fin = bufs
        g = geo
        self.group = comm.group()
        self.sc, self.sz = comm.slots(1)[0], comm.slots(5 if g.line else g.C - 1)
        half = g.chip // 2
        self.near, self.inner, self.other, self.opposite = 3 * half, 1 + half, 2 - half, 3 - 3 * half
        self.end = (g.chip == 0) | (g.chip == 3)

    def start(self):
        g, comm = self.g, self.comm
        for j in range(g.C):
            block = self.src.at[g.wrows(2 * j + 1 - g.core)]
            comm.send(self.group, self.sc, block, self.sib_in.at[j], (g.sib, g.t))

    def _sum(self, chip):
        return self.src[self.g.wrows(2 * chip + self.g.core)].astype(F32) + self.sib_in[chip].astype(F32)

    def meet(self):
        g, comm = self.g, self.comm
        comm.recv(self.sc, self.sib_in, (g.sib, g.t))

    def part(self, b):
        g, comm = self.g, self.comm
        if not g.line:
            for k in range(1, g.C) if b == 0 else ():
                self.out[k - 1][...] = self._sum((g.chip + k) % g.C).astype(BF)
                comm.send(self.group, self.sz[k - 1], self.out[k - 1], self.fin.at[k - 1], (g.zto(k), g.t))
            return

        @pl.when(self.end)
        def _():
            self.out[b][...] = self._sum((self.opposite, self.other, self.inner)[b]).astype(BF)

        to = (self.inner * 2 + g.core, g.t)
        comm.send(self.group, self.sz[b], self.out[b], self.fin.at[b], to, when=self.end)

    def pass_on(self):
        self.meet()
        for b in range(3):
            self.part(b)

    def relay(self, b):
        g, comm = self.g, self.comm
        if not g.line:
            return
        middle = jnp.logical_not(self.end)
        came = (0, 1, 3)[b]

        @pl.when(middle)
        def _():
            comm.recv(self.sz[came], self.fin.at[came], (g.sib, g.t))
            mine = self._sum((self.opposite, self.other, self.near)[b])
            self.out[b][...] = (mine + self.fin[came].astype(F32)).astype(BF)

        goes = (3, 4, 0)[b]
        to = ((self.other, self.other, self.near)[b] * 2 + g.core, g.t)
        comm.send(self.group, self.sz[goes], self.out[b], self.fin.at[goes], to, when=middle)

    def sent(self):
        g = self.g
        self.comm.sent(self.group, self.src.at[0 : (2 * g.C - 1) * g.Dn], (g.sib, g.t))

    def total(self):
        g, comm = self.g, self.comm
        mine = self.src[g.wrows(g.d)].astype(F32) + self.sib_in[g.chip].astype(F32)
        if not g.line:
            for k in range(1, g.C):
                comm.recv(self.sz[k - 1], self.fin.at[k - 1], (g.zfrom(k), g.t))
                mine = mine + self.fin[k - 1].astype(F32)
            return mine
        middle = jnp.logical_not(self.end)
        comm.recv(self.sz[0], self.fin.at[0], (g.sib, g.t), when=self.end)
        comm.recv(self.sz[2], self.fin.at[2], (g.sib, g.t), when=middle)
        comm.recv(self.sz[4], self.fin.at[4], (g.sib, g.t), when=middle)
        at_end = self.fin[0].astype(F32)
        between = self.fin[2].astype(F32) + self.fin[4].astype(F32)
        return mine + jnp.where(self.end, at_end, between)


def weight_scatter_scratch(g, n, w):
    steps = 5 if g.line else g.C - 1
    return [pltpu.VMEM((n, g.C, g.Dn, w), BF), pltpu.VMEM((n, g.C - 1, g.Dn, w), BF), pltpu.VMEM((n, steps, g.Dn, w), BF)]


def rotated(v, cosine, sine):
    n = v.shape[1]
    if n > cosine.shape[1]:
        cosine = jnp.concatenate([cosine] * (n // cosine.shape[1]), axis=1)
        sine = jnp.concatenate([sine] * (n // sine.shape[1]), axis=1)
    lower = lax.broadcasted_iota(jnp.int32, v.shape, 1) % HD < HD // 2
    swapped = jnp.where(lower, pltpu.roll(v, n - HD // 2, 1), pltpu.roll(v, HD // 2, 1))
    return v * cosine + swapped * sine


def head_lanes(v, h):
    lane = lax.broadcasted_iota(jnp.int32, v.shape, 1)
    keep = (lane >= h * HD) & (lane < (h + 1) * HD)
    return jnp.where(keep, v, jnp.zeros_like(v))


def attend(g, hi, q_blk, keys_rot, values_t, bias, probs, inverse):
    H, R = g.H, g.R
    step = min(512, hi)
    spans = [slice(k, k + step) for k in range(0, hi, step)]
    scores, top, sums, mix = {}, [None] * H, [None] * H, [None] * H

    def fold(v, op):
        return op(v.reshape(v.shape[0] // 8, 8, v.shape[1]), axis=0)

    def first(h, span):
        s = dot(keys_rot[span], head_lanes(q_blk, h), NT) + bias[span]
        scores[h, span.start] = s
        most = fold(s, jnp.max)
        top[h] = most if top[h] is None else jnp.maximum(top[h], most)

    def second(h, span):
        if span.start == 0:
            top[h] = jnp.max(top[h], axis=0, keepdims=True)
        e = jnp.exp(scores.pop((h, span.start)) - top[h])
        some = fold(e, jnp.sum)
        sums[h] = some if sums[h] is None else sums[h] + some
        low = e.astype(BF)
        probs[span, h * R : (h + 1) * R] = low
        out = dot(values_t[h * HD : (h + 1) * HD, span], low)
        mix[h] = out if mix[h] is None else mix[h] + out

    for h in range(H + 1):
        for span in spans:
            if h < H:
                first(h, span)
            if h > 0:
                second(h - 1, span)
    for h in range(H):
        inv = 1.0 / jnp.sum(sums[h], axis=0, keepdims=True)
        inverse[h : h + 1, :] = inv
        mix[h] = mix[h] * inv
    return jnp.concatenate(mix, axis=0)


def attend_back(g, hi, values, keys_t, probs, go, qm, dots, dk, dv):
    H, R = g.H, g.R
    step = 256 if hi < g.S else hi
    grads = [None] * H
    for k in range(0, hi + step, step):
        now, past = slice(k, k + step), slice(k - step, k)
        if k < hi:
            if step < hi:
                dv[now] += dot(probs[now], go[...])
            ahead = [dot(values[now], go[0:R], NT)]
            for h in range(H):
                cols = slice(h * R, (h + 1) * R)
                if h + 1 < H:
                    ahead.append(dot(values[now], go[(h + 1) * R : (h + 2) * R], NT))
                low = (probs[now, cols].astype(F32) * (ahead[h] - dots[h])).astype(BF)
                if h == 0 and step == hi:
                    dv[now] += dot(probs[now], go[...])
                probs[now, cols] = low
                out = dot(keys_t[h * HD : (h + 1) * HD, now], low)
                grads[h] = out if grads[h] is None else grads[h] + out
        if k > 0:
            dk[past] += dot(probs[past], qm[...])
    return jnp.concatenate(grads, axis=0)


def bias_of(qinfo, kinfo, first, size, rows):
    shape = (size, rows)
    doc_q, pic_q = qinfo[0:1, :], qinfo[1:2, :]
    key_doc, pic_k = kinfo[:, 0:1], kinfo[:, 1:2]
    key_pos = lax.broadcasted_iota(jnp.int32, shape, 0)
    query_pos = lax.broadcasted_iota(jnp.int32, shape, 1) + first
    before = key_pos <= query_pos
    open_ = (doc_q == key_doc) & (before | (pic_q == pic_k))
    ok = open_ | (key_pos == query_pos)
    return jnp.where(ok, 0.0, MASKED).astype(F32)


def rotary(length, cols):
    half = HD // 2
    frequency = 10000.0 ** (-2.0 * np.arange(half) / HD)
    angle = np.arange(length)[:, None] * frequency[None, :]
    cosine = np.concatenate([np.cos(angle)] * 2, axis=1)
    sine = np.concatenate([-np.sin(angle), np.sin(angle)], axis=1)
    reps = max(1, min(cols, 128) // HD)
    return (jnp.asarray(np.tile(cosine, (1, reps)), F32), jnp.asarray(np.tile(sine, (1, reps)), F32))


def in_slot(g, n_pic, blk):
    per = g.n_t // n_pic

    def run(body):
        for p in range(n_pic):
            pl.when(blk // per == p)(functools.partial(body, p, blk - p * per, (p + 1) * (g.S // n_pic)))

    return run


def layer_body(g, n_pic, x, teacher, valid_mask, documents, starts, wq, wk, wv, wo, wg, wu, wd, cosine, sine,
               o_out, o_in, o_q, o_k, o_v, o_o, o_g, o_u, o_d, o_loss,
               rows1, rows2, gm, ga, wa, wm, qkv, mixed, mixt, turn, wo_t, probs0, probs1, acc2, qm, gom, mids, middle, cot,
               qinfo, kinfo, rinv, cnt, err,
               part, into, out, fin,
               sib_m, fin_m, sib_a, out_a, fin_a, output, grad_inputs, dattn, dout, dmlp, stats,
               ts, tr, zs, zr, local):
    g.place()
    g.greet()
    R, S, c, H, C, Dn = g.R, g.S, g.c, g.H, g.C, g.Dn
    tc, zc = Comm(ts, tr), Comm(zs, zr)
    sums = (part, into, out, fin)
    few, ag_group, rs_group = tc.group(), tc.group(), tc.group()
    ag_slots = tc.slots(10 if g.square else g.n_t - 1)
    rs_slots = tc.slots(8 if g.square else g.n_t - 1)
    te = tc.slots(2 if g.square else g.n_t - 1)
    gather = functools.partial(Gather, g, tc, ag_slots, ag_group)
    scatter = functools.partial(Scatter, g, tc, rs_slots, rs_group, sums)
    q, kk, v = qkv.at[0], qkv.at[1], qkv.at[2]
    probs = (probs0, probs1)
    bias, dk, dv = acc2.at[:, :, :R], acc2.at[0, :, :c], acc2.at[1, :, :c]
    stores = []

    def store(buf, to):
        copy = pltpu.make_async_copy(buf, to, local.at[1 + len(stores)])
        copy.start()
        stores.append(copy)

    get_teacher = pltpu.make_async_copy(teacher, cot, local.at[0])
    get_teacher.start()

    one, _ = normed(x[...])
    rows1[g.rows(g.t)] = one.astype(BF)
    block = g.wrows(g.d)
    wa[0, block] = wq[...]
    wa[1, block] = wk[...]
    wa[2, block] = wv[...]
    g.meet()
    ag = gather(rows1)
    ag.begin(0)
    ag.begin(1)
    za, zo = WeightGather(g, zc, wa, 0, 3), WeightGather(g, zc, wa, 3, 1)
    zg, zd = WeightGather(g, zc, wm, 0, 2), WeightGather(g, zc, wm, 2, 1)
    za.far()
    wa[3, block] = turned(wo[...])
    zo.far()
    za.near()
    wm[0, block] = turned(wg[...])
    wm[1, block] = turned(wu[...])
    wm[2, block] = turned(wd[...])

    csib, cz = zc.slots(1)[0], zc.slots(C - 1)
    gsib, gz = zc.group(), zc.group()
    valid, doc = valid_mask[...], documents[...]
    cnt[0] = jnp.broadcast_to(jnp.sum(valid.astype(F32), axis=1, keepdims=True), (8, 128))
    zc.send(gsib, csib, cnt.at[0], cnt.at[1], (g.sib, g.t))
    at = lax.broadcasted_iota(jnp.int32, (1, S), 1)
    pic = jnp.zeros((1, S), jnp.int32)
    for p in range(n_pic):
        first = starts[0:1, p : p + 1]
        pic = jnp.where((at >= first) & (at < first + PIECE), p + 1, pic)
    qinfo[0:1] = doc
    qinfo[1:2] = pic
    as_keys = [jnp.where(valid == 1, doc, -1), jnp.where(pic > 0, pic, -1), valid]
    as_keys = jnp.concatenate([a.astype(F32) for a in as_keys] + [jnp.zeros((125, S), F32)], axis=0)
    kinfo[...] = as_keys.T.astype(jnp.int32)
    zc.recv(csib, cnt.at[1], (g.sib, g.t))
    cnt[2] = cnt[0] + cnt[1]
    for k in range(1, C):
        zc.send(gz, cz[k - 1], cnt.at[2], cnt.at[2 + k], (g.zto(k), g.t))

    def set_bias(i, blk):
        @in_slot(g, n_pic, blk)
        def _(p, index, hi):
            bias[i % 2, 0:hi] = bias_of(qinfo[:, g.rows(blk)], kinfo[0:hi], blk * R, hi, R)

    set_bias(0, g.leave[0])

    ag.relay()
    za.relay()
    zo.relay()
    zo.near()
    za.pass_on()
    za.wait()
    zg.far()
    zg.near()
    for i, blk in enumerate(ag.order):
        ag.wait(i)
        at = g.rows(blk)
        row = rows1[at]
        cos_b, sin_b = cosine[at], sine[at]
        q[at] = (rotated(dot(row, wa[0]), cos_b, sin_b) * HD**-0.5).astype(BF)
        kk[at] = rotated(dot(row, wa[1]), cos_b, sin_b).astype(BF)
        v[at] = dot(row, wa[2]).astype(BF)
    zo.pass_on()
    turn[...] = turned(v[...])

    rs = scatter()
    @pl.loop(0, g.n_t)
    def _(i):
        blk = g.leave_at(i)
        at = g.rows(blk)

        @pl.when(i > 0)
        def _():
            set_bias(i, blk)

        @in_slot(g, n_pic, blk)
        def _(p, index, hi):
            both = attend(g, hi, q[at], kk, turn, bias.at[i % 2], probs[p].at[index], rinv.at[blk])
            mixt[blk] = both.astype(BF)
            mixed[at] = both.T.astype(BF)

        pl.when(i == 0)(zo.wait)

        @pl.when(i == 2)
        def _():
            zg.relay()
            zd.far()
            zd.near()

        @pl.when(i < g.n_t - 1)
        def _():
            rs.give(i, dot(mixed[at], wa[3], NT))

    rs.relay()
    middle[0:R] = x[...] + dot(mixed[g.rows(g.t)], wa[3], NT)
    ag.sent()
    ag = gather(rows2, far_first=True)

    for i in range(2):
        for rows, summed in rs.take(i, middle):
            middle[rows] = summed
            two, _ = normed(summed)
            rows2[g.rows(g.t, rows.start, R // 4)] = two.astype(BF)
        ag.begin(i)
    rs = scatter()
    zd.relay()
    ag.relay()
    zg.pass_on()
    zg.wait()

    @pl.loop(0, g.n_t)
    def _(i):
        for k in range(1, g.n_t):
            pl.when(i == k)(functools.partial(ag.wait, k))
        at = g.rows(g.far_at(i))
        row = rows2[at]
        gate, up = dot(row, wm[0]), dot(row, wm[1])
        sig = jax.nn.sigmoid(gate)
        act = gate * sig
        mids[0, at] = (act * up).astype(BF)
        mids[2, at] = act.astype(BF)
        mids[1, at] = (up * sig * (1.0 + gate * (1.0 - sig))).astype(BF)

        @pl.when(i == 1)
        def _():
            zd.pass_on()
            zd.wait()

        @pl.when(i > 0)
        def _():
            rs.give(g.far_lead(i), dot(mids[0, at], wm[2], NT))

    output[...] = middle[0:R] + dot(mids[0, g.rows(g.t)], wm[2], NT)
    wo_t[...] = turned(wa[3])
    rs.relay()

    get_teacher.wait()
    tokens = cnt[2]
    for k in range(1, C):
        zc.recv(cz[k - 1], cnt.at[2 + k], (g.zfrom(k), g.t))
        tokens = tokens + cnt[2 + k]
    share = 1.0 * S * g.n_dp / tokens[0:1, 0:1]
    ag.sent()
    ag = gather(gm, far_first=True)
    errors = jnp.zeros((R // 4, 1), F32)
    for i in range(2):
        for rows, summed in rs.take(i, output):
            output[rows] = summed
            dev = summed - cot[rows]
            kept = kinfo[g.rows(g.t, rows.start, R // 4), 2:3].astype(F32) * dev
            cotangent = kept * share
            cot[rows] = cotangent
            gm[g.rows(g.t, rows.start, R // 4)] = cotangent.astype(BF)
            errors += jnp.sum(kept * dev, axis=1, keepdims=True)
        ag.begin(i)
    store(output, o_out)
    err[0] = jnp.broadcast_to(jnp.sum(errors, axis=0, keepdims=True), (8, 128))

    rs = scatter()
    if g.square:
        tc.send(few, te[0], err.at[0], err.at[1], (g.d, g.tx))
    else:
        for k, peer in enumerate(g.to):
            tc.send(few, te[k], err.at[0], err.at[1 + k], (g.d, peer))

    @pl.loop(0, g.n_t)
    def _(i):
        for k in range(1, g.n_t):
            pl.when(i == k)(functools.partial(ag.wait, k))
        at = g.rows(g.far_at(i))
        gh = dot(gm[at], wm[2])
        mids[1, at] = (gh * mids[1, at].astype(F32)).astype(BF)
        mids[2, at] = (gh * mids[2, at].astype(F32)).astype(BF)

        @pl.when(i == 0)
        def _():
            ag.relay()
            rows2[...] = turned(rows2[...])
            turn[...] = turned(kk[...])

        @pl.when(i > 0)
        def _():
            rs.give(g.far_lead(i), dot(mids[1, at], wm[0], NT) + dot(mids[2, at], wm[1], NT))

    at = g.rows(g.t)
    grad_inputs[...] = dot(mids[1, at], wm[0], NT) + dot(mids[2, at], wm[1], NT)
    zg.sent()
    zd.sent()
    wm[0] = dot(rows2[...], mids[1]).astype(BF)

    zscat = []

    def start_mlp(j, used):
        spare = [mids.at[used, k * Dn : (k + 1) * Dn] for k in range(C - 1)]
        zscat.append(WeightScatter(g, zc, wm.at[j], (sib_m.at[j], spare, fin_m.at[j])))
        zscat[-1].start()

    start_mlp(0, 1)
    rs.relay()
    zscat[0].pass_on()
    wm[1] = dot(rows2[...], mids[2]).astype(BF)
    start_mlp(1, 2)
    for k in range(0, g.D, 256):
        wm[2, k : k + 256] = dot(turned(gm[:, k : k + 256]), mids[0]).astype(BF)
    start_mlp(2, 0)
    zscat[1].pass_on()
    two, inv = normed(middle[0:R])
    ag.sent()
    ag = gather(ga)
    for i in range(2):
        for rows, back in rs.take(i, grad_inputs):
            grad_middle = cot[rows] + normed_back(two[rows], inv[rows], back)
            cot[rows] = grad_middle
            ga[g.rows(g.t, rows.start, R // 4)] = grad_middle.astype(BF)
        ag.begin(i)

    for j in (3, 0, 1, 2):
        spare = [out_a.at[j, k] for k in range(C - 1)]
        zscat.append(WeightScatter(g, zc, wa.at[j], (sib_a.at[j], spare, fin_a.at[j])))

    rs = scatter()
    zscat[2].pass_on()
    zscat[0].relay(0)
    zscat[0].relay(1)
    base = 4 if g.square else g.n_t
    ec, ez = zc.slots(1)[0], zc.slots(C - 1)
    gec, gez = zc.group(), zc.group()
    if g.square:
        tc.recv(te[0], err.at[1], (g.d, g.tx))
        err[2] = err[0] + err[1]
        tc.send(few, te[1], err.at[2], err.at[3], (g.d, g.ty))
    acc2[...] = jnp.zeros_like(acc2)
    middle[0:c] = jnp.zeros((c, g.D), F32)

    @pl.loop(0, g.n_t)
    def _(i):
        @pl.when(i == 1)
        def _():
            zscat[0].relay(2)
            rows1[...] = turned(rows1[...])
            if g.square:
                tc.recv(te[1], err.at[3], (g.d, g.ty))
                err[base] = err[2] + err[3]
            else:
                total = err[0]
                for k in range(1, g.n_t):
                    tc.recv(te[k - 1], err.at[k], (g.d, (g.t + g.n_t - k) % g.n_t))
                    total = total + err[k]
                err[base] = total
            zc.send(gec, ec, err.at[base], err.at[base + 1], (g.sib, g.t))

        @pl.when(i == 2)
        def _():
            zc.recv(ec, err.at[base + 1], (g.sib, g.t))
            err[base + 2] = err[base] + err[base + 1]
            for k in range(1, C):
                zc.send(gez, ez[k - 1], err.at[base + 2], err.at[base + 2 + k], (g.zto(k), g.t))

        for k in range(1, g.n_t):
            pl.when(i == k)(functools.partial(ag.wait, k))
        blk = g.arrive_at(i)
        at = g.rows(blk)
        middle[0:c] += dot(mixt[blk], ga[at])

        @pl.when(i == g.n_t - 1)
        def _():
            zo.sent()
            wa[3] = turned(middle[0:c].astype(BF))
            zscat[3].start()

        go_t = dot(wo_t[...], ga[at], NT).astype(BF).astype(F32)
        mix_t = mixt[blk].astype(F32)
        scaled, dots = [], []
        for h in range(H):
            one_head = go_t[h * HD : (h + 1) * HD] * rinv[blk, h : h + 1, :]
            scaled.append(one_head)
            dots.append(jnp.sum(one_head * mix_t[h * HD : (h + 1) * HD], axis=0, keepdims=True))
        go = jnp.concatenate(scaled, axis=0).T.astype(BF)
        q_blk = q[at]
        for h in range(H):
            gom[h * R : (h + 1) * R] = head_lanes(go, h)
            qm[h * R : (h + 1) * R] = head_lanes(q_blk, h)

        @in_slot(g, n_pic, blk)
        def _(p, index, hi):
            dq = attend_back(g, hi, v, turn, probs[p].at[index], gom, qm, dots, dk, dv).T * HD**-0.5
            q[at] = rotated(dq, cosine[at], -sine[at]).astype(BF)

        pl.when(i == 0)(ag.relay)

        @pl.when(i == 2)
        def _():
            zscat[1].relay(0)
            zscat[1].relay(1)

    @pl.loop(0, g.n_t)
    def _(i):
        at = g.rows(g.leave_at(i))
        kk[at] = rotated(dk[at], cosine[at], -sine[at]).astype(BF)
        v[at] = dv[at].astype(BF)
        partial = dot(q[at], wa[0], NT) + dot(kk[at], wa[1], NT) + dot(v[at], wa[2], NT)

        @pl.when(i < g.n_t - 1)
        def _():
            rs.give(i, partial)

        @pl.when(i == g.n_t - 1)
        def _():
            grad_inputs[...] = partial


    zscat[3].pass_on()
    zscat[1].relay(2)
    zscat[2].relay(0)
    zscat[2].relay(1)
    za.sent()
    for j in range(3):
        wa[j] = dot(rows1[...], qkv[j]).astype(BF)
        zscat[4 + j].start()
    for j in (4, 5, 6):
        zscat[j].meet()
        zscat[j].part(0)
    rs.relay()
    for k in (1, 2):
        for j in (4, 5, 6):
            zscat[j].part(k)
    zscat[2].relay(2)
    zscat[3].relay(0)
    zscat[3].relay(1)
    one, inv = normed(x[...])

    for j, to in enumerate((o_g, o_u, o_d)):
        dmlp[j] = zscat[j].total().T
        store(dmlp.at[j], to)
    for j in (4, 5, 6):
        zscat[j].relay(0)
    zscat[3].relay(2)
    for j, k in ((4, 2), (5, 2), (4, 1), (6, 2), (5, 1)):
        zscat[j].relay(k)
    for i in range(2):
        for rows, back in rs.take(i, grad_inputs):
            grad_inputs[rows] = cot[rows] + normed_back(one[rows], inv[rows], back)
    store(grad_inputs, o_in)
    zscat[6].relay(1)
    dout[...] = zscat[3].total().T
    store(dout, o_o)
    total = err[base + 2]
    for k in range(1, C):
        zc.recv(ez[k - 1], err.at[base + 2 + k], (g.zfrom(k), g.t))
        total = total + err[base + 2 + k]
    stats[...] = (total * (1.0 / g.D) / tokens)[0:1, 0:1]
    store(stats, o_loss)
    for j, to in enumerate((o_q, o_k, o_v)):
        dattn[j] = zscat[4 + j].total()
        store(dattn.at[j], to)
    for copy in stores:
        copy.wait()
    ag.sent()
    for scat in zscat:
        scat.sent()
    tc.sent(few, err.at[0 : len(te)], (g.sib, g.t))
    for group, n in ((gsib, 1), (gz, C - 1), (gec, 1), (gez, C - 1)):
        zc.sent(group, cnt.at[0:n], (g.sib, g.t))
    assert tc.n <= tr.shape[0] and zc.n <= zr.shape[0] and tc.groups <= ts.shape[0] and zc.groups <= zs.shape[0]


def layer(g, n_pic, args):
    S, R, D, c, f, H, C, Dn = g.S, g.R, g.D, g.c, g.f, g.H, g.C, g.Dn
    sds, V = jax.ShapeDtypeStruct, pltpu.VMEM
    shapes = [(R, D), (R, D), (Dn, c), (Dn, c), (Dn, c), (c, Dn), (f, Dn), (f, Dn), (f, Dn), (1, 1)]
    outs = [sds(s, F32) for s in shapes]
    base = 4 if g.square else g.n_t
    scratch = [V((S, D), BF)] * 4 + [
        V((4, D, c), BF), V((3, D, f), BF), V((3, S, c), BF), V((S, c), BF), V((g.n_t, c, R), BF), V((c, S), BF), V((c, D), BF),
        V((g.n_t // 2, S // 2, H * R), BF), V((g.n_t // 2, S, H * R), BF), V((2, S, max(R, c)), F32), V((H * R, c), BF), V((H * R, c), BF), V((3, S, f), BF),
        V((max(R, c), D), F32), V((R, D), F32), V((8, S), jnp.int32), V((S, 128), jnp.int32), V((g.n_t, 8, R), F32),
        V((2 + C, 8, 128), F32), V((base + 2 + C, 8, 128), F32),
    ]
    scratch += scatter_scratch(g)
    m = weight_scatter_scratch(g, 3, f)
    scratch += [m[0], m[2]] + weight_scatter_scratch(g, 4, c)
    scratch += [V((R, D), F32), V((R, D), F32), V((3, Dn, c), F32), V((c, Dn), F32), V((3, f, Dn), F32), V((1, 1), F32)]
    nt = 20 if g.square else 3 * (g.n_t - 1)
    nz = 4 * (2 * C - 1) + 7 * (6 if g.line else C) + 2 * C
    sem = pltpu.SemaphoreType.DMA
    scratch += [sem((3,)), sem((nt,)), sem((15,)), sem((nz,)), sem((11,))]
    whole = pl.BlockSpec(memory_space=pltpu.VMEM)
    specs = [whole] * len(args)
    specs[1] = pl.BlockSpec(memory_space=pl.ANY)
    return pl.pallas_call(
        functools.partial(layer_body, g, n_pic),
        name="layer",
        out_shape=outs,
        in_specs=specs,
        out_specs=[pl.BlockSpec(memory_space=pl.ANY)] * len(outs),
        scratch_shapes=scratch,
        compiler_params=pltpu.CompilerParams(collective_id=1, has_side_effects=True, vmem_limit_bytes=VMEM_BYTES),
    )(*args)


def finish_body(n, *refs):
    parts, outs, bufs, come, go = refs[:n], refs[n : 2 * n], refs[2 * n : 3 * n], refs[3 * n], refs[3 * n + 1]
    loads = [pltpu.make_async_copy(a, b, come.at[k]) for k, (a, b) in enumerate(zip(parts, bufs))]
    stores = [pltpu.make_async_copy(a, b, go.at[k]) for k, (a, b) in enumerate(zip(bufs, outs))]
    for copy in loads:
        copy.start()
    for load, store in zip(loads, stores):
        load.wait()
        store.start()
    for copy in stores:
        copy.wait()


def finish(parts):
    anywhere, n = pl.BlockSpec(memory_space=pl.ANY), len(parts)
    return pl.pallas_call(
        functools.partial(finish_body, n),
        name="finish",
        out_shape=[jax.ShapeDtypeStruct(p.shape, F32) for p in parts],
        in_specs=[anywhere] * n,
        out_specs=[anywhere] * n,
        scratch_shapes=[pltpu.VMEM(p.shape, F32) for p in parts] + [pltpu.SemaphoreType.DMA((n,))] * 2,
    )(*parts)


def per_device(n_dp, n_t, inputs, teacher, valid_mask, documents, picture_starts,
               w_query, w_key, w_value, w_out, w_gate, w_up, w_down):
    R, D = inputs.shape
    c, f = w_query.shape[1], w_gate.shape[1]
    g = Geo(n_dp, n_t, R, D, c, f)
    args = (inputs, teacher, valid_mask, documents, picture_starts, w_query, w_key, w_value, w_out, w_gate.T, w_up.T, w_down)
    parts = layer(g, picture_starts.shape[1], (*args, *rotary(g.S, c)))
    out, *grads, gate, up, down, loss = finish(parts)
    return (out, loss.reshape(()), *grads, gate.T, up.T, down)


def solution(mesh):
    rows, pair = P(("dp", "tensor"), None), P("dp", None)
    cut, across = P("dp", "tensor"), P("tensor", "dp")
    return jax.shard_map(
        functools.partial(per_device, mesh.shape["dp"], mesh.shape["tensor"]),
        mesh=mesh,
        in_specs=(rows, rows, pair, pair, pair, cut, cut, cut, across, cut, cut, across),
        out_specs=(rows, P(), rows, cut, cut, cut, across, cut, cut, across),
        check_vma=False,
    )
```

```python
import functools

import jax
import jax.numpy as jnp
import numpy as np
from jax import lax
from jax.experimental import pallas as pl
from jax.experimental.pallas import tpu as pltpu
from jax.sharding import PartitionSpec as P

MESH = pl.DeviceIdType.MESH
HD = 64
PIECE = 256
EPS = 1e-5
MASKED = -1e30
VMEM_BYTES = 60 * 2**20
BF = jnp.bfloat16
F32 = jnp.float32
NT = (((1,), (1,)), ((), ()))
NN = (((1,), (0,)), ((), ()))


def dot(a, b, dims=NN):
    return lax.dot_general(a, b, dims, preferred_element_type=F32)


def eye(n):
    return (
        lax.broadcasted_iota(jnp.int32, (n, n), 0) == lax.broadcasted_iota(jnp.int32, (n, n), 1)
    ).astype(F32).astype(BF)


def turned(a):
    n = a.shape[1]
    step = min(n, 256)
    parts = [dot(eye(min(step, n - k)), a[:, k : k + step], NT).astype(BF) for k in range(0, n, step)]
    return parts[0] if len(parts) == 1 else jnp.concatenate(parts, axis=0)


def mean_of(v):
    return jnp.sum(v, axis=1, keepdims=True) * (1.0 / v.shape[1])


def normed(v):
    centred = v - mean_of(v)
    inv = lax.rsqrt(mean_of(centred * centred) + EPS)
    return centred * inv, inv


def normed_back(n, inv, g):
    return inv * (g - mean_of(g) - n * mean_of(g * n))


class Geo:
    def __init__(self, n_dp, n_t, tok_rows, d_model, cols, hid):
        self.n_dp, self.n_t, self.R, self.D, self.c, self.f = n_dp, n_t, tok_rows, d_model, cols, hid
        self.C = n_dp // 2
        self.S = tok_rows * n_t
        self.H = cols // HD
        self.Dn = d_model // n_dp
        self.square = n_t == 4
        self.line = self.C == 4

    def place(self):
        self.d = lax.axis_index("dp")
        self.t = lax.axis_index("tensor")
        self.chip = self.d // 2
        self.core = self.d % 2
        if self.square:
            self.tx = self.t + 1 - 2 * (self.t % 2)
            self.ty = (self.t + 2) % 4
            self.td = 3 - self.t
            self.to = [self.tx, self.ty]
            self.leave = [self.td, self.tx, self.ty, self.t]
        else:
            n = self.n_t
            self.to = [(self.t + k) % n for k in range(1, n)]
            self.leave = [(self.t + k) % n for k in range(1, n)] + [self.t]
        self.sib = self.d + 1 - 2 * self.core
        return self

    def leave_at(self, i):
        if self.square:
            return 2 * ((self.t // 2 + i + 1) % 2) + (self.t % 2 + 1 - i // 2) % 2
        return (self.t + 1 + i) % self.n_t

    def arrive_at(self, i):
        if self.square:
            return 2 * ((self.t // 2 + i // 2) % 2) + (self.t % 2 + i % 2) % 2
        return (self.t + self.n_t - i) % self.n_t

    def far_at(self, i):
        if self.square:
            return 2 * ((self.t // 2 + i % 2) % 2) + (self.t % 2 + (i + 1) // 2) % 2
        return (self.t + self.n_t - i) % self.n_t

    def far_lead(self, i):
        return i - 1 if self.square else self.n_t - 1 - i

    def zto(self, k):
        return ((self.chip + k) % self.C) * 2 + self.core

    def zfrom(self, k):
        return ((self.chip + self.C - k) % self.C) * 2 + self.core

    def rows(self, blk, first=0, count=None):
        count = self.R if count is None else count
        return pl.ds(pl.multiple_of(blk * self.R + first, count), count)

    def wrows(self, d):
        return pl.ds(pl.multiple_of(d * self.Dn, self.Dn), self.Dn)

    def greet(self):
        bar = pltpu.get_barrier_semaphore()
        out = [(self.d, p) for p in self.to]
        out += [(self.zto(k), self.t) for k in range(1, self.C)] + [(self.sib, self.t)]
        for dev in out:
            pl.semaphore_signal(bar, inc=1, device_id=dev, device_id_type=MESH)
        self.met = len(out)

    def meet(self):
        pl.semaphore_wait(pltpu.get_barrier_semaphore(), self.met)


class Comm:
    def __init__(self, send_sem, recv_sem):
        self.ss, self.rs = send_sem, recv_sem
        self.n = self.groups = 0

    def slots(self, k):
        self.n += k
        return list(range(self.n - k, self.n))

    def group(self):
        self.groups += 1
        return self.groups - 1

    def _copy(self, group, slot, src, dst, dev):
        return pltpu.make_async_remote_copy(
            src_ref=src, dst_ref=dst, send_sem=self.ss.at[group], recv_sem=self.rs.at[slot], device_id=dev, device_id_type=MESH
        )

    def send(self, group, slot, src, dst, dev, when=None):
        copy = self._copy(group, slot, src, dst, dev)
        if when is None:
            copy.start()
        else:
            pl.when(when)(copy.start)

    def recv(self, slot, dst, dev, when=None):
        copy = self._copy(0, slot, dst, dst, dev)
        if when is None:
            copy.wait_recv()
        else:
            pl.when(when)(copy.wait_recv)

    def sent(self, group, like, dev, when=None):
        copy = self._copy(group, 0, like, like, dev)
        if when is None:
            copy.wait_send()
        else:
            pl.when(when)(copy.wait_send)


class Gather:
    def __init__(self, geo, comm, slots, group, buf, far_first=False):
        self.g, self.comm, self.buf, self.group = geo, comm, buf, group
        g = geo
        self.far_first = far_first and g.square
        if not g.square:
            self.s = slots
            self.order = [(g.t + g.n_t - k) % g.n_t for k in range(g.n_t)]
            self.lead = [g.n_t - 1] + [g.n_t - 1 - k for k in range(1, g.n_t)]
            return
        self.sx, self.sy = slots[:5], slots[5:]
        if self.far_first:
            self.order, self.lead = [g.t, g.td, g.tx, g.ty], [3, 0, 1, 2]
        else:
            self.order, self.lead = [g.t, g.tx, g.ty, g.td], [3, 1, 2, 0]

    def begin(self, i):
        g, comm = self.g, self.comm
        if g.square:
            self._give(self.sx[i], g.t, i, 1, g.tx)
            self._give(self.sy[i], g.t, 2 + i, 1, g.ty)
            if i == 1 and not self.far_first:
                self._rest()
        elif i == 1:
            own = self.buf.at[g.rows(g.t)]
            for k, peer in enumerate(g.to):
                comm.send(self.group, self.s[k], own, own, (g.d, peer))

    def sent(self):
        self.comm.sent(self.group, self.buf.at[0 : (self.g.n_t - 1) * self.g.R], (self.g.d, self.g.to[0]))

    def piece(self, blk, first, count):
        q = self.g.R // 4
        rows = pl.ds(pl.multiple_of(blk * self.g.R + first * q, q), count * q)
        return self.buf.at[rows]

    def _give(self, slot, blk, first, count, to):
        part = self.piece(blk, first, count)
        self.comm.send(self.group, slot, part, part, (self.g.d, to))

    def _rest(self):
        g = self.g
        self._give(self.sx[4], g.t, 2, 2, g.tx)
        self._give(self.sy[4], g.t, 0, 2, g.ty)

    def relay(self):
        g, comm = self.g, self.comm
        if not g.square:
            return
        for i in range(2):
            comm.recv(self.sx[i], self.piece(g.tx, i, 1), (g.d, g.tx))
            self._give(self.sy[2 + i], g.tx, i, 1, g.ty)
            comm.recv(self.sy[i], self.piece(g.ty, 2 + i, 1), (g.d, g.ty))
            self._give(self.sx[2 + i], g.ty, 2 + i, 1, g.tx)
        if self.far_first:
            self._rest()

    def wait(self, i):
        g, comm = self.g, self.comm
        if i == 0:
            return
        if not g.square:
            comm.recv(self.s[i - 1], self.buf.at[g.rows(self.order[i])], (g.d, self.order[i]))
            return
        which = "dxy"[i - 1] if self.far_first else "xyd"[i - 1]
        if which == "x":
            comm.recv(self.sx[4], self.piece(g.tx, 2, 2), (g.d, g.tx))
        elif which == "y":
            comm.recv(self.sy[4], self.piece(g.ty, 0, 2), (g.d, g.ty))
        else:
            for k in range(2):
                comm.recv(self.sx[2 + k], self.piece(g.td, 2 + k, 1), (g.d, g.tx))
                comm.recv(self.sy[2 + k], self.piece(g.td, k, 1), (g.d, g.ty))


def scatter_scratch(g):
    h = g.R // 2
    if g.square:
        return [pltpu.VMEM((3, 2, h, g.D), BF), pltpu.VMEM((2, h, g.D), BF), pltpu.VMEM((2, h, g.D), BF), pltpu.VMEM((2, 2, h, g.D), BF)]
    return [pltpu.VMEM((g.n_t - 1, 2, h, g.D), BF), pltpu.VMEM((1, 16, 128), BF), pltpu.VMEM((1, 16, 128), BF), pltpu.VMEM((g.n_t - 1, 2, h, g.D), BF)]


class Scatter:
    def __init__(self, geo, comm, slots, group, bufs):
        self.g, self.comm, self.group = geo, comm, group
        self.part, self.into, self.out, self.fin = bufs
        g = geo
        if g.square:
            self.sx, self.sy = slots[:4], slots[4:]
        else:
            self.s = slots

    def give(self, i, value):
        h = self.g.R // 2
        for j in range(2):
            self.part[i, j] = value[j * h : (j + 1) * h].astype(BF)
        if isinstance(i, int):
            self.send(i)
        else:
            for k in range(self.g.n_t - 1):
                pl.when(i == k)(functools.partial(self.send, k))

    def send(self, i):
        g, comm = self.g, self.comm
        if not g.square:
            comm.send(self.group, self.s[i], self.part.at[i], self.fin.at[i], (g.d, g.leave[i]))
        elif i == 0:
            comm.send(self.group, self.sx[0], self.part.at[0, 0], self.into.at[0], (g.d, g.tx))
            comm.send(self.group, self.sy[0], self.part.at[0, 1], self.into.at[1], (g.d, g.ty))
        elif i == 1:
            comm.send(self.group, self.sx[1], self.part.at[1, 0], self.fin.at[0, 0], (g.d, g.tx))
        else:
            comm.send(self.group, self.sy[1], self.part.at[2, 1], self.fin.at[1, 1], (g.d, g.ty))

    def relay(self):
        g, comm = self.g, self.comm
        if not g.square:
            return
        q = g.R // 4
        comm.recv(self.sx[0], self.into.at[0], (g.d, g.tx))
        comm.recv(self.sy[0], self.into.at[1], (g.d, g.ty))
        for k in range(2):
            rows = slice(k * q, (k + 1) * q)
            for a, mine, slots, to in ((0, (2, 0), self.sy, g.ty), (1, (1, 1), self.sx, g.tx)):
                self.out[a, rows] = (self.into[a, rows].astype(F32) + self.part[(*mine, rows)].astype(F32)).astype(BF)
                comm.send(self.group, slots[2 + k], self.out.at[a, rows], self.fin.at[1 - a, a, rows], (g.d, to))

    def take(self, i, own):
        g, comm = self.g, self.comm
        q = g.R // 4
        count = 2 if g.square else g.n_t - 1
        inner = slice(i * q, (i + 1) * q)
        if g.square:
            if i == 0:
                comm.recv(self.sx[1], self.fin.at[0, 0], (g.d, g.tx))
                comm.recv(self.sy[1], self.fin.at[1, 1], (g.d, g.ty))
            comm.recv(self.sx[2 + i], self.fin.at[0, 1, inner], (g.d, g.tx))
            comm.recv(self.sy[2 + i], self.fin.at[1, 0, inner], (g.d, g.ty))
        elif i == 0:
            for k in range(count):
                comm.recv(self.s[k], self.fin.at[k], (g.d, (g.t + g.n_t - k - 1) % g.n_t))
        pairs = []
        for j in range(2):
            rows = slice(2 * j * q + i * q, 2 * j * q + (i + 1) * q)
            v = own[rows]
            for k in range(count):
                v = v + self.fin[k, j, inner].astype(F32)
            pairs.append((rows, v))
        if i == 1:
            comm.sent(self.group, self.part, (g.d, g.to[0]))
        return pairs


class WeightGather:
    def __init__(self, geo, comm, buf, first, n):
        self.g, self.comm, self.buf, self.of = geo, comm, buf, pl.ds(first, n)
        g = geo
        self.group = comm.group()
        self.inner = (g.chip == 1) | (g.chip == 2)
        self.sz, self.sc = comm.slots(g.C - 1), comm.slots(g.C)

    def at(self, d):
        return self.buf.at[self.of, self.g.wrows(d)]

    def far(self):
        g, comm = self.g, self.comm
        if g.line:
            comm.send(self.group, self.sz[1], self.at(g.d), self.at(g.d), (g.zto(2), g.t))

    def near(self):
        g, comm = self.g, self.comm
        own = self.at(g.d)
        for k in range(1, g.C):
            if g.line and k == 2:
                continue
            near = g.chip != (0 if k == 3 else 3) if g.line else None
            comm.send(self.group, self.sz[k - 1], own, own, (g.zto(k), g.t), when=near)
        comm.send(self.group, self.sc[0], own, own, (g.sib, g.t))

    def _take(self, k, when=None):
        g, comm = self.g, self.comm
        block = self.at(g.zfrom(k))
        comm.recv(self.sz[k - 1], block, (g.zfrom(k), g.t), when=when)
        comm.send(self.group, self.sc[k], block, block, (g.sib, g.t), when=when)

    def relay(self):
        g, comm = self.g, self.comm
        if not g.line:
            return
        self._take(2, self.inner)
        block = self.at(g.zfrom(2))
        comm.send(self.group, self.sz[2], block, block, (6 + g.core, g.t), when=g.chip == 2)
        comm.send(self.group, self.sz[0], block, block, (g.core, g.t), when=g.chip == 1)

    def pass_on(self):
        g = self.g
        for k in range(1, g.C):
            self._take(k, jnp.logical_not(self.inner) if g.line and k == 2 else None)

    def wait(self):
        g, comm = self.g, self.comm
        for k in range(g.C):
            other = g.zfrom(k) + 1 - 2 * g.core
            comm.recv(self.sc[k], self.at(other), (g.sib, g.t))

    def sent(self):
        g, comm = self.g, self.comm

        def some(n, when=None):
            comm.sent(self.group, self.buf.at[self.of, 0 : n * g.Dn], (g.sib, g.t), when)

        if g.line:
            some(8, self.inner)
            some(6, jnp.logical_not(self.inner))
        else:
            some(2 * g.C - 1)


class WeightScatter:
    def __init__(self, geo, comm, block, most, bufs):
        self.g, self.comm, self.block, self.most = geo, comm, block, most
        self.sib_in, self.out, self.fin = bufs
        g = geo
        self.group = comm.group()
        self.sc, self.sz = comm.slots(1)[0], comm.slots(5 if g.line else g.C - 1)
        half = g.chip // 2
        self.near, self.inner, self.other, self.opposite = 3 * half, 1 + half, 2 - half, 3 - 3 * half
        self.end = (g.chip == 0) | (g.chip == 3)

    def start(self):
        g, comm = self.g, self.comm
        for j in range(g.C):
            comm.send(self.group, self.sc, self.block(2 * j + 1 - g.core), self.sib_in.at[j], (g.sib, g.t))

    def _sum(self, chip):
        return self.block(2 * chip + self.g.core)[...].astype(F32) + self.sib_in[chip].astype(F32)

    def meet(self):
        g, comm = self.g, self.comm
        comm.recv(self.sc, self.sib_in, (g.sib, g.t))

    def part(self, b):
        g, comm = self.g, self.comm
        if not g.line:
            for k in range(1, g.C) if b == 0 else ():
                self.out[k - 1][...] = self._sum((g.chip + k) % g.C).astype(BF)
                comm.send(self.group, self.sz[k - 1], self.out[k - 1], self.fin.at[k - 1], (g.zto(k), g.t))
            return

        @pl.when(self.end)
        def _():
            self.out[b][...] = self._sum((self.opposite, self.other, self.inner)[b]).astype(BF)

        to = (self.inner * 2 + g.core, g.t)
        comm.send(self.group, self.sz[b], self.out[b], self.fin.at[b], to, when=self.end)

    def pass_on(self):
        self.meet()
        for b in range(3):
            self.part(b)

    def relay(self, b):
        g, comm = self.g, self.comm
        if not g.line:
            return
        middle = jnp.logical_not(self.end)
        came = (0, 1, 3)[b]

        @pl.when(middle)
        def _():
            comm.recv(self.sz[came], self.fin.at[came], (g.sib, g.t))
            mine = self._sum((self.opposite, self.other, self.near)[b])
            self.out[b][...] = (mine + self.fin[came].astype(F32)).astype(BF)

        goes = (3, 4, 0)[b]
        to = ((self.other, self.other, self.near)[b] * 2 + g.core, g.t)
        comm.send(self.group, self.sz[goes], self.out[b], self.fin.at[goes], to, when=middle)

    def sent(self):
        self.comm.sent(self.group, self.most, (self.g.sib, self.g.t))

    def total(self):
        g, comm = self.g, self.comm
        mine = self.block(g.d)[...].astype(F32) + self.sib_in[g.chip].astype(F32)
        if not g.line:
            for k in range(1, g.C):
                comm.recv(self.sz[k - 1], self.fin.at[k - 1], (g.zfrom(k), g.t))
                mine = mine + self.fin[k - 1].astype(F32)
            return mine
        middle = jnp.logical_not(self.end)
        comm.recv(self.sz[0], self.fin.at[0], (g.sib, g.t), when=self.end)
        comm.recv(self.sz[2], self.fin.at[2], (g.sib, g.t), when=middle)
        comm.recv(self.sz[4], self.fin.at[4], (g.sib, g.t), when=middle)
        at_end = self.fin[0].astype(F32)
        between = self.fin[2].astype(F32) + self.fin[4].astype(F32)
        return mine + jnp.where(self.end, at_end, between)


def weight_scatter_scratch(g, n, rows, w):
    steps = 5 if g.line else g.C - 1
    return [pltpu.VMEM((n, g.C, rows, w), BF), pltpu.VMEM((n, g.C - 1, rows, w), BF), pltpu.VMEM((n, steps, rows, w), BF)]


def rotated(v, cosine, sine):
    n = v.shape[1]
    if n > cosine.shape[1]:
        cosine = jnp.concatenate([cosine] * (n // cosine.shape[1]), axis=1)
        sine = jnp.concatenate([sine] * (n // sine.shape[1]), axis=1)
    lower = lax.broadcasted_iota(jnp.int32, v.shape, 1) % HD < HD // 2
    swapped = jnp.where(lower, pltpu.roll(v, n - HD // 2, 1), pltpu.roll(v, HD // 2, 1))
    return v * cosine + swapped * sine


def head_lanes(v, h):
    lane = lax.broadcasted_iota(jnp.int32, v.shape, 1)
    keep = (lane >= h * HD) & (lane < (h + 1) * HD)
    return jnp.where(keep, v, jnp.zeros_like(v))


def attend(g, hi, q_blk, keys_rot, values_t, bias, probs, inverse):
    H, R = g.H, g.R
    step = min(512, hi)
    spans = [slice(k, k + step) for k in range(0, hi, step)]
    scores, top, sums, mix = {}, [None] * H, [None] * H, [None] * H

    def fold(v, op):
        return op(v.reshape(v.shape[0] // 8, 8, v.shape[1]), axis=0)

    def first(h, span):
        s = dot(keys_rot[span], head_lanes(q_blk, h), NT) + bias[span]
        scores[h, span.start] = s
        most = fold(s, jnp.max)
        top[h] = most if top[h] is None else jnp.maximum(top[h], most)

    def second(h, span):
        if span.start == 0:
            top[h] = jnp.max(top[h], axis=0, keepdims=True)
        e = jnp.exp(scores.pop((h, span.start)) - top[h])
        some = fold(e, jnp.sum)
        sums[h] = some if sums[h] is None else sums[h] + some
        low = e.astype(BF)
        probs[span, h * R : (h + 1) * R] = low
        out = dot(values_t[h * HD : (h + 1) * HD, span], low)
        mix[h] = out if mix[h] is None else mix[h] + out

    for h in range(H + 1):
        for span in spans:
            if h < H:
                first(h, span)
            if h > 0:
                second(h - 1, span)
    for h in range(H):
        inv = 1.0 / jnp.sum(sums[h], axis=0, keepdims=True)
        inverse[h : h + 1, :] = inv
        mix[h] = mix[h] * inv
    return jnp.concatenate(mix, axis=0)


def attend_back(g, hi, values, keys_t, probs, go, qm, dots, dk, dv):
    H, R = g.H, g.R
    step = 256 if hi < g.S else hi
    grads = [None] * H
    for k in range(0, hi + step, step):
        now, past = slice(k, k + step), slice(k - step, k)
        if k < hi:
            if step < hi:
                dv[now] += dot(probs[now], go[...])
            ahead = [dot(values[now], go[0:R], NT)]
            for h in range(H):
                cols = slice(h * R, (h + 1) * R)
                if h + 1 < H:
                    ahead.append(dot(values[now], go[(h + 1) * R : (h + 2) * R], NT))
                low = (probs[now, cols].astype(F32) * (ahead[h] - dots[h])).astype(BF)
                if h == 0 and step == hi:
                    dv[now] += dot(probs[now], go[...])
                probs[now, cols] = low
                out = dot(keys_t[h * HD : (h + 1) * HD, now], low)
                grads[h] = out if grads[h] is None else grads[h] + out
        if k > 0:
            dk[past] += dot(probs[past], qm[...])
    return jnp.concatenate(grads, axis=0)


def bias_of(qinfo, kinfo, first, size, rows):
    shape = (size, rows)
    doc_q, pic_q = qinfo[0:1, :], qinfo[1:2, :]
    key_doc, pic_k = kinfo[:, 0:1], kinfo[:, 1:2]
    key_pos = lax.broadcasted_iota(jnp.int32, shape, 0)
    query_pos = lax.broadcasted_iota(jnp.int32, shape, 1) + first
    before = key_pos <= query_pos
    open_ = (doc_q == key_doc) & (before | (pic_q == pic_k))
    ok = open_ | (key_pos == query_pos)
    return jnp.where(ok, 0.0, MASKED).astype(F32)


def rotary(length, cols):
    half = HD // 2
    frequency = 10000.0 ** (-2.0 * np.arange(half) / HD)
    angle = np.arange(length)[:, None] * frequency[None, :]
    cosine = np.concatenate([np.cos(angle)] * 2, axis=1)
    sine = np.concatenate([-np.sin(angle), np.sin(angle)], axis=1)
    reps = max(1, min(cols, 128) // HD)
    return (jnp.asarray(np.tile(cosine, (1, reps)), F32), jnp.asarray(np.tile(sine, (1, reps)), F32))


def in_lanes(g):
    return g.Dn % 128 == 0 and g.f <= g.S and (g.C - 1) * g.Dn <= g.f and 2 * g.Dn <= max(g.R, g.c)


def in_slot(g, n_pic, blk):
    per = g.n_t // n_pic

    def run(body):
        for p in range(n_pic):
            pl.when(blk // per == p)(functools.partial(body, p, blk - p * per, (p + 1) * (g.S // n_pic)))

    return run


def layer_body(g, n_pic, x, teacher, valid_mask, documents, starts, wq, wk, wv, wo, wg, wu, wd, cosine, sine,
               o_out, o_in, o_q, o_k, o_v, o_o, o_g, o_u, o_d, o_loss,
               rows1, rows2, gm, ga, wa, wm, qkv, mixed, mixt, turn, wo_t, probs0, probs1, acc2, qm, gom, mids, middle, cot,
               qinfo, kinfo, rinv, cnt, err,
               part, into, out, fin,
               hidden_t, down, sib_d, spare_d, fin_d, sib_m, fin_m, sib_a, out_a, fin_a, output, grad_inputs, dattn, dout, spare_m, stats,
               ts, tr, zs, zr, local):
    g.place()
    g.greet()
    R, S, c, H, C, Dn = g.R, g.S, g.c, g.H, g.C, g.Dn
    tc, zc = Comm(ts, tr), Comm(zs, zr)
    sums = (part, into, out, fin)
    few, ag_group, rs_group = tc.group(), tc.group(), tc.group()
    ag_slots = tc.slots(10 if g.square else g.n_t - 1)
    rs_slots = tc.slots(8 if g.square else g.n_t - 1)
    te = tc.slots(2 if g.square else g.n_t - 1)
    gather = functools.partial(Gather, g, tc, ag_slots, ag_group)
    scatter = functools.partial(Scatter, g, tc, rs_slots, rs_group, sums)
    q, kk, v = qkv.at[0], qkv.at[1], qkv.at[2]
    probs = (probs0, probs1)
    bias, dk, dv = acc2.at[:, :, :R], acc2.at[0, :, :c], acc2.at[1, :, :c]
    packed = in_lanes(g)
    stores = []

    def out_d(k):
        return mids.at[0, 0 : g.f, k * Dn : (k + 1) * Dn] if packed else spare_d.at[k]

    def total_m(j):
        return acc2.at[j % 2, 0 : g.f, j // 2 * Dn : (j // 2 + 1) * Dn] if packed else spare_m.at[j]

    def store(buf, to):
        copy = pltpu.make_async_copy(buf, to, local.at[1 + len(stores)])
        copy.start()
        stores.append(copy)

    get_teacher = pltpu.make_async_copy(teacher, cot, local.at[0])
    get_teacher.start()

    one, _ = normed(x[...])
    rows1[g.rows(g.t)] = one.astype(BF)
    block = g.wrows(g.d)
    wa[0, block] = wq[...]
    wa[1, block] = wk[...]
    wa[2, block] = wv[...]
    g.meet()
    ag = gather(rows1)
    ag.begin(0)
    ag.begin(1)
    za, zo = WeightGather(g, zc, wa, 0, 3), WeightGather(g, zc, wa, 3, 1)
    zg, zd = WeightGather(g, zc, wm, 0, 2), WeightGather(g, zc, wm, 2, 1)
    za.far()
    wa[3, block] = turned(wo[...])
    zo.far()
    za.near()
    wm[0, block] = turned(wg[...])
    wm[1, block] = turned(wu[...])
    wm[2, block] = turned(wd[...])

    csib, cz = zc.slots(1)[0], zc.slots(C - 1)
    gsib, gz = zc.group(), zc.group()
    valid, doc = valid_mask[...], documents[...]
    cnt[0] = jnp.broadcast_to(jnp.sum(valid.astype(F32), axis=1, keepdims=True), (8, 128))
    zc.send(gsib, csib, cnt.at[0], cnt.at[1], (g.sib, g.t))
    at = lax.broadcasted_iota(jnp.int32, (1, S), 1)
    pic = jnp.zeros((1, S), jnp.int32)
    for p in range(n_pic):
        first = starts[0:1, p : p + 1]
        pic = jnp.where((at >= first) & (at < first + PIECE), p + 1, pic)
    qinfo[0:1] = doc
    qinfo[1:2] = pic
    as_keys = [jnp.where(valid == 1, doc, -1), jnp.where(pic > 0, pic, -1), valid]
    as_keys = jnp.concatenate([a.astype(F32) for a in as_keys] + [jnp.zeros((125, S), F32)], axis=0)
    kinfo[...] = as_keys.T.astype(jnp.int32)
    zc.recv(csib, cnt.at[1], (g.sib, g.t))
    cnt[2] = cnt[0] + cnt[1]
    for k in range(1, C):
        zc.send(gz, cz[k - 1], cnt.at[2], cnt.at[2 + k], (g.zto(k), g.t))

    def set_bias(i, blk):
        @in_slot(g, n_pic, blk)
        def _(p, index, hi):
            bias[i % 2, 0:hi] = bias_of(qinfo[:, g.rows(blk)], kinfo[0:hi], blk * R, hi, R)

    set_bias(0, g.leave[0])

    ag.relay()
    za.relay()
    zo.relay()
    zo.near()
    za.pass_on()
    za.wait()
    zg.far()
    zg.near()
    for i, blk in enumerate(ag.order):
        ag.wait(i)
        at = g.rows(blk)
        row = rows1[at]
        cos_b, sin_b = cosine[at], sine[at]
        q[at] = (rotated(dot(row, wa[0]), cos_b, sin_b) * HD**-0.5).astype(BF)
        kk[at] = rotated(dot(row, wa[1]), cos_b, sin_b).astype(BF)
        v[at] = dot(row, wa[2]).astype(BF)
    zo.pass_on()
    turn[...] = turned(v[...])

    rs = scatter()
    @pl.loop(0, g.n_t)
    def _(i):
        blk = g.leave_at(i)
        at = g.rows(blk)

        @pl.when(i > 0)
        def _():
            set_bias(i, blk)

        @in_slot(g, n_pic, blk)
        def _(p, index, hi):
            both = attend(g, hi, q[at], kk, turn, bias.at[i % 2], probs[p].at[index], rinv.at[blk])
            mixt[blk] = both.astype(BF)
            mixed[at] = both.T.astype(BF)

        pl.when(i == 0)(zo.wait)

        @pl.when(i == 2)
        def _():
            zg.relay()
            zd.far()
            zd.near()

        @pl.when(i < g.n_t - 1)
        def _():
            rs.give(i, dot(mixed[at], wa[3], NT))

    rs.relay()
    middle[0:R] = x[...] + dot(mixed[g.rows(g.t)], wa[3], NT)
    ag.sent()
    ag = gather(rows2, far_first=True)

    for i in range(2):
        for rows, summed in rs.take(i, middle):
            middle[rows] = summed
            two, _ = normed(summed)
            rows2[g.rows(g.t, rows.start, R // 4)] = two.astype(BF)
        ag.begin(i)
    rs = scatter()
    zd.relay()
    ag.relay()
    zg.pass_on()
    zg.wait()

    @pl.loop(0, g.n_t)
    def _(i):
        for k in range(1, g.n_t):
            pl.when(i == k)(functools.partial(ag.wait, k))
        at = g.rows(g.far_at(i))
        row = rows2[at]
        gate, up = dot(row, wm[0]), dot(row, wm[1])
        sig = jax.nn.sigmoid(gate)
        act = gate * sig
        mids[0, at] = (act * up).astype(BF)
        mids[2, at] = act.astype(BF)
        mids[1, at] = (up * sig * (1.0 + gate * (1.0 - sig))).astype(BF)

        @pl.when(i == 1)
        def _():
            zd.pass_on()
            zd.wait()

        @pl.when(i > 0)
        def _():
            rs.give(g.far_lead(i), dot(mids[0, at], wm[2], NT))

    output[...] = middle[0:R] + dot(mids[0, g.rows(g.t)], wm[2], NT)
    wo_t[...] = turned(wa[3])
    rs.relay()
    hidden_t[...] = turned(mids[0])

    get_teacher.wait()
    tokens = cnt[2]
    for k in range(1, C):
        zc.recv(cz[k - 1], cnt.at[2 + k], (g.zfrom(k), g.t))
        tokens = tokens + cnt[2 + k]
    share = 1.0 * S * g.n_dp / tokens[0:1, 0:1]
    ag.sent()
    ag = gather(gm, far_first=True)
    errors = jnp.zeros((R // 4, 1), F32)
    for i in range(2):
        for rows, summed in rs.take(i, output):
            output[rows] = summed
            dev = summed - cot[rows]
            kept = kinfo[g.rows(g.t, rows.start, R // 4), 2:3].astype(F32) * dev
            cotangent = kept * share
            cot[rows] = cotangent
            gm[g.rows(g.t, rows.start, R // 4)] = cotangent.astype(BF)
            errors += jnp.sum(kept * dev, axis=1, keepdims=True)
        ag.begin(i)
    store(output, o_out)
    err[0] = jnp.broadcast_to(jnp.sum(errors, axis=0, keepdims=True), (8, 128))

    rs = scatter()
    if g.square:
        tc.send(few, te[0], err.at[0], err.at[1], (g.d, g.tx))
    else:
        for k, peer in enumerate(g.to):
            tc.send(few, te[k], err.at[0], err.at[1 + k], (g.d, peer))

    zscat = [WeightScatter(g, zc, lambda d: down.at[d], down.at[0 : 2 * C - 1],
                           (sib_d.at[0], [out_d(k) for k in range(C - 1)], fin_d.at[0]))]

    @pl.loop(0, g.n_t)
    def _(i):
        for k in range(1, g.n_t):
            pl.when(i == k)(functools.partial(ag.wait, k))
        at = g.rows(g.far_at(i))
        gh = dot(gm[at], wm[2])
        mids[1, at] = (gh * mids[1, at].astype(F32)).astype(BF)
        mids[2, at] = (gh * mids[2, at].astype(F32)).astype(BF)

        @pl.when(i == 0)
        def _():
            ag.relay()
            rows2[...] = turned(rows2[...])
            turn[...] = turned(kk[...])

        @pl.when(i > 0)
        def _():
            rs.give(g.far_lead(i), dot(mids[1, at], wm[0], NT) + dot(mids[2, at], wm[1], NT))

    wide = max(256, Dn)

    @pl.loop(0, g.D // wide)
    def _(k):
        some = dot(hidden_t[...], gm[:, pl.ds(pl.multiple_of(k * wide, wide), wide)]).astype(BF)
        for n in range(wide // Dn):
            down[k * (wide // Dn) + n] = some[:, n * Dn : (n + 1) * Dn]

    zscat[0].start()
    rs.relay()
    at = g.rows(g.t)
    grad_inputs[...] = dot(mids[1, at], wm[0], NT) + dot(mids[2, at], wm[1], NT)
    zscat[0].pass_on()
    zg.sent()
    zd.sent()
    for j in range(2):
        wm[j] = dot(rows2[...], mids[1 + j]).astype(BF)
        spare = [mids.at[1 + j, k * Dn : (k + 1) * Dn] for k in range(C - 1)]
        zscat.append(WeightScatter(g, zc, lambda d, j=j: wm.at[j, g.wrows(d)], wm.at[j, 0 : (2 * C - 1) * Dn],
                                   (sib_m.at[j], spare, fin_m.at[j])))
        zscat[-1].start()
    zscat[1].pass_on()
    two, inv = normed(middle[0:R])
    ag.sent()
    ag = gather(ga)
    for i in range(2):
        for rows, back in rs.take(i, grad_inputs):
            grad_middle = cot[rows] + normed_back(two[rows], inv[rows], back)
            cot[rows] = grad_middle
            ga[g.rows(g.t, rows.start, R // 4)] = grad_middle.astype(BF)
        ag.begin(i)

    for j in (3, 0, 1, 2):
        spare = [out_a.at[j, k] for k in range(C - 1)]
        zscat.append(WeightScatter(g, zc, lambda d, j=j: wa.at[j, g.wrows(d)], wa.at[j, 0 : (2 * C - 1) * Dn],
                                   (sib_a.at[j], spare, fin_a.at[j])))

    rs = scatter()
    zscat[2].pass_on()
    zscat[0].relay(0)
    zscat[0].relay(1)
    base = 4 if g.square else g.n_t
    ec, ez = zc.slots(1)[0], zc.slots(C - 1)
    gec, gez = zc.group(), zc.group()
    if g.square:
        tc.recv(te[0], err.at[1], (g.d, g.tx))
        err[2] = err[0] + err[1]
        tc.send(few, te[1], err.at[2], err.at[3], (g.d, g.ty))
    acc2[...] = jnp.zeros_like(acc2)
    middle[0:c] = jnp.zeros((c, g.D), F32)

    @pl.loop(0, g.n_t)
    def _(i):
        @pl.when(i == 1)
        def _():
            zscat[0].relay(2)
            rows1[...] = turned(rows1[...])
            if g.square:
                tc.recv(te[1], err.at[3], (g.d, g.ty))
                err[base] = err[2] + err[3]
            else:
                total = err[0]
                for k in range(1, g.n_t):
                    tc.recv(te[k - 1], err.at[k], (g.d, (g.t + g.n_t - k) % g.n_t))
                    total = total + err[k]
                err[base] = total
            zc.send(gec, ec, err.at[base], err.at[base + 1], (g.sib, g.t))

        @pl.when(i == 2)
        def _():
            zc.recv(ec, err.at[base + 1], (g.sib, g.t))
            err[base + 2] = err[base] + err[base + 1]
            for k in range(1, C):
                zc.send(gez, ez[k - 1], err.at[base + 2], err.at[base + 2 + k], (g.zto(k), g.t))

        for k in range(1, g.n_t):
            pl.when(i == k)(functools.partial(ag.wait, k))
        blk = g.arrive_at(i)
        at = g.rows(blk)
        middle[0:c] += dot(mixt[blk], ga[at])

        @pl.when(i == g.n_t - 1)
        def _():
            zo.sent()
            wa[3] = turned(middle[0:c].astype(BF))
            zscat[3].start()

        go_t = dot(wo_t[...], ga[at], NT).astype(BF).astype(F32)
        mix_t = mixt[blk].astype(F32)
        scaled, dots = [], []
        for h in range(H):
            one_head = go_t[h * HD : (h + 1) * HD] * rinv[blk, h : h + 1, :]
            scaled.append(one_head)
            dots.append(jnp.sum(one_head * mix_t[h * HD : (h + 1) * HD], axis=0, keepdims=True))
        go = jnp.concatenate(scaled, axis=0).T.astype(BF)
        q_blk = q[at]
        for h in range(H):
            gom[h * R : (h + 1) * R] = head_lanes(go, h)
            qm[h * R : (h + 1) * R] = head_lanes(q_blk, h)

        @in_slot(g, n_pic, blk)
        def _(p, index, hi):
            dq = attend_back(g, hi, v, turn, probs[p].at[index], gom, qm, dots, dk, dv).T * HD**-0.5
            q[at] = rotated(dq, cosine[at], -sine[at]).astype(BF)

        pl.when(i == 0)(ag.relay)

        @pl.when(i == 2)
        def _():
            zscat[1].relay(0)
            zscat[1].relay(1)

    @pl.loop(0, g.n_t)
    def _(i):
        at = g.rows(g.leave_at(i))
        kk[at] = rotated(dk[at], cosine[at], -sine[at]).astype(BF)
        v[at] = dv[at].astype(BF)
        partial = dot(q[at], wa[0], NT) + dot(kk[at], wa[1], NT) + dot(v[at], wa[2], NT)

        @pl.when(i < g.n_t - 1)
        def _():
            rs.give(i, partial)

        @pl.when(i == g.n_t - 1)
        def _():
            grad_inputs[...] = partial


    zscat[3].pass_on()
    zscat[1].relay(2)
    zscat[2].relay(0)
    zscat[2].relay(1)
    za.sent()
    for j in range(3):
        wa[j] = dot(rows1[...], qkv[j]).astype(BF)
        zscat[4 + j].start()
    for j in (4, 5, 6):
        zscat[j].meet()
        zscat[j].part(0)
    rs.relay()
    for k in (1, 2):
        for j in (4, 5, 6):
            zscat[j].part(k)
    zscat[2].relay(2)
    zscat[3].relay(0)
    zscat[3].relay(1)
    one, inv = normed(x[...])

    for j, to in enumerate((o_d, o_g, o_u)):
        total_m(j)[...] = zscat[j].total().T if j else zscat[j].total()
        store(total_m(j), to)
    for j in (4, 5, 6):
        zscat[j].relay(0)
    zscat[3].relay(2)
    for j, k in ((4, 2), (5, 2), (4, 1), (6, 2), (5, 1)):
        zscat[j].relay(k)
    for i in range(2):
        for rows, back in rs.take(i, grad_inputs):
            grad_inputs[rows] = cot[rows] + normed_back(one[rows], inv[rows], back)
    store(grad_inputs, o_in)
    zscat[6].relay(1)
    dout_at = acc2.at[1, 0:c, Dn : 2 * Dn] if packed else dout
    dout_at[...] = zscat[3].total().T
    store(dout_at, o_o)
    total = err[base + 2]
    for k in range(1, C):
        zc.recv(ez[k - 1], err.at[base + 2 + k], (g.zfrom(k), g.t))
        total = total + err[base + 2 + k]
    stats[...] = (total * (1.0 / g.D) / tokens)[0:1, 0:1]
    store(stats, o_loss)
    for j, to in enumerate((o_q, o_k, o_v)):
        dattn[j] = zscat[4 + j].total()
        store(dattn.at[j], to)
    for copy in stores:
        copy.wait()
    ag.sent()
    for scat in zscat:
        scat.sent()
    tc.sent(few, err.at[0 : len(te)], (g.sib, g.t))
    for group, n in ((gsib, 1), (gz, C - 1), (gec, 1), (gez, C - 1)):
        zc.sent(group, cnt.at[0:n], (g.sib, g.t))
    assert tc.n <= tr.shape[0] and zc.n <= zr.shape[0] and tc.groups <= ts.shape[0] and zc.groups <= zs.shape[0]


def layer(g, n_pic, args):
    S, R, D, c, f, H, C, Dn = g.S, g.R, g.D, g.c, g.f, g.H, g.C, g.Dn
    sds, V = jax.ShapeDtypeStruct, pltpu.VMEM
    shapes = [(R, D), (R, D), (Dn, c), (Dn, c), (Dn, c), (c, Dn), (f, Dn), (f, Dn), (f, Dn), (1, 1)]
    outs = [sds(s, F32) for s in shapes]
    base = 4 if g.square else g.n_t
    scratch = [V((S, D), BF)] * 4 + [
        V((4, D, c), BF), V((3, D, f), BF), V((3, S, c), BF), V((S, c), BF), V((g.n_t, c, R), BF), V((c, S), BF), V((c, D), BF),
        V((g.n_t // 2, S // 2, H * R), BF), V((g.n_t // 2, S, H * R), BF), V((2, S, max(R, c)), F32), V((H * R, c), BF), V((H * R, c), BF), V((3, S, f), BF),
        V((max(R, c), D), F32), V((R, D), F32), V((8, S), jnp.int32), V((S, 128), jnp.int32), V((g.n_t, 8, R), F32),
        V((2 + C, 8, 128), F32), V((base + 2 + C, 8, 128), F32),
    ]
    scratch += scatter_scratch(g)
    m = weight_scatter_scratch(g, 2, Dn, f)
    d = weight_scatter_scratch(g, 1, f, Dn)
    few = V((1, 16, 128), BF)
    scratch += [V((f, S), BF), V((g.n_dp, f, Dn), BF), d[0], few if in_lanes(g) else V((C - 1, f, Dn), BF), d[2]]
    scratch += [m[0], m[2]] + weight_scatter_scratch(g, 4, Dn, c)
    scratch += [V((R, D), F32), V((R, D), F32), V((3, Dn, c), F32), few if in_lanes(g) else V((c, Dn), F32), few if in_lanes(g) else V((3, f, Dn), F32), V((1, 1), F32)]
    nt = 20 if g.square else 3 * (g.n_t - 1)
    nz = 4 * (2 * C - 1) + 7 * (6 if g.line else C) + 2 * C
    sem = pltpu.SemaphoreType.DMA
    scratch += [sem((3,)), sem((nt,)), sem((15,)), sem((nz,)), sem((11,))]
    whole = pl.BlockSpec(memory_space=pltpu.VMEM)
    specs = [whole] * len(args)
    specs[1] = pl.BlockSpec(memory_space=pl.ANY)
    return pl.pallas_call(
        functools.partial(layer_body, g, n_pic),
        name="layer",
        out_shape=outs,
        in_specs=specs,
        out_specs=[pl.BlockSpec(memory_space=pl.ANY)] * len(outs),
        scratch_shapes=scratch,
        compiler_params=pltpu.CompilerParams(collective_id=1, has_side_effects=True, vmem_limit_bytes=VMEM_BYTES),
    )(*args)


def finish_body(n, *refs):
    parts, outs, bufs, come, go = refs[:n], refs[n : 2 * n], refs[2 * n : 3 * n], refs[3 * n], refs[3 * n + 1]
    loads = [pltpu.make_async_copy(a, b, come.at[k]) for k, (a, b) in enumerate(zip(parts, bufs))]
    stores = [pltpu.make_async_copy(a, b, go.at[k]) for k, (a, b) in enumerate(zip(bufs, outs))]
    for copy in loads:
        copy.start()
    for load, store in zip(loads, stores):
        load.wait()
        store.start()
    for copy in stores:
        copy.wait()


def finish(parts):
    anywhere, n = pl.BlockSpec(memory_space=pl.ANY), len(parts)
    return pl.pallas_call(
        functools.partial(finish_body, n),
        name="finish",
        out_shape=[jax.ShapeDtypeStruct(p.shape, F32) for p in parts],
        in_specs=[anywhere] * n,
        out_specs=[anywhere] * n,
        scratch_shapes=[pltpu.VMEM(p.shape, F32) for p in parts] + [pltpu.SemaphoreType.DMA((n,))] * 2,
    )(*parts)


def per_device(n_dp, n_t, inputs, teacher, valid_mask, documents, picture_starts,
               w_query, w_key, w_value, w_out, w_gate, w_up, w_down):
    R, D = inputs.shape
    c, f = w_query.shape[1], w_gate.shape[1]
    g = Geo(n_dp, n_t, R, D, c, f)
    args = (inputs, teacher, valid_mask, documents, picture_starts, w_query, w_key, w_value, w_out, w_gate.T, w_up.T, w_down)
    parts = layer(g, picture_starts.shape[1], (*args, *rotary(g.S, c)))
    out, *grads, gate, up, down, loss = finish(parts)
    return (out, loss.reshape(()), *grads, gate.T, up.T, down)


def solution(mesh):
    rows, pair = P(("dp", "tensor"), None), P("dp", None)
    cut, across = P("dp", "tensor"), P("tensor", "dp")
    return jax.shard_map(
        functools.partial(per_device, mesh.shape["dp"], mesh.shape["tensor"]),
        mesh=mesh,
        in_specs=(rows, rows, pair, pair, pair, cut, cut, cut, across, cut, cut, across),
        out_specs=(rows, P(), rows, cut, cut, cut, across, cut, cut, across),
        check_vma=False,
    )
```

```python
import functools

import jax
import jax.numpy as jnp
import numpy as np
from jax import lax
from jax.experimental import pallas as pl
from jax.experimental.pallas import tpu as pltpu
from jax.sharding import PartitionSpec as P

MESH = pl.DeviceIdType.MESH
HD = 64
PIECE = 256
EPS = 1e-5
MASKED = -1e30
VMEM_BYTES = 60 * 2**20
BF = jnp.bfloat16
F32 = jnp.float32
NT = (((1,), (1,)), ((), ()))
NN = (((1,), (0,)), ((), ()))


def dot(a, b, dims=NN):
    return lax.dot_general(a, b, dims, preferred_element_type=F32)


def eye(n):
    return (
        lax.broadcasted_iota(jnp.int32, (n, n), 0) == lax.broadcasted_iota(jnp.int32, (n, n), 1)
    ).astype(F32).astype(BF)


def turned(a):
    n = a.shape[1]
    step = min(n, 256)
    parts = [dot(eye(min(step, n - k)), a[:, k : k + step], NT).astype(BF) for k in range(0, n, step)]
    return parts[0] if len(parts) == 1 else jnp.concatenate(parts, axis=0)


def mean_of(v):
    return jnp.sum(v, axis=1, keepdims=True) * (1.0 / v.shape[1])


def normed(v):
    centred = v - mean_of(v)
    inv = lax.rsqrt(mean_of(centred * centred) + EPS)
    return centred * inv, inv


def normed_back(n, inv, g):
    return inv * (g - mean_of(g) - n * mean_of(g * n))


class Geo:
    def __init__(self, n_dp, n_t, tok_rows, d_model, cols, hid):
        self.n_dp, self.n_t, self.R, self.D, self.c, self.f = n_dp, n_t, tok_rows, d_model, cols, hid
        self.C = n_dp // 2
        self.S = tok_rows * n_t
        self.H = cols // HD
        self.Dn = d_model // n_dp
        self.square = n_t == 4
        self.line = self.C == 4

    def place(self):
        self.d = lax.axis_index("dp")
        self.t = lax.axis_index("tensor")
        self.chip = self.d // 2
        self.core = self.d % 2
        if self.square:
            self.tx = self.t + 1 - 2 * (self.t % 2)
            self.ty = (self.t + 2) % 4
            self.td = 3 - self.t
            self.to = [self.tx, self.ty]
            self.leave = [self.td, self.tx, self.ty, self.t]
        else:
            n = self.n_t
            self.to = [(self.t + k) % n for k in range(1, n)]
            self.leave = [(self.t + k) % n for k in range(1, n)] + [self.t]
        self.sib = self.d + 1 - 2 * self.core
        return self

    def leave_at(self, i):
        if self.square:
            return 2 * ((self.t // 2 + i + 1) % 2) + (self.t % 2 + 1 - i // 2) % 2
        return (self.t + 1 + i) % self.n_t

    def arrive_at(self, i):
        if self.square:
            return 2 * ((self.t // 2 + i // 2) % 2) + (self.t % 2 + i % 2) % 2
        return (self.t + self.n_t - i) % self.n_t

    def far_at(self, i):
        if self.square:
            return 2 * ((self.t // 2 + i % 2) % 2) + (self.t % 2 + (i + 1) // 2) % 2
        return (self.t + self.n_t - i) % self.n_t

    def far_lead(self, i):
        return i - 1 if self.square else self.n_t - 1 - i

    def zto(self, k):
        return ((self.chip + k) % self.C) * 2 + self.core

    def zfrom(self, k):
        return ((self.chip + self.C - k) % self.C) * 2 + self.core

    def rows(self, blk, first=0, count=None):
        count = self.R if count is None else count
        return pl.ds(pl.multiple_of(blk * self.R + first, count), count)

    def wrows(self, d):
        return pl.ds(pl.multiple_of(d * self.Dn, self.Dn), self.Dn)

    def greet(self):
        bar = pltpu.get_barrier_semaphore()
        out = [(self.d, p) for p in self.to]
        out += [(self.zto(k), self.t) for k in range(1, self.C)] + [(self.sib, self.t)]
        for dev in out:
            pl.semaphore_signal(bar, inc=1, device_id=dev, device_id_type=MESH)
        self.met = len(out)

    def meet(self):
        pl.semaphore_wait(pltpu.get_barrier_semaphore(), self.met)


class Comm:
    def __init__(self, send_sem, recv_sem):
        self.ss, self.rs = send_sem, recv_sem
        self.n = self.groups = 0

    def slots(self, k):
        self.n += k
        return list(range(self.n - k, self.n))

    def group(self):
        self.groups += 1
        return self.groups - 1

    def _copy(self, group, slot, src, dst, dev):
        return pltpu.make_async_remote_copy(
            src_ref=src, dst_ref=dst, send_sem=self.ss.at[group], recv_sem=self.rs.at[slot], device_id=dev, device_id_type=MESH
        )

    def send(self, group, slot, src, dst, dev, when=None):
        copy = self._copy(group, slot, src, dst, dev)
        if when is None:
            copy.start()
        else:
            pl.when(when)(copy.start)

    def recv(self, slot, dst, dev, when=None):
        copy = self._copy(0, slot, dst, dst, dev)
        if when is None:
            copy.wait_recv()
        else:
            pl.when(when)(copy.wait_recv)

    def sent(self, group, like, dev, when=None):
        copy = self._copy(group, 0, like, like, dev)
        if when is None:
            copy.wait_send()
        else:
            pl.when(when)(copy.wait_send)


class Gather:
    def __init__(self, geo, comm, slots, group, buf, far_first=False):
        self.g, self.comm, self.buf, self.group = geo, comm, buf, group
        g = geo
        self.far_first = far_first and g.square
        if not g.square:
            self.s = slots
            self.order = [(g.t + g.n_t - k) % g.n_t for k in range(g.n_t)]
            self.lead = [g.n_t - 1] + [g.n_t - 1 - k for k in range(1, g.n_t)]
            return
        self.sx, self.sy = slots[:5], slots[5:]
        if self.far_first:
            self.order, self.lead = [g.t, g.td, g.tx, g.ty], [3, 0, 1, 2]
        else:
            self.order, self.lead = [g.t, g.tx, g.ty, g.td], [3, 1, 2, 0]

    def begin(self, i):
        g, comm = self.g, self.comm
        if g.square:
            self._give(self.sx[i], g.t, i, 1, g.tx)
            self._give(self.sy[i], g.t, 2 + i, 1, g.ty)
            if i == 1 and not self.far_first:
                self._rest()
        elif i == 1:
            own = self.buf.at[g.rows(g.t)]
            for k, peer in enumerate(g.to):
                comm.send(self.group, self.s[k], own, own, (g.d, peer))

    def sent(self):
        self.comm.sent(self.group, self.buf.at[0 : (self.g.n_t - 1) * self.g.R], (self.g.d, self.g.to[0]))

    def piece(self, blk, first, count):
        q = self.g.R // 4
        rows = pl.ds(pl.multiple_of(blk * self.g.R + first * q, q), count * q)
        return self.buf.at[rows]

    def _give(self, slot, blk, first, count, to):
        part = self.piece(blk, first, count)
        self.comm.send(self.group, slot, part, part, (self.g.d, to))

    def _rest(self):
        g = self.g
        self._give(self.sx[4], g.t, 2, 2, g.tx)
        self._give(self.sy[4], g.t, 0, 2, g.ty)

    def relay(self):
        g, comm = self.g, self.comm
        if not g.square:
            return
        for i in range(2):
            comm.recv(self.sx[i], self.piece(g.tx, i, 1), (g.d, g.tx))
            self._give(self.sy[2 + i], g.tx, i, 1, g.ty)
            comm.recv(self.sy[i], self.piece(g.ty, 2 + i, 1), (g.d, g.ty))
            self._give(self.sx[2 + i], g.ty, 2 + i, 1, g.tx)
        if self.far_first:
            self._rest()

    def wait(self, i):
        g, comm = self.g, self.comm
        if i == 0:
            return
        if not g.square:
            comm.recv(self.s[i - 1], self.buf.at[g.rows(self.order[i])], (g.d, self.order[i]))
            return
        which = "dxy"[i - 1] if self.far_first else "xyd"[i - 1]
        if which == "x":
            comm.recv(self.sx[4], self.piece(g.tx, 2, 2), (g.d, g.tx))
        elif which == "y":
            comm.recv(self.sy[4], self.piece(g.ty, 0, 2), (g.d, g.ty))
        else:
            for k in range(2):
                comm.recv(self.sx[2 + k], self.piece(g.td, 2 + k, 1), (g.d, g.tx))
                comm.recv(self.sy[2 + k], self.piece(g.td, k, 1), (g.d, g.ty))


def scatter_scratch(g):
    h = g.R // 2
    if g.square:
        return [pltpu.VMEM((3, 2, h, g.D), BF), pltpu.VMEM((2, h, g.D), BF), pltpu.VMEM((2, h, g.D), BF), pltpu.VMEM((2, 2, h, g.D), BF)]
    return [pltpu.VMEM((g.n_t - 1, 2, h, g.D), BF), pltpu.VMEM((1, 16, 128), BF), pltpu.VMEM((1, 16, 128), BF), pltpu.VMEM((g.n_t - 1, 2, h, g.D), BF)]


class Scatter:
    def __init__(self, geo, comm, slots, group, bufs):
        self.g, self.comm, self.group = geo, comm, group
        self.part, self.into, self.out, self.fin = bufs
        g = geo
        if g.square:
            self.sx, self.sy = slots[:4], slots[4:]
        else:
            self.s = slots

    def give(self, i, value):
        h = self.g.R // 2
        for j in range(2):
            self.part[i, j] = value[j * h : (j + 1) * h].astype(BF)
        if isinstance(i, int):
            self.send(i)
        else:
            for k in range(self.g.n_t - 1):
                pl.when(i == k)(functools.partial(self.send, k))

    def send(self, i):
        g, comm = self.g, self.comm
        if not g.square:
            comm.send(self.group, self.s[i], self.part.at[i], self.fin.at[i], (g.d, g.leave[i]))
        elif i == 0:
            comm.send(self.group, self.sx[0], self.part.at[0, 0], self.into.at[0], (g.d, g.tx))
            comm.send(self.group, self.sy[0], self.part.at[0, 1], self.into.at[1], (g.d, g.ty))
        elif i == 1:
            comm.send(self.group, self.sx[1], self.part.at[1, 0], self.fin.at[0, 0], (g.d, g.tx))
        else:
            comm.send(self.group, self.sy[1], self.part.at[2, 1], self.fin.at[1, 1], (g.d, g.ty))

    def relay(self):
        g, comm = self.g, self.comm
        if not g.square:
            return
        q = g.R // 4
        comm.recv(self.sx[0], self.into.at[0], (g.d, g.tx))
        comm.recv(self.sy[0], self.into.at[1], (g.d, g.ty))
        for k in range(2):
            rows = slice(k * q, (k + 1) * q)
            for a, mine, slots, to in ((0, (2, 0), self.sy, g.ty), (1, (1, 1), self.sx, g.tx)):
                self.out[a, rows] = (self.into[a, rows].astype(F32) + self.part[(*mine, rows)].astype(F32)).astype(BF)
                comm.send(self.group, slots[2 + k], self.out.at[a, rows], self.fin.at[1 - a, a, rows], (g.d, to))

    def take(self, i, own):
        g, comm = self.g, self.comm
        q = g.R // 4
        count = 2 if g.square else g.n_t - 1
        inner = slice(i * q, (i + 1) * q)
        if g.square:
            if i == 0:
                comm.recv(self.sx[1], self.fin.at[0, 0], (g.d, g.tx))
                comm.recv(self.sy[1], self.fin.at[1, 1], (g.d, g.ty))
            comm.recv(self.sx[2 + i], self.fin.at[0, 1, inner], (g.d, g.tx))
            comm.recv(self.sy[2 + i], self.fin.at[1, 0, inner], (g.d, g.ty))
        elif i == 0:
            for k in range(count):
                comm.recv(self.s[k], self.fin.at[k], (g.d, (g.t + g.n_t - k - 1) % g.n_t))
        pairs = []
        for j in range(2):
            rows = slice(2 * j * q + i * q, 2 * j * q + (i + 1) * q)
            v = own[rows]
            for k in range(count):
                v = v + self.fin[k, j, inner].astype(F32)
            pairs.append((rows, v))
        if i == 1:
            comm.sent(self.group, self.part, (g.d, g.to[0]))
        return pairs


class WeightGather:
    def __init__(self, geo, comm, buf, first, n):
        self.g, self.comm, self.buf, self.of = geo, comm, buf, pl.ds(first, n)
        g = geo
        self.group = comm.group()
        self.inner = (g.chip == 1) | (g.chip == 2)
        self.sz, self.sc = comm.slots(g.C - 1), comm.slots(g.C)

    def at(self, d):
        return self.buf.at[self.of, self.g.wrows(d)]

    def far(self):
        g, comm = self.g, self.comm
        if g.line:
            comm.send(self.group, self.sz[1], self.at(g.d), self.at(g.d), (g.zto(2), g.t))

    def near(self):
        g, comm = self.g, self.comm
        own = self.at(g.d)
        for k in range(1, g.C):
            if g.line and k == 2:
                continue
            near = g.chip != (0 if k == 3 else 3) if g.line else None
            comm.send(self.group, self.sz[k - 1], own, own, (g.zto(k), g.t), when=near)
        comm.send(self.group, self.sc[0], own, own, (g.sib, g.t))

    def _take(self, k, when=None):
        g, comm = self.g, self.comm
        block = self.at(g.zfrom(k))
        comm.recv(self.sz[k - 1], block, (g.zfrom(k), g.t), when=when)
        comm.send(self.group, self.sc[k], block, block, (g.sib, g.t), when=when)

    def relay(self):
        g, comm = self.g, self.comm
        if not g.line:
            return
        self._take(2, self.inner)
        block = self.at(g.zfrom(2))
        comm.send(self.group, self.sz[2], block, block, (6 + g.core, g.t), when=g.chip == 2)
        comm.send(self.group, self.sz[0], block, block, (g.core, g.t), when=g.chip == 1)

    def pass_on(self):
        g = self.g
        for k in range(1, g.C):
            self._take(k, jnp.logical_not(self.inner) if g.line and k == 2 else None)

    def wait(self):
        g, comm = self.g, self.comm
        for k in range(g.C):
            other = g.zfrom(k) + 1 - 2 * g.core
            comm.recv(self.sc[k], self.at(other), (g.sib, g.t))

    def sent(self):
        g, comm = self.g, self.comm

        def some(n, when=None):
            comm.sent(self.group, self.buf.at[self.of, 0 : n * g.Dn], (g.sib, g.t), when)

        if g.line:
            some(8, self.inner)
            some(6, jnp.logical_not(self.inner))
        else:
            some(2 * g.C - 1)


class WeightScatter:
    def __init__(self, geo, comm, block, most, bufs):
        self.g, self.comm, self.block, self.most = geo, comm, block, most
        self.sib_in, self.out, self.fin = bufs
        g = geo
        self.group = comm.group()
        self.sc, self.sz = comm.slots(1)[0], comm.slots(5 if g.line else g.C - 1)
        half = g.chip // 2
        self.near, self.inner, self.other, self.opposite = 3 * half, 1 + half, 2 - half, 3 - 3 * half
        self.end = (g.chip == 0) | (g.chip == 3)

    def start(self):
        g, comm = self.g, self.comm
        for j in range(g.C):
            comm.send(self.group, self.sc, self.block(2 * j + 1 - g.core), self.sib_in.at[j], (g.sib, g.t))

    def _sum(self, chip):
        return self.block(2 * chip + self.g.core)[...].astype(F32) + self.sib_in[chip].astype(F32)

    def meet(self):
        g, comm = self.g, self.comm
        comm.recv(self.sc, self.sib_in, (g.sib, g.t))

    def part(self, b):
        g, comm = self.g, self.comm
        if not g.line:
            for k in range(1, g.C) if b == 0 else ():
                self.out[k - 1][...] = self._sum((g.chip + k) % g.C).astype(BF)
                comm.send(self.group, self.sz[k - 1], self.out[k - 1], self.fin.at[k - 1], (g.zto(k), g.t))
            return

        @pl.when(self.end)
        def _():
            self.out[b][...] = self._sum((self.opposite, self.other, self.inner)[b]).astype(BF)

        to = (self.inner * 2 + g.core, g.t)
        comm.send(self.group, self.sz[b], self.out[b], self.fin.at[b], to, when=self.end)

    def pass_on(self):
        self.meet()
        for b in range(3):
            self.part(b)

    def relay(self, b):
        g, comm = self.g, self.comm
        if not g.line:
            return
        middle = jnp.logical_not(self.end)
        came = (0, 1, 3)[b]

        @pl.when(middle)
        def _():
            comm.recv(self.sz[came], self.fin.at[came], (g.sib, g.t))
            mine = self._sum((self.opposite, self.other, self.near)[b])
            self.out[b][...] = (mine + self.fin[came].astype(F32)).astype(BF)

        goes = (3, 4, 0)[b]
        to = ((self.other, self.other, self.near)[b] * 2 + g.core, g.t)
        comm.send(self.group, self.sz[goes], self.out[b], self.fin.at[goes], to, when=middle)

    def sent(self):
        self.comm.sent(self.group, self.most, (self.g.sib, self.g.t))

    def total(self):
        g, comm = self.g, self.comm
        mine = self.block(g.d)[...].astype(F32) + self.sib_in[g.chip].astype(F32)
        if not g.line:
            for k in range(1, g.C):
                comm.recv(self.sz[k - 1], self.fin.at[k - 1], (g.zfrom(k), g.t))
                mine = mine + self.fin[k - 1].astype(F32)
            return mine
        middle = jnp.logical_not(self.end)
        comm.recv(self.sz[0], self.fin.at[0], (g.sib, g.t), when=self.end)
        comm.recv(self.sz[2], self.fin.at[2], (g.sib, g.t), when=middle)
        comm.recv(self.sz[4], self.fin.at[4], (g.sib, g.t), when=middle)
        at_end = self.fin[0].astype(F32)
        between = self.fin[2].astype(F32) + self.fin[4].astype(F32)
        return mine + jnp.where(self.end, at_end, between)


def weight_scatter_scratch(g, n, rows, w):
    steps = 5 if g.line else g.C - 1
    return [pltpu.VMEM((n, g.C, rows, w), BF), pltpu.VMEM((n, g.C - 1, rows, w), BF), pltpu.VMEM((n, steps, rows, w), BF)]


def rotated(v, cosine, sine):
    n = v.shape[1]
    if n > cosine.shape[1]:
        cosine = jnp.concatenate([cosine] * (n // cosine.shape[1]), axis=1)
        sine = jnp.concatenate([sine] * (n // sine.shape[1]), axis=1)
    lower = lax.broadcasted_iota(jnp.int32, v.shape, 1) % HD < HD // 2
    swapped = jnp.where(lower, pltpu.roll(v, n - HD // 2, 1), pltpu.roll(v, HD // 2, 1))
    return v * cosine + swapped * sine


def head_lanes(v, h):
    lane = lax.broadcasted_iota(jnp.int32, v.shape, 1)
    keep = (lane >= h * HD) & (lane < (h + 1) * HD)
    return jnp.where(keep, v, jnp.zeros_like(v))


def attend(g, hi, q_blk, keys_rot, values_t, bias, probs, inverse):
    H, R = g.H, g.R
    step = min(512, hi)
    spans = [slice(k, k + step) for k in range(0, hi, step)]
    scores, top, sums, mix = {}, [None] * H, [None] * H, [None] * H

    def fold(v, op):
        return op(v.reshape(v.shape[0] // 8, 8, v.shape[1]), axis=0)

    def first(h, span):
        s = dot(keys_rot[span], head_lanes(q_blk, h), NT) + bias[span]
        scores[h, span.start] = s
        most = fold(s, jnp.max)
        top[h] = most if top[h] is None else jnp.maximum(top[h], most)

    def second(h, span):
        if span.start == 0:
            top[h] = jnp.max(top[h], axis=0, keepdims=True)
        e = jnp.exp(scores.pop((h, span.start)) - top[h])
        some = fold(e, jnp.sum)
        sums[h] = some if sums[h] is None else sums[h] + some
        low = e.astype(BF)
        probs[span, h * R : (h + 1) * R] = low
        out = dot(values_t[h * HD : (h + 1) * HD, span], low)
        mix[h] = out if mix[h] is None else mix[h] + out

    for h in range(H + 1):
        for span in spans:
            if h < H:
                first(h, span)
            if h > 0:
                second(h - 1, span)
    for h in range(H):
        inv = 1.0 / jnp.sum(sums[h], axis=0, keepdims=True)
        inverse[h : h + 1, :] = inv
        mix[h] = mix[h] * inv
    return jnp.concatenate(mix, axis=0)


def attend_back(g, hi, values, keys_t, probs, go, qm, dots, dk, dv):
    H, R = g.H, g.R
    step = 256 if hi < g.S else hi
    grads = [None] * H
    for k in range(0, hi + step, step):
        now, past = slice(k, k + step), slice(k - step, k)
        if k < hi:
            if step < hi:
                dv[now] += dot(probs[now], go[...])
            ahead = [dot(values[now], go[0:R], NT)]
            for h in range(H):
                cols = slice(h * R, (h + 1) * R)
                if h + 1 < H:
                    ahead.append(dot(values[now], go[(h + 1) * R : (h + 2) * R], NT))
                low = (probs[now, cols].astype(F32) * (ahead[h] - dots[h])).astype(BF)
                if h == 0 and step == hi:
                    dv[now] += dot(probs[now], go[...])
                probs[now, cols] = low
                out = dot(keys_t[h * HD : (h + 1) * HD, now], low)
                grads[h] = out if grads[h] is None else grads[h] + out
        if k > 0:
            dk[past] += dot(probs[past], qm[...])
    return jnp.concatenate(grads, axis=0)


def bias_of(qinfo, kinfo, first, size, rows):
    shape = (size, rows)
    doc_q, pic_q = qinfo[0:1, :], qinfo[1:2, :]
    key_doc, pic_k = kinfo[:, 0:1], kinfo[:, 1:2]
    key_pos = lax.broadcasted_iota(jnp.int32, shape, 0)
    query_pos = lax.broadcasted_iota(jnp.int32, shape, 1) + first
    before = key_pos <= query_pos
    open_ = (doc_q == key_doc) & (before | (pic_q == pic_k))
    ok = open_ | (key_pos == query_pos)
    return jnp.where(ok, 0.0, MASKED).astype(F32)


def rotary(length, cols):
    half = HD // 2
    frequency = 10000.0 ** (-2.0 * np.arange(half) / HD)
    angle = np.arange(length)[:, None] * frequency[None, :]
    cosine = np.concatenate([np.cos(angle)] * 2, axis=1)
    sine = np.concatenate([-np.sin(angle), np.sin(angle)], axis=1)
    reps = max(1, min(cols, 128) // HD)
    return (jnp.asarray(np.tile(cosine, (1, reps)), F32), jnp.asarray(np.tile(sine, (1, reps)), F32))


def in_lanes(g):
    return g.Dn % 128 == 0 and g.f <= g.S and (g.C - 1) * g.Dn <= g.f and 2 * g.Dn <= max(g.R, g.c)


def in_slot(g, n_pic, blk):
    per = g.n_t // n_pic

    def run(body):
        for p in range(n_pic):
            pl.when(blk // per == p)(functools.partial(body, p, blk - p * per, (p + 1) * (g.S // n_pic)))

    return run


def layer_body(g, n_pic, x, teacher, valid_mask, documents, starts, wq, wk, wv, wo_in, wg_in, wu_in, wd_in, cosine_in, sine_in,
               o_out, o_in, o_q, o_k, o_v, o_o, o_g, o_u, o_d, o_loss,
               rows1, rows2, gm, ga, wa, wm, qkv, mixed, mixt, turn, wo_t, probs0, probs1, acc2, qm, gom, mids, middle, cot,
               qinfo, kinfo, rinv, cnt, err,
               part, into, out, fin,
               hidden_t, down, sib_d, spare_d, fin_d, sib_m, fin_m, sib_a, out_a, fin_a, output, grad_inputs, dattn, dout, spare_m, stats,
               wo, wg, wu, wd, cosine, sine, ts, tr, zs, zr, local):
    g.place()
    g.greet()
    R, S, c, H, C, Dn = g.R, g.S, g.c, g.H, g.C, g.Dn
    tc, zc = Comm(ts, tr), Comm(zs, zr)
    sums = (part, into, out, fin)
    few, ag_group, rs_group = tc.group(), tc.group(), tc.group()
    ag_slots = tc.slots(10 if g.square else g.n_t - 1)
    rs_slots = tc.slots(8 if g.square else g.n_t - 1)
    te = tc.slots(2 if g.square else g.n_t - 1)
    gather = functools.partial(Gather, g, tc, ag_slots, ag_group)
    scatter = functools.partial(Scatter, g, tc, rs_slots, rs_group, sums)
    q, kk, v = qkv.at[0], qkv.at[1], qkv.at[2]
    probs = (probs0, probs1)
    bias, dk, dv = acc2.at[:, :, :R], acc2.at[0, :, :c], acc2.at[1, :, :c]
    packed = in_lanes(g)
    stores = []

    def out_d(k):
        return mids.at[0, 0 : g.f, k * Dn : (k + 1) * Dn] if packed else spare_d.at[k]

    def total_m(j):
        return acc2.at[j % 2, 0 : g.f, j // 2 * Dn : (j // 2 + 1) * Dn] if packed else spare_m.at[j]

    def store(buf, to):
        copy = pltpu.make_async_copy(buf, to, local.at[1 + len(stores)])
        copy.start()
        stores.append(copy)

    def load(k, source, into):
        copy = pltpu.make_async_copy(source, into, local.at[k])
        copy.start()
        return copy

    block = g.wrows(g.d)
    get_qkv = [load(11 + j, w, wa.at[j, block]) for j, w in enumerate((wq, wk, wv))]
    get_rest = [load(14, wo_in, wo), load(15, wg_in, wg), load(16, wu_in, wu), load(17, wd_in, wd)]
    get_tables = [load(18, cosine_in, cosine), load(19, sine_in, sine)]
    get_teacher = load(0, teacher, cot)

    one, _ = normed(x[...])
    rows1[g.rows(g.t)] = one.astype(BF)
    for copy in get_qkv:
        copy.wait()
    g.meet()
    ag = gather(rows1)
    ag.begin(0)
    ag.begin(1)
    za, zo = WeightGather(g, zc, wa, 0, 3), WeightGather(g, zc, wa, 3, 1)
    zg, zd = WeightGather(g, zc, wm, 0, 2), WeightGather(g, zc, wm, 2, 1)
    za.far()
    for copy in get_rest + get_tables:
        copy.wait()
    wa[3, block] = turned(wo[...])
    zo.far()
    za.near()
    wm[0, block] = turned(wg[...])
    wm[1, block] = turned(wu[...])
    wm[2, block] = turned(wd[...])

    csib, cz = zc.slots(1)[0], zc.slots(C - 1)
    gsib, gz = zc.group(), zc.group()
    valid, doc = valid_mask[...], documents[...]
    cnt[0] = jnp.broadcast_to(jnp.sum(valid.astype(F32), axis=1, keepdims=True), (8, 128))
    zc.send(gsib, csib, cnt.at[0], cnt.at[1], (g.sib, g.t))
    at = lax.broadcasted_iota(jnp.int32, (1, S), 1)
    pic = jnp.zeros((1, S), jnp.int32)
    for p in range(n_pic):
        first = starts[0:1, p : p + 1]
        pic = jnp.where((at >= first) & (at < first + PIECE), p + 1, pic)
    qinfo[0:1] = doc
    qinfo[1:2] = pic
    as_keys = [jnp.where(valid == 1, doc, -1), jnp.where(pic > 0, pic, -1), valid]
    as_keys = jnp.concatenate([a.astype(F32) for a in as_keys] + [jnp.zeros((125, S), F32)], axis=0)
    kinfo[...] = as_keys.T.astype(jnp.int32)
    zc.recv(csib, cnt.at[1], (g.sib, g.t))
    cnt[2] = cnt[0] + cnt[1]
    for k in range(1, C):
        zc.send(gz, cz[k - 1], cnt.at[2], cnt.at[2 + k], (g.zto(k), g.t))

    def set_bias(i, blk):
        @in_slot(g, n_pic, blk)
        def _(p, index, hi):
            bias[i % 2, 0:hi] = bias_of(qinfo[:, g.rows(blk)], kinfo[0:hi], blk * R, hi, R)

    set_bias(0, g.leave[0])

    ag.relay()
    za.relay()
    zo.relay()
    zo.near()
    za.pass_on()
    za.wait()
    zg.far()
    zg.near()
    for i, blk in enumerate(ag.order):
        ag.wait(i)
        at = g.rows(blk)
        row = rows1[at]
        cos_b, sin_b = cosine[at], sine[at]
        q[at] = (rotated(dot(row, wa[0]), cos_b, sin_b) * HD**-0.5).astype(BF)
        kk[at] = rotated(dot(row, wa[1]), cos_b, sin_b).astype(BF)
        v[at] = dot(row, wa[2]).astype(BF)
    zo.pass_on()
    turn[...] = turned(v[...])

    rs = scatter()
    @pl.loop(0, g.n_t)
    def _(i):
        blk = g.leave_at(i)
        at = g.rows(blk)

        @pl.when(i > 0)
        def _():
            set_bias(i, blk)

        @in_slot(g, n_pic, blk)
        def _(p, index, hi):
            both = attend(g, hi, q[at], kk, turn, bias.at[i % 2], probs[p].at[index], rinv.at[blk])
            mixt[blk] = both.astype(BF)
            mixed[at] = both.T.astype(BF)

        pl.when(i == 0)(zo.wait)

        @pl.when(i == 2)
        def _():
            zg.relay()
            zd.far()
            zd.near()

        @pl.when(i < g.n_t - 1)
        def _():
            rs.give(i, dot(mixed[at], wa[3], NT))

    rs.relay()
    middle[0:R] = x[...] + dot(mixed[g.rows(g.t)], wa[3], NT)
    ag.sent()
    ag = gather(rows2, far_first=True)

    for i in range(2):
        for rows, summed in rs.take(i, middle):
            middle[rows] = summed
            two, _ = normed(summed)
            rows2[g.rows(g.t, rows.start, R // 4)] = two.astype(BF)
        ag.begin(i)
    rs = scatter()
    zd.relay()
    ag.relay()
    zg.pass_on()
    zg.wait()

    @pl.loop(0, g.n_t)
    def _(i):
        for k in range(1, g.n_t):
            pl.when(i == k)(functools.partial(ag.wait, k))
        at = g.rows(g.far_at(i))
        row = rows2[at]
        gate, up = dot(row, wm[0]), dot(row, wm[1])
        sig = jax.nn.sigmoid(gate)
        act = gate * sig
        mids[0, at] = (act * up).astype(BF)
        mids[2, at] = act.astype(BF)
        mids[1, at] = (up * sig * (1.0 + gate * (1.0 - sig))).astype(BF)

        @pl.when(i == 1)
        def _():
            zd.pass_on()
            zd.wait()

        @pl.when(i > 0)
        def _():
            rs.give(g.far_lead(i), dot(mids[0, at], wm[2], NT))

    output[...] = middle[0:R] + dot(mids[0, g.rows(g.t)], wm[2], NT)
    wo_t[...] = turned(wa[3])
    rs.relay()
    hidden_t[...] = turned(mids[0])

    get_teacher.wait()
    tokens = cnt[2]
    for k in range(1, C):
        zc.recv(cz[k - 1], cnt.at[2 + k], (g.zfrom(k), g.t))
        tokens = tokens + cnt[2 + k]
    share = 1.0 * S * g.n_dp / tokens[0:1, 0:1]
    ag.sent()
    ag = gather(gm, far_first=True)
    errors = jnp.zeros((R // 4, 1), F32)
    for i in range(2):
        for rows, summed in rs.take(i, output):
            output[rows] = summed
            dev = summed - cot[rows]
            kept = kinfo[g.rows(g.t, rows.start, R // 4), 2:3].astype(F32) * dev
            cotangent = kept * share
            cot[rows] = cotangent
            gm[g.rows(g.t, rows.start, R // 4)] = cotangent.astype(BF)
            errors += jnp.sum(kept * dev, axis=1, keepdims=True)
        ag.begin(i)
    store(output, o_out)
    err[0] = jnp.broadcast_to(jnp.sum(errors, axis=0, keepdims=True), (8, 128))

    rs = scatter()
    if g.square:
        tc.send(few, te[0], err.at[0], err.at[1], (g.d, g.tx))
    else:
        for k, peer in enumerate(g.to):
            tc.send(few, te[k], err.at[0], err.at[1 + k], (g.d, peer))

    zscat = [WeightScatter(g, zc, lambda d: down.at[d], down.at[0 : 2 * C - 1],
                           (sib_d.at[0], [out_d(k) for k in range(C - 1)], fin_d.at[0]))]

    @pl.loop(0, g.n_t)
    def _(i):
        for k in range(1, g.n_t):
            pl.when(i == k)(functools.partial(ag.wait, k))
        at = g.rows(g.far_at(i))
        gh = dot(gm[at], wm[2])
        mids[1, at] = (gh * mids[1, at].astype(F32)).astype(BF)
        mids[2, at] = (gh * mids[2, at].astype(F32)).astype(BF)

        @pl.when(i == 0)
        def _():
            ag.relay()
            rows2[...] = turned(rows2[...])
            turn[...] = turned(kk[...])

        @pl.when(i > 0)
        def _():
            rs.give(g.far_lead(i), dot(mids[1, at], wm[0], NT) + dot(mids[2, at], wm[1], NT))

    wide = max(256, Dn)

    @pl.loop(0, g.D // wide)
    def _(k):
        some = dot(hidden_t[...], gm[:, pl.ds(pl.multiple_of(k * wide, wide), wide)]).astype(BF)
        for n in range(wide // Dn):
            down[k * (wide // Dn) + n] = some[:, n * Dn : (n + 1) * Dn]

    zscat[0].start()
    rs.relay()
    at = g.rows(g.t)
    grad_inputs[...] = dot(mids[1, at], wm[0], NT) + dot(mids[2, at], wm[1], NT)
    zscat[0].pass_on()
    zg.sent()
    zd.sent()
    for j in range(2):
        wm[j] = dot(rows2[...], mids[1 + j]).astype(BF)
        spare = [mids.at[1 + j, k * Dn : (k + 1) * Dn] for k in range(C - 1)]
        zscat.append(WeightScatter(g, zc, lambda d, j=j: wm.at[j, g.wrows(d)], wm.at[j, 0 : (2 * C - 1) * Dn],
                                   (sib_m.at[j], spare, fin_m.at[j])))
        zscat[-1].start()
    zscat[1].pass_on()
    two, inv = normed(middle[0:R])
    ag.sent()
    ag = gather(ga)
    for i in range(2):
        for rows, back in rs.take(i, grad_inputs):
            grad_middle = cot[rows] + normed_back(two[rows], inv[rows], back)
            cot[rows] = grad_middle
            ga[g.rows(g.t, rows.start, R // 4)] = grad_middle.astype(BF)
        ag.begin(i)

    for j in (3, 0, 1, 2):
        spare = [out_a.at[j, k] for k in range(C - 1)]
        zscat.append(WeightScatter(g, zc, lambda d, j=j: wa.at[j, g.wrows(d)], wa.at[j, 0 : (2 * C - 1) * Dn],
                                   (sib_a.at[j], spare, fin_a.at[j])))

    rs = scatter()
    zscat[2].pass_on()
    zscat[0].relay(0)
    zscat[0].relay(1)
    base = 4 if g.square else g.n_t
    ec, ez = zc.slots(1)[0], zc.slots(C - 1)
    gec, gez = zc.group(), zc.group()
    if g.square:
        tc.recv(te[0], err.at[1], (g.d, g.tx))
        err[2] = err[0] + err[1]
        tc.send(few, te[1], err.at[2], err.at[3], (g.d, g.ty))
    acc2[...] = jnp.zeros_like(acc2)
    middle[0:c] = jnp.zeros((c, g.D), F32)

    @pl.loop(0, g.n_t)
    def _(i):
        @pl.when(i == 1)
        def _():
            zscat[0].relay(2)
            rows1[...] = turned(rows1[...])
            if g.square:
                tc.recv(te[1], err.at[3], (g.d, g.ty))
                err[base] = err[2] + err[3]
            else:
                total = err[0]
                for k in range(1, g.n_t):
                    tc.recv(te[k - 1], err.at[k], (g.d, (g.t + g.n_t - k) % g.n_t))
                    total = total + err[k]
                err[base] = total
            zc.send(gec, ec, err.at[base], err.at[base + 1], (g.sib, g.t))

        @pl.when(i == 2)
        def _():
            zc.recv(ec, err.at[base + 1], (g.sib, g.t))
            err[base + 2] = err[base] + err[base + 1]
            for k in range(1, C):
                zc.send(gez, ez[k - 1], err.at[base + 2], err.at[base + 2 + k], (g.zto(k), g.t))

        for k in range(1, g.n_t):
            pl.when(i == k)(functools.partial(ag.wait, k))
        blk = g.arrive_at(i)
        at = g.rows(blk)
        middle[0:c] += dot(mixt[blk], ga[at])

        @pl.when(i == g.n_t - 1)
        def _():
            zo.sent()
            wa[3] = turned(middle[0:c].astype(BF))
            zscat[3].start()

        go_t = dot(wo_t[...], ga[at], NT).astype(BF).astype(F32)
        mix_t = mixt[blk].astype(F32)
        scaled, dots = [], []
        for h in range(H):
            one_head = go_t[h * HD : (h + 1) * HD] * rinv[blk, h : h + 1, :]
            scaled.append(one_head)
            dots.append(jnp.sum(one_head * mix_t[h * HD : (h + 1) * HD], axis=0, keepdims=True))
        go = jnp.concatenate(scaled, axis=0).T.astype(BF)
        q_blk = q[at]
        for h in range(H):
            gom[h * R : (h + 1) * R] = head_lanes(go, h)
            qm[h * R : (h + 1) * R] = head_lanes(q_blk, h)

        @in_slot(g, n_pic, blk)
        def _(p, index, hi):
            dq = attend_back(g, hi, v, turn, probs[p].at[index], gom, qm, dots, dk, dv).T * HD**-0.5
            q[at] = rotated(dq, cosine[at], -sine[at]).astype(BF)

        pl.when(i == 0)(ag.relay)

        @pl.when(i == 2)
        def _():
            zscat[1].relay(0)
            zscat[1].relay(1)

    @pl.loop(0, g.n_t)
    def _(i):
        at = g.rows(g.leave_at(i))
        kk[at] = rotated(dk[at], cosine[at], -sine[at]).astype(BF)
        v[at] = dv[at].astype(BF)
        partial = dot(q[at], wa[0], NT) + dot(kk[at], wa[1], NT) + dot(v[at], wa[2], NT)

        @pl.when(i < g.n_t - 1)
        def _():
            rs.give(i, partial)

        @pl.when(i == g.n_t - 1)
        def _():
            grad_inputs[...] = partial


    zscat[3].pass_on()
    zscat[1].relay(2)
    zscat[2].relay(0)
    zscat[2].relay(1)
    za.sent()
    for j in range(3):
        wa[j] = dot(rows1[...], qkv[j]).astype(BF)
        zscat[4 + j].start()
    for j in (4, 5, 6):
        zscat[j].meet()
        zscat[j].part(0)
    rs.relay()
    for k in (1, 2):
        for j in (4, 5, 6):
            zscat[j].part(k)
    zscat[2].relay(2)
    zscat[3].relay(0)
    zscat[3].relay(1)
    one, inv = normed(x[...])

    for j, to in enumerate((o_d, o_g, o_u)):
        total_m(j)[...] = zscat[j].total().T if j else zscat[j].total()
        store(total_m(j), to)
    for j in (4, 5, 6):
        zscat[j].relay(0)
    zscat[3].relay(2)
    for j, k in ((4, 2), (5, 2), (4, 1), (6, 2), (5, 1)):
        zscat[j].relay(k)
    for i in range(2):
        for rows, back in rs.take(i, grad_inputs):
            grad_inputs[rows] = cot[rows] + normed_back(one[rows], inv[rows], back)
    store(grad_inputs, o_in)
    zscat[6].relay(1)
    dout_at = acc2.at[1, 0:c, Dn : 2 * Dn] if packed else dout
    dout_at[...] = zscat[3].total().T
    store(dout_at, o_o)
    total = err[base + 2]
    for k in range(1, C):
        zc.recv(ez[k - 1], err.at[base + 2 + k], (g.zfrom(k), g.t))
        total = total + err[base + 2 + k]
    stats[...] = (total * (1.0 / g.D) / tokens)[0:1, 0:1]
    store(stats, o_loss)
    for j, to in enumerate((o_q, o_k, o_v)):
        dattn[j] = zscat[4 + j].total()
        store(dattn.at[j], to)
    for copy in stores:
        copy.wait()
    ag.sent()
    for scat in zscat:
        scat.sent()
    tc.sent(few, err.at[0 : len(te)], (g.sib, g.t))
    for group, n in ((gsib, 1), (gz, C - 1), (gec, 1), (gez, C - 1)):
        zc.sent(group, cnt.at[0:n], (g.sib, g.t))
    assert tc.n <= tr.shape[0] and zc.n <= zr.shape[0] and tc.groups <= ts.shape[0] and zc.groups <= zs.shape[0]


def layer(g, n_pic, args):
    S, R, D, c, f, H, C, Dn = g.S, g.R, g.D, g.c, g.f, g.H, g.C, g.Dn
    sds, V = jax.ShapeDtypeStruct, pltpu.VMEM
    shapes = [(R, D), (R, D), (Dn, c), (Dn, c), (Dn, c), (c, Dn), (f, Dn), (f, Dn), (f, Dn), (1, 1)]
    outs = [sds(s, F32) for s in shapes]
    base = 4 if g.square else g.n_t
    scratch = [V((S, D), BF)] * 4 + [
        V((4, D, c), BF), V((3, D, f), BF), V((3, S, c), BF), V((S, c), BF), V((g.n_t, c, R), BF), V((c, S), BF), V((c, D), BF),
        V((g.n_t // 2, S // 2, H * R), BF), V((g.n_t // 2, S, H * R), BF), V((2, S, max(R, c)), F32), V((H * R, c), BF), V((H * R, c), BF), V((3, S, f), BF),
        V((max(R, c), D), F32), V((R, D), F32), V((8, S), jnp.int32), V((S, 128), jnp.int32), V((g.n_t, 8, R), F32),
        V((2 + C, 8, 128), F32), V((base + 2 + C, 8, 128), F32),
    ]
    scratch += scatter_scratch(g)
    m = weight_scatter_scratch(g, 2, Dn, f)
    d = weight_scatter_scratch(g, 1, f, Dn)
    few = V((1, 16, 128), BF)
    scratch += [V((f, S), BF), V((g.n_dp, f, Dn), BF), d[0], few if in_lanes(g) else V((C - 1, f, Dn), BF), d[2]]
    scratch += [m[0], m[2]] + weight_scatter_scratch(g, 4, Dn, c)
    scratch += [V((R, D), F32), V((R, D), F32), V((3, Dn, c), F32), few if in_lanes(g) else V((c, Dn), F32), few if in_lanes(g) else V((3, f, Dn), F32), V((1, 1), F32)]
    nt = 20 if g.square else 3 * (g.n_t - 1)
    nz = 4 * (2 * C - 1) + 7 * (6 if g.line else C) + 2 * C
    sem = pltpu.SemaphoreType.DMA
    scratch += [V(a.shape, a.dtype) for a in args[8:14]]
    scratch += [sem((3,)), sem((nt,)), sem((15,)), sem((nz,)), sem((20,))]
    whole = pl.BlockSpec(memory_space=pltpu.VMEM)
    specs = [whole] * len(args)
    for k in (1, *range(5, 14)):
        specs[k] = pl.BlockSpec(memory_space=pl.ANY)
    return pl.pallas_call(
        functools.partial(layer_body, g, n_pic),
        name="layer",
        out_shape=outs,
        in_specs=specs,
        out_specs=[pl.BlockSpec(memory_space=pl.ANY)] * len(outs),
        scratch_shapes=scratch,
        compiler_params=pltpu.CompilerParams(collective_id=1, has_side_effects=True, vmem_limit_bytes=VMEM_BYTES),
    )(*args)


def finish_body(n, *refs):
    parts, outs, bufs, come, go = refs[:n], refs[n : 2 * n], refs[2 * n : 3 * n], refs[3 * n], refs[3 * n + 1]
    loads = [pltpu.make_async_copy(a, b, come.at[k]) for k, (a, b) in enumerate(zip(parts, bufs))]
    stores = [pltpu.make_async_copy(a, b, go.at[k]) for k, (a, b) in enumerate(zip(bufs, outs))]
    for copy in loads:
        copy.start()
    for load, store in zip(loads, stores):
        load.wait()
        store.start()
    for copy in stores:
        copy.wait()


def finish(parts):
    anywhere, n = pl.BlockSpec(memory_space=pl.ANY), len(parts)
    return pl.pallas_call(
        functools.partial(finish_body, n),
        name="finish",
        out_shape=[jax.ShapeDtypeStruct(p.shape, F32) for p in parts],
        in_specs=[anywhere] * n,
        out_specs=[anywhere] * n,
        scratch_shapes=[pltpu.VMEM(p.shape, F32) for p in parts] + [pltpu.SemaphoreType.DMA((n,))] * 2,
    )(*parts)


def per_device(n_dp, n_t, inputs, teacher, valid_mask, documents, picture_starts,
               w_query, w_key, w_value, w_out, w_gate, w_up, w_down):
    R, D = inputs.shape
    c, f = w_query.shape[1], w_gate.shape[1]
    g = Geo(n_dp, n_t, R, D, c, f)
    args = (inputs, teacher, valid_mask, documents, picture_starts, w_query, w_key, w_value, w_out, w_gate.T, w_up.T, w_down)
    parts = layer(g, picture_starts.shape[1], (*args, *rotary(g.S, c)))
    out, *grads, gate, up, down, loss = finish(parts)
    return (out, loss.reshape(()), *grads, gate.T, up.T, down)


def solution(mesh):
    rows, pair = P(("dp", "tensor"), None), P("dp", None)
    cut, across = P("dp", "tensor"), P("tensor", "dp")
    return jax.shard_map(
        functools.partial(per_device, mesh.shape["dp"], mesh.shape["tensor"]),
        mesh=mesh,
        in_specs=(rows, rows, pair, pair, pair, cut, cut, cut, across, cut, cut, across),
        out_specs=(rows, P(), rows, cut, cut, cut, across, cut, cut, across),
        check_vma=False,
    )
```

```python
import functools

import jax
import jax.numpy as jnp
import numpy as np
from jax import lax
from jax.experimental import pallas as pl
from jax.experimental.pallas import tpu as pltpu
from jax.sharding import PartitionSpec as P

MESH = pl.DeviceIdType.MESH
HD = 64
PIECE = 256
EPS = 1e-5
MASKED = -1e30
VMEM_BYTES = 60 * 2**20
BF = jnp.bfloat16
F32 = jnp.float32
NT = (((1,), (1,)), ((), ()))
NN = (((1,), (0,)), ((), ()))


def dot(a, b, dims=NN):
    return lax.dot_general(a, b, dims, preferred_element_type=F32)


def eye(n):
    return (
        lax.broadcasted_iota(jnp.int32, (n, n), 0) == lax.broadcasted_iota(jnp.int32, (n, n), 1)
    ).astype(F32).astype(BF)


def turned(a):
    n = a.shape[1]
    step = min(n, 256)
    parts = [dot(eye(min(step, n - k)), a[:, k : k + step], NT).astype(BF) for k in range(0, n, step)]
    return parts[0] if len(parts) == 1 else jnp.concatenate(parts, axis=0)


def mean_of(v):
    return jnp.sum(v, axis=1, keepdims=True) * (1.0 / v.shape[1])


def normed(v):
    centred = v - mean_of(v)
    inv = lax.rsqrt(mean_of(centred * centred) + EPS)
    return centred * inv, inv


def normed_back(n, inv, g):
    return inv * (g - mean_of(g) - n * mean_of(g * n))


class Geo:
    def __init__(self, n_dp, n_t, tok_rows, d_model, cols, hid):
        self.n_dp, self.n_t, self.R, self.D, self.c, self.f = n_dp, n_t, tok_rows, d_model, cols, hid
        self.C = n_dp // 2
        self.S = tok_rows * n_t
        self.H = cols // HD
        self.Dn = d_model // n_dp
        self.square = n_t == 4
        self.line = self.C == 4

    def place(self):
        self.d = lax.axis_index("dp")
        self.t = lax.axis_index("tensor")
        self.chip = self.d // 2
        self.core = self.d % 2
        if self.square:
            self.tx = self.t + 1 - 2 * (self.t % 2)
            self.ty = (self.t + 2) % 4
            self.td = 3 - self.t
            self.to = [self.tx, self.ty]
            self.leave = [self.td, self.tx, self.ty, self.t]
        else:
            n = self.n_t
            self.to = [(self.t + k) % n for k in range(1, n)]
            self.leave = [(self.t + k) % n for k in range(1, n)] + [self.t]
        self.sib = self.d + 1 - 2 * self.core
        return self

    def leave_at(self, i):
        if self.square:
            return 2 * ((self.t // 2 + i + 1) % 2) + (self.t % 2 + 1 - i // 2) % 2
        return (self.t + 1 + i) % self.n_t

    def arrive_at(self, i):
        if self.square:
            return 2 * ((self.t // 2 + i // 2) % 2) + (self.t % 2 + i % 2) % 2
        return (self.t + self.n_t - i) % self.n_t

    def far_at(self, i):
        if self.square:
            return 2 * ((self.t // 2 + i % 2) % 2) + (self.t % 2 + (i + 1) // 2) % 2
        return (self.t + self.n_t - i) % self.n_t

    def far_lead(self, i):
        return i - 1 if self.square else self.n_t - 1 - i

    def zto(self, k):
        return ((self.chip + k) % self.C) * 2 + self.core

    def zfrom(self, k):
        return ((self.chip + self.C - k) % self.C) * 2 + self.core

    def rows(self, blk, first=0, count=None):
        count = self.R if count is None else count
        return pl.ds(pl.multiple_of(blk * self.R + first, count), count)

    def wrows(self, d):
        return pl.ds(pl.multiple_of(d * self.Dn, self.Dn), self.Dn)

    def greet(self):
        bar = pltpu.get_barrier_semaphore()
        out = [(self.d, p) for p in self.to]
        out += [(self.zto(k), self.t) for k in range(1, self.C)] + [(self.sib, self.t)]
        for dev in out:
            pl.semaphore_signal(bar, inc=1, device_id=dev, device_id_type=MESH)
        self.met = len(out)

    def meet(self):
        pl.semaphore_wait(pltpu.get_barrier_semaphore(), self.met)


class Comm:
    def __init__(self, send_sem, recv_sem):
        self.ss, self.rs = send_sem, recv_sem
        self.n = self.groups = 0

    def slots(self, k):
        self.n += k
        return list(range(self.n - k, self.n))

    def group(self):
        self.groups += 1
        return self.groups - 1

    def _copy(self, group, slot, src, dst, dev):
        return pltpu.make_async_remote_copy(
            src_ref=src, dst_ref=dst, send_sem=self.ss.at[group], recv_sem=self.rs.at[slot], device_id=dev, device_id_type=MESH
        )

    def send(self, group, slot, src, dst, dev, when=None):
        copy = self._copy(group, slot, src, dst, dev)
        if when is None:
            copy.start()
        else:
            pl.when(when)(copy.start)

    def recv(self, slot, dst, dev, when=None):
        copy = self._copy(0, slot, dst, dst, dev)
        if when is None:
            copy.wait_recv()
        else:
            pl.when(when)(copy.wait_recv)

    def sent(self, group, like, dev, when=None):
        copy = self._copy(group, 0, like, like, dev)
        if when is None:
            copy.wait_send()
        else:
            pl.when(when)(copy.wait_send)


class Gather:
    def __init__(self, geo, comm, slots, group, buf, far_first=False):
        self.g, self.comm, self.buf, self.group = geo, comm, buf, group
        g = geo
        self.far_first = far_first and g.square
        if not g.square:
            self.s = slots
            self.order = [(g.t + g.n_t - k) % g.n_t for k in range(g.n_t)]
            self.lead = [g.n_t - 1] + [g.n_t - 1 - k for k in range(1, g.n_t)]
            return
        self.sx, self.sy = slots[:5], slots[5:]
        if self.far_first:
            self.order, self.lead = [g.t, g.td, g.tx, g.ty], [3, 0, 1, 2]
        else:
            self.order, self.lead = [g.t, g.tx, g.ty, g.td], [3, 1, 2, 0]

    def begin(self, i):
        g, comm = self.g, self.comm
        if g.square:
            self._give(self.sx[i], g.t, i, 1, g.tx)
            self._give(self.sy[i], g.t, 2 + i, 1, g.ty)
            if i == 1 and not self.far_first:
                self._rest()
        elif i == 1:
            own = self.buf.at[g.rows(g.t)]
            for k, peer in enumerate(g.to):
                comm.send(self.group, self.s[k], own, own, (g.d, peer))

    def sent(self):
        self.comm.sent(self.group, self.buf.at[0 : (self.g.n_t - 1) * self.g.R], (self.g.d, self.g.to[0]))

    def piece(self, blk, first, count):
        q = self.g.R // 4
        rows = pl.ds(pl.multiple_of(blk * self.g.R + first * q, q), count * q)
        return self.buf.at[rows]

    def _give(self, slot, blk, first, count, to):
        part = self.piece(blk, first, count)
        self.comm.send(self.group, slot, part, part, (self.g.d, to))

    def _rest(self):
        g = self.g
        self._give(self.sx[4], g.t, 2, 2, g.tx)
        self._give(self.sy[4], g.t, 0, 2, g.ty)

    def relay(self):
        g, comm = self.g, self.comm
        if not g.square:
            return
        for i in range(2):
            comm.recv(self.sx[i], self.piece(g.tx, i, 1), (g.d, g.tx))
            self._give(self.sy[2 + i], g.tx, i, 1, g.ty)
            comm.recv(self.sy[i], self.piece(g.ty, 2 + i, 1), (g.d, g.ty))
            self._give(self.sx[2 + i], g.ty, 2 + i, 1, g.tx)
        if self.far_first:
            self._rest()

    def wait(self, i):
        g, comm = self.g, self.comm
        if i == 0:
            return
        if not g.square:
            comm.recv(self.s[i - 1], self.buf.at[g.rows(self.order[i])], (g.d, self.order[i]))
            return
        which = "dxy"[i - 1] if self.far_first else "xyd"[i - 1]
        if which == "x":
            comm.recv(self.sx[4], self.piece(g.tx, 2, 2), (g.d, g.tx))
        elif which == "y":
            comm.recv(self.sy[4], self.piece(g.ty, 0, 2), (g.d, g.ty))
        else:
            for k in range(2):
                comm.recv(self.sx[2 + k], self.piece(g.td, 2 + k, 1), (g.d, g.tx))
                comm.recv(self.sy[2 + k], self.piece(g.td, k, 1), (g.d, g.ty))


def scatter_scratch(g):
    h = g.R // 2
    if g.square:
        return [pltpu.VMEM((3, 2, h, g.D), BF), pltpu.VMEM((2, h, g.D), BF), pltpu.VMEM((2, h, g.D), BF), pltpu.VMEM((2, 2, h, g.D), BF)]
    return [pltpu.VMEM((g.n_t - 1, 2, h, g.D), BF), pltpu.VMEM((1, 16, 128), BF), pltpu.VMEM((1, 16, 128), BF), pltpu.VMEM((g.n_t - 1, 2, h, g.D), BF)]


class Scatter:
    def __init__(self, geo, comm, slots, group, bufs):
        self.g, self.comm, self.group = geo, comm, group
        self.part, self.into, self.out, self.fin = bufs
        g = geo
        if g.square:
            self.sx, self.sy = slots[:4], slots[4:]
        else:
            self.s = slots

    def give(self, i, value):
        h = self.g.R // 2
        for j in range(2):
            self.part[i, j] = value[j * h : (j + 1) * h].astype(BF)
        if isinstance(i, int):
            self.send(i)
        else:
            for k in range(self.g.n_t - 1):
                pl.when(i == k)(functools.partial(self.send, k))

    def send(self, i):
        g, comm = self.g, self.comm
        if not g.square:
            comm.send(self.group, self.s[i], self.part.at[i], self.fin.at[i], (g.d, g.leave[i]))
        elif i == 0:
            comm.send(self.group, self.sx[0], self.part.at[0, 0], self.into.at[0], (g.d, g.tx))
            comm.send(self.group, self.sy[0], self.part.at[0, 1], self.into.at[1], (g.d, g.ty))
        elif i == 1:
            comm.send(self.group, self.sx[1], self.part.at[1, 0], self.fin.at[0, 0], (g.d, g.tx))
        else:
            comm.send(self.group, self.sy[1], self.part.at[2, 1], self.fin.at[1, 1], (g.d, g.ty))

    def relay(self):
        g, comm = self.g, self.comm
        if not g.square:
            return
        q = g.R // 4
        comm.recv(self.sx[0], self.into.at[0], (g.d, g.tx))
        comm.recv(self.sy[0], self.into.at[1], (g.d, g.ty))
        for k in range(2):
            rows = slice(k * q, (k + 1) * q)
            for a, mine, slots, to in ((0, (2, 0), self.sy, g.ty), (1, (1, 1), self.sx, g.tx)):
                self.out[a, rows] = (self.into[a, rows].astype(F32) + self.part[(*mine, rows)].astype(F32)).astype(BF)
                comm.send(self.group, slots[2 + k], self.out.at[a, rows], self.fin.at[1 - a, a, rows], (g.d, to))

    def take(self, i, own):
        g, comm = self.g, self.comm
        q = g.R // 4
        count = 2 if g.square else g.n_t - 1
        inner = slice(i * q, (i + 1) * q)
        if g.square:
            if i == 0:
                comm.recv(self.sx[1], self.fin.at[0, 0], (g.d, g.tx))
                comm.recv(self.sy[1], self.fin.at[1, 1], (g.d, g.ty))
            comm.recv(self.sx[2 + i], self.fin.at[0, 1, inner], (g.d, g.tx))
            comm.recv(self.sy[2 + i], self.fin.at[1, 0, inner], (g.d, g.ty))
        elif i == 0:
            for k in range(count):
                comm.recv(self.s[k], self.fin.at[k], (g.d, (g.t + g.n_t - k - 1) % g.n_t))
        pairs = []
        for j in range(2):
            rows = slice(2 * j * q + i * q, 2 * j * q + (i + 1) * q)
            v = own[rows]
            for k in range(count):
                v = v + self.fin[k, j, inner].astype(F32)
            pairs.append((rows, v))
        if i == 1:
            comm.sent(self.group, self.part, (g.d, g.to[0]))
        return pairs


class WeightGather:
    def __init__(self, geo, comm, buf, first, n):
        self.g, self.comm, self.buf, self.of = geo, comm, buf, pl.ds(first, n)
        g = geo
        self.group = comm.group()
        self.inner = (g.chip == 1) | (g.chip == 2)
        self.sz, self.sc = comm.slots(g.C - 1), comm.slots(g.C)

    def at(self, d):
        return self.buf.at[self.of, self.g.wrows(d)]

    def far(self):
        g, comm = self.g, self.comm
        if g.line:
            comm.send(self.group, self.sz[1], self.at(g.d), self.at(g.d), (g.zto(2), g.t))

    def near(self):
        g, comm = self.g, self.comm
        own = self.at(g.d)
        for k in range(1, g.C):
            if g.line and k == 2:
                continue
            near = g.chip != (0 if k == 3 else 3) if g.line else None
            comm.send(self.group, self.sz[k - 1], own, own, (g.zto(k), g.t), when=near)
        comm.send(self.group, self.sc[0], own, own, (g.sib, g.t))

    def _take(self, k, when=None):
        g, comm = self.g, self.comm
        block = self.at(g.zfrom(k))
        comm.recv(self.sz[k - 1], block, (g.zfrom(k), g.t), when=when)
        comm.send(self.group, self.sc[k], block, block, (g.sib, g.t), when=when)

    def relay(self):
        g, comm = self.g, self.comm
        if not g.line:
            return
        self._take(2, self.inner)
        block = self.at(g.zfrom(2))
        comm.send(self.group, self.sz[2], block, block, (6 + g.core, g.t), when=g.chip == 2)
        comm.send(self.group, self.sz[0], block, block, (g.core, g.t), when=g.chip == 1)

    def pass_on(self):
        g = self.g
        for k in range(1, g.C):
            self._take(k, jnp.logical_not(self.inner) if g.line and k == 2 else None)

    def wait(self):
        g, comm = self.g, self.comm
        for k in range(g.C):
            other = g.zfrom(k) + 1 - 2 * g.core
            comm.recv(self.sc[k], self.at(other), (g.sib, g.t))

    def sent(self):
        g, comm = self.g, self.comm

        def some(n, when=None):
            comm.sent(self.group, self.buf.at[self.of, 0 : n * g.Dn], (g.sib, g.t), when)

        if g.line:
            some(8, self.inner)
            some(6, jnp.logical_not(self.inner))
        else:
            some(2 * g.C - 1)


class WeightScatter:
    def __init__(self, geo, comm, block, most, bufs):
        self.g, self.comm, self.block, self.most = geo, comm, block, most
        self.sib_in, self.out, self.fin = bufs
        g = geo
        self.group = comm.group()
        self.sc, self.sz = comm.slots(1)[0], comm.slots(5 if g.line else g.C - 1)
        half = g.chip // 2
        self.near, self.inner, self.other, self.opposite = 3 * half, 1 + half, 2 - half, 3 - 3 * half
        self.end = (g.chip == 0) | (g.chip == 3)

    def start(self):
        g, comm = self.g, self.comm
        for j in range(g.C):
            comm.send(self.group, self.sc, self.block(2 * j + 1 - g.core), self.sib_in.at[j], (g.sib, g.t))

    def _sum(self, chip):
        return self.block(2 * chip + self.g.core)[...].astype(F32) + self.sib_in[chip].astype(F32)

    def meet(self):
        g, comm = self.g, self.comm
        comm.recv(self.sc, self.sib_in, (g.sib, g.t))

    def part(self, b):
        g, comm = self.g, self.comm
        if not g.line:
            for k in range(1, g.C) if b == 0 else ():
                self.out[k - 1][...] = self._sum((g.chip + k) % g.C).astype(BF)
                comm.send(self.group, self.sz[k - 1], self.out[k - 1], self.fin.at[k - 1], (g.zto(k), g.t))
            return

        @pl.when(self.end)
        def _():
            self.out[b][...] = self._sum((self.opposite, self.other, self.inner)[b]).astype(BF)

        to = (self.inner * 2 + g.core, g.t)
        comm.send(self.group, self.sz[b], self.out[b], self.fin.at[b], to, when=self.end)

    def pass_on(self):
        self.meet()
        for b in range(3):
            self.part(b)

    def relay(self, b):
        g, comm = self.g, self.comm
        if not g.line:
            return
        middle = jnp.logical_not(self.end)
        came = (0, 1, 3)[b]

        @pl.when(middle)
        def _():
            comm.recv(self.sz[came], self.fin.at[came], (g.sib, g.t))
            mine = self._sum((self.opposite, self.other, self.near)[b])
            self.out[b][...] = (mine + self.fin[came].astype(F32)).astype(BF)

        goes = (3, 4, 0)[b]
        to = ((self.other, self.other, self.near)[b] * 2 + g.core, g.t)
        comm.send(self.group, self.sz[goes], self.out[b], self.fin.at[goes], to, when=middle)

    def sent(self):
        self.comm.sent(self.group, self.most, (self.g.sib, self.g.t))

    def total(self):
        g, comm = self.g, self.comm
        mine = self.block(g.d)[...].astype(F32) + self.sib_in[g.chip].astype(F32)
        if not g.line:
            for k in range(1, g.C):
                comm.recv(self.sz[k - 1], self.fin.at[k - 1], (g.zfrom(k), g.t))
                mine = mine + self.fin[k - 1].astype(F32)
            return mine
        middle = jnp.logical_not(self.end)
        comm.recv(self.sz[0], self.fin.at[0], (g.sib, g.t), when=self.end)
        comm.recv(self.sz[2], self.fin.at[2], (g.sib, g.t), when=middle)
        comm.recv(self.sz[4], self.fin.at[4], (g.sib, g.t), when=middle)
        at_end = self.fin[0].astype(F32)
        between = self.fin[2].astype(F32) + self.fin[4].astype(F32)
        return mine + jnp.where(self.end, at_end, between)


def weight_scatter_scratch(g, n, rows, w):
    steps = 5 if g.line else g.C - 1
    return [pltpu.VMEM((n, g.C, rows, w), BF), pltpu.VMEM((n, g.C - 1, rows, w), BF), pltpu.VMEM((n, steps, rows, w), BF)]


def rotated(v, cosine, sine):
    n = v.shape[1]
    if n > cosine.shape[1]:
        cosine = jnp.concatenate([cosine] * (n // cosine.shape[1]), axis=1)
        sine = jnp.concatenate([sine] * (n // sine.shape[1]), axis=1)
    lower = lax.broadcasted_iota(jnp.int32, v.shape, 1) % HD < HD // 2
    swapped = jnp.where(lower, pltpu.roll(v, n - HD // 2, 1), pltpu.roll(v, HD // 2, 1))
    return v * cosine + swapped * sine


def head_lanes(v, h):
    lane = lax.broadcasted_iota(jnp.int32, v.shape, 1)
    keep = (lane >= h * HD) & (lane < (h + 1) * HD)
    return jnp.where(keep, v, jnp.zeros_like(v))


def attend(g, hi, q_blk, keys_rot, values_t, bias, probs, inverse):
    H, R = g.H, g.R
    step = min(512, hi)
    spans = [slice(k, k + step) for k in range(0, hi, step)]
    scores, top, sums, mix = {}, [None] * H, [None] * H, [None] * H

    def fold(v, op):
        return op(v.reshape(v.shape[0] // 8, 8, v.shape[1]), axis=0)

    def first(h, span):
        s = dot(keys_rot[span], head_lanes(q_blk, h), NT) + bias[span]
        scores[h, span.start] = s
        most = fold(s, jnp.max)
        top[h] = most if top[h] is None else jnp.maximum(top[h], most)

    def second(h, span):
        if span.start == 0:
            top[h] = jnp.max(top[h], axis=0, keepdims=True)
        e = jnp.exp(scores.pop((h, span.start)) - top[h])
        some = fold(e, jnp.sum)
        sums[h] = some if sums[h] is None else sums[h] + some
        low = e.astype(BF)
        probs[span, h * R : (h + 1) * R] = low
        out = dot(values_t[h * HD : (h + 1) * HD, span], low)
        mix[h] = out if mix[h] is None else mix[h] + out

    for h in range(H + 1):
        for span in spans:
            if h < H:
                first(h, span)
            if h > 0:
                second(h - 1, span)
    for h in range(H):
        inv = 1.0 / jnp.sum(sums[h], axis=0, keepdims=True)
        inverse[h : h + 1, :] = inv
        mix[h] = mix[h] * inv
    return jnp.concatenate(mix, axis=0)


def attend_back(g, hi, values, keys_t, probs, go, qm, dots, dk, dv):
    H, R = g.H, g.R
    step = 256 if hi < g.S else hi
    grads = [None] * H
    for k in range(0, hi + step, step):
        now, past = slice(k, k + step), slice(k - step, k)
        if k < hi:
            if step < hi:
                dv[now] += dot(probs[now], go[...])
            ahead = [dot(values[now], go[0:R], NT)]
            for h in range(H):
                cols = slice(h * R, (h + 1) * R)
                if h + 1 < H:
                    ahead.append(dot(values[now], go[(h + 1) * R : (h + 2) * R], NT))
                low = (probs[now, cols].astype(F32) * (ahead[h] - dots[h])).astype(BF)
                if h == 0 and step == hi:
                    dv[now] += dot(probs[now], go[...])
                probs[now, cols] = low
                out = dot(keys_t[h * HD : (h + 1) * HD, now], low)
                grads[h] = out if grads[h] is None else grads[h] + out
        if k > 0:
            dk[past] += dot(probs[past], qm[...])
    return jnp.concatenate(grads, axis=0)


def bias_of(qinfo, kinfo, first, size, rows):
    shape = (size, rows)
    doc_q, pic_q = qinfo[0:1, :], qinfo[1:2, :]
    key_doc, pic_k = kinfo[:, 0:1], kinfo[:, 1:2]
    key_pos = lax.broadcasted_iota(jnp.int32, shape, 0)
    query_pos = lax.broadcasted_iota(jnp.int32, shape, 1) + first
    before = key_pos <= query_pos
    open_ = (doc_q == key_doc) & (before | (pic_q == pic_k))
    ok = open_ | (key_pos == query_pos)
    return jnp.where(ok, 0.0, MASKED).astype(F32)


def rotary(length, cols):
    half = HD // 2
    frequency = 10000.0 ** (-2.0 * np.arange(half) / HD)
    angle = np.arange(length)[:, None] * frequency[None, :]
    cosine = np.concatenate([np.cos(angle)] * 2, axis=1)
    sine = np.concatenate([-np.sin(angle), np.sin(angle)], axis=1)
    reps = max(1, min(cols, 128) // HD)
    return (jnp.asarray(np.tile(cosine, (1, reps)), F32), jnp.asarray(np.tile(sine, (1, reps)), F32))


def in_lanes(g):
    return g.Dn % 128 == 0 and g.f <= g.S and (g.C - 1) * g.Dn <= g.f and 2 * g.Dn <= max(g.R, g.c)


def in_slot(g, n_pic, blk):
    per = g.n_t // n_pic

    def run(body):
        for p in range(n_pic):
            pl.when(blk // per == p)(functools.partial(body, p, blk - p * per, (p + 1) * (g.S // n_pic)))

    return run


def layer_body(g, n_pic, x, teacher, valid_mask, documents, starts, wq, wk, wv, wo_in, wg_in, wu_in, wd_in, cosine_in, sine_in,
               o_out, o_in, o_q, o_k, o_v, o_o, o_g, o_u, o_d, o_loss,
               rows1, rows2, gm, ga, wa, wm, qkv, mixed, mixt, turn, wo_t, probs0, probs1, acc2, qm, gom, mids, middle, cot,
               qinfo, kinfo, rinv, cnt, err,
               part, into, out, fin,
               hidden_t, down, sib_d, spare_d, fin_d, sib_m, fin_m, sib_a, out_a, fin_a, output, grad_inputs, dattn, dout, spare_m, stats,
               wo, wg, wu, wd, cosine, sine, ts, tr, zs, zr, local):
    g.place()
    g.greet()
    R, S, c, H, C, Dn = g.R, g.S, g.c, g.H, g.C, g.Dn
    tc, zc = Comm(ts, tr), Comm(zs, zr)
    sums = (part, into, out, fin)
    few, ag_group, rs_group = tc.group(), tc.group(), tc.group()
    ag_slots = tc.slots(10 if g.square else g.n_t - 1)
    rs_slots = tc.slots(8 if g.square else g.n_t - 1)
    te = tc.slots(2 if g.square else g.n_t - 1)
    gather = functools.partial(Gather, g, tc, ag_slots, ag_group)
    scatter = functools.partial(Scatter, g, tc, rs_slots, rs_group, sums)
    q, kk, v = qkv.at[0], qkv.at[1], qkv.at[2]
    probs = (probs0, probs1)
    bias, dk, dv = acc2.at[:, :, :R], acc2.at[0, :, :c], acc2.at[1, :, :c]
    packed = in_lanes(g)
    stores = []

    def out_d(k):
        return mids.at[0, 0 : g.f, k * Dn : (k + 1) * Dn] if packed else spare_d.at[k]

    def total_m(j):
        return acc2.at[j % 2, 0 : g.f, j // 2 * Dn : (j // 2 + 1) * Dn] if packed else spare_m.at[j]

    def store(buf, to):
        copy = pltpu.make_async_copy(buf, to, local.at[1 + len(stores)])
        copy.start()
        stores.append(copy)

    def load(k, source, into):
        copy = pltpu.make_async_copy(source, into, local.at[k])
        copy.start()
        return copy

    block = g.wrows(g.d)
    get_qkv = [load(11 + j, w, wa.at[j, block]) for j, w in enumerate((wq, wk, wv))]
    get_rest = [load(14, wo_in, wo), load(15, wg_in, wg), load(16, wu_in, wu), load(17, wd_in, wd)]
    get_tables = [load(18, cosine_in, cosine), load(19, sine_in, sine)]
    get_teacher = load(0, teacher, cot)

    one, _ = normed(x[...])
    rows1[g.rows(g.t)] = one.astype(BF)
    for copy in get_qkv:
        copy.wait()
    g.meet()
    ag = gather(rows1)
    ag.begin(0)
    ag.begin(1)
    za, zo = WeightGather(g, zc, wa, 0, 3), WeightGather(g, zc, wa, 3, 1)
    zg, zd = WeightGather(g, zc, wm, 0, 2), WeightGather(g, zc, wm, 2, 1)
    za.far()
    for copy in get_rest + get_tables:
        copy.wait()
    wa[3, block] = turned(wo[...])
    zo.far()
    za.near()
    wm[0, block] = turned(wg[...])
    wm[1, block] = turned(wu[...])
    wm[2, block] = turned(wd[...])

    csib, cz = zc.slots(1)[0], zc.slots(C - 1)
    gsib, gz = zc.group(), zc.group()
    valid, doc = valid_mask[...], documents[...]
    cnt[0] = jnp.broadcast_to(jnp.sum(valid.astype(F32), axis=1, keepdims=True), (8, 128))
    zc.send(gsib, csib, cnt.at[0], cnt.at[1], (g.sib, g.t))
    at = lax.broadcasted_iota(jnp.int32, (1, S), 1)
    pic = jnp.zeros((1, S), jnp.int32)
    for p in range(n_pic):
        first = starts[0:1, p : p + 1]
        pic = jnp.where((at >= first) & (at < first + PIECE), p + 1, pic)
    qinfo[0:1] = doc
    qinfo[1:2] = pic
    as_keys = [jnp.where(valid == 1, doc, -1), jnp.where(pic > 0, pic, -1), valid]
    as_keys = jnp.concatenate([a.astype(F32) for a in as_keys] + [jnp.zeros((125, S), F32)], axis=0)
    kinfo[...] = as_keys.T.astype(jnp.int32)
    zc.recv(csib, cnt.at[1], (g.sib, g.t))
    cnt[2] = cnt[0] + cnt[1]
    for k in range(1, C):
        zc.send(gz, cz[k - 1], cnt.at[2], cnt.at[2 + k], (g.zto(k), g.t))

    def set_bias(i, blk):
        @in_slot(g, n_pic, blk)
        def _(p, index, hi):
            bias[i % 2, 0:hi] = bias_of(qinfo[:, g.rows(blk)], kinfo[0:hi], blk * R, hi, R)

    set_bias(0, g.leave[0])

    ag.relay()
    za.relay()
    zo.relay()
    zo.near()
    za.pass_on()
    za.wait()
    zg.far()
    zg.near()
    for i, blk in enumerate(ag.order):
        ag.wait(i)
        at = g.rows(blk)
        row = rows1[at]
        cos_b, sin_b = cosine[at], sine[at]
        q[at] = (rotated(dot(row, wa[0]), cos_b, sin_b) * HD**-0.5).astype(BF)
        kk[at] = rotated(dot(row, wa[1]), cos_b, sin_b).astype(BF)
        v[at] = dot(row, wa[2]).astype(BF)
    zo.pass_on()
    turn[...] = turned(v[...])

    rs = scatter()
    @pl.loop(0, g.n_t)
    def _(i):
        blk = g.leave_at(i)
        at = g.rows(blk)

        @pl.when(i > 0)
        def _():
            set_bias(i, blk)

        @in_slot(g, n_pic, blk)
        def _(p, index, hi):
            both = attend(g, hi, q[at], kk, turn, bias.at[i % 2], probs[p].at[index], rinv.at[blk])
            mixt[blk] = both.astype(BF)
            mixed[at] = both.T.astype(BF)

        pl.when(i == 0)(zo.wait)

        @pl.when(i == 2)
        def _():
            zg.relay()
            zd.far()
            zd.near()

        @pl.when(i < g.n_t - 1)
        def _():
            rs.give(i, dot(mixed[at], wa[3], NT))

    rs.relay()
    middle[0:R] = x[...] + dot(mixed[g.rows(g.t)], wa[3], NT)
    ag.sent()
    ag = gather(rows2, far_first=True)

    for i in range(2):
        for rows, summed in rs.take(i, middle):
            middle[rows] = summed
            two, _ = normed(summed)
            rows2[g.rows(g.t, rows.start, R // 4)] = two.astype(BF)
        ag.begin(i)
    rs = scatter()
    zd.relay()
    ag.relay()
    zg.pass_on()
    zg.wait()

    @pl.loop(0, g.n_t)
    def _(i):
        for k in range(1, g.n_t):
            pl.when(i == k)(functools.partial(ag.wait, k))
        at = g.rows(g.far_at(i))
        row = rows2[at]
        gate, up = dot(row, wm[0]), dot(row, wm[1])
        sig = jax.nn.sigmoid(gate)
        act = gate * sig
        mids[0, at] = (act * up).astype(BF)
        mids[2, at] = act.astype(BF)
        mids[1, at] = (up * sig * (1.0 + gate * (1.0 - sig))).astype(BF)

        @pl.when(i == 1)
        def _():
            zd.pass_on()
            zd.wait()

        @pl.when(i > 0)
        def _():
            rs.give(g.far_lead(i), dot(mids[0, at], wm[2], NT))

    output[...] = middle[0:R] + dot(mids[0, g.rows(g.t)], wm[2], NT)
    wo_t[...] = turned(wa[3])
    rs.relay()
    hidden_t[...] = turned(mids[0])

    get_teacher.wait()
    tokens = cnt[2]
    for k in range(1, C):
        zc.recv(cz[k - 1], cnt.at[2 + k], (g.zfrom(k), g.t))
        tokens = tokens + cnt[2 + k]
    share = 1.0 * S * g.n_dp / tokens[0:1, 0:1]
    ag.sent()
    ag = gather(gm, far_first=True)
    errors = jnp.zeros((R // 4, 1), F32)
    for i in range(2):
        for rows, summed in rs.take(i, output):
            output[rows] = summed
            dev = summed - cot[rows]
            kept = kinfo[g.rows(g.t, rows.start, R // 4), 2:3].astype(F32) * dev
            cotangent = kept * share
            cot[rows] = cotangent
            gm[g.rows(g.t, rows.start, R // 4)] = cotangent.astype(BF)
            errors += jnp.sum(kept * dev, axis=1, keepdims=True)
        ag.begin(i)
    store(output, o_out)
    err[0] = jnp.broadcast_to(jnp.sum(errors, axis=0, keepdims=True), (8, 128))

    rs = scatter()
    if g.square:
        tc.send(few, te[0], err.at[0], err.at[1], (g.d, g.tx))
    else:
        for k, peer in enumerate(g.to):
            tc.send(few, te[k], err.at[0], err.at[1 + k], (g.d, peer))

    zscat = [WeightScatter(g, zc, lambda d: down.at[d], down.at[0 : 2 * C - 1],
                           (sib_d.at[0], [out_d(k) for k in range(C - 1)], fin_d.at[0]))]

    @pl.loop(0, g.n_t)
    def _(i):
        for k in range(1, g.n_t):
            pl.when(i == k)(functools.partial(ag.wait, k))
        at = g.rows(g.far_at(i))
        gh = dot(gm[at], wm[2])
        mids[1, at] = (gh * mids[1, at].astype(F32)).astype(BF)
        mids[2, at] = (gh * mids[2, at].astype(F32)).astype(BF)

        @pl.when(i == 0)
        def _():
            ag.relay()
            rows2[...] = turned(rows2[...])
            turn[...] = turned(kk[...])

        @pl.when(i > 0)
        def _():
            rs.give(g.far_lead(i), dot(mids[1, at], wm[0], NT) + dot(mids[2, at], wm[1], NT))

    wide = max(256, Dn)

    @pl.loop(0, g.D // wide)
    def _(k):
        some = dot(hidden_t[...], gm[:, pl.ds(pl.multiple_of(k * wide, wide), wide)]).astype(BF)
        for n in range(wide // Dn):
            down[k * (wide // Dn) + n] = some[:, n * Dn : (n + 1) * Dn]

    zscat[0].start()
    rs.relay()
    zscat[0].pass_on()
    at = g.rows(g.t)
    grad_inputs[...] = dot(mids[1, at], wm[0], NT) + dot(mids[2, at], wm[1], NT)
    zg.sent()
    zd.sent()
    for j in range(2):
        wm[j] = dot(rows2[...], mids[1 + j]).astype(BF)
        spare = [mids.at[1 + j, k * Dn : (k + 1) * Dn] for k in range(C - 1)]
        zscat.append(WeightScatter(g, zc, lambda d, j=j: wm.at[j, g.wrows(d)], wm.at[j, 0 : (2 * C - 1) * Dn],
                                   (sib_m.at[j], spare, fin_m.at[j])))
        zscat[-1].start()
    zscat[1].pass_on()
    two, inv = normed(middle[0:R])
    ag.sent()
    ag = gather(ga)
    for i in range(2):
        for rows, back in rs.take(i, grad_inputs):
            grad_middle = cot[rows] + normed_back(two[rows], inv[rows], back)
            cot[rows] = grad_middle
            ga[g.rows(g.t, rows.start, R // 4)] = grad_middle.astype(BF)
        ag.begin(i)

    for j in (3, 0, 1, 2):
        spare = [out_a.at[j, k] for k in range(C - 1)]
        zscat.append(WeightScatter(g, zc, lambda d, j=j: wa.at[j, g.wrows(d)], wa.at[j, 0 : (2 * C - 1) * Dn],
                                   (sib_a.at[j], spare, fin_a.at[j])))

    rs = scatter()
    zscat[2].pass_on()
    zscat[0].relay(0)
    zscat[0].relay(1)
    base = 4 if g.square else g.n_t
    ec, ez = zc.slots(1)[0], zc.slots(C - 1)
    gec, gez = zc.group(), zc.group()
    if g.square:
        tc.recv(te[0], err.at[1], (g.d, g.tx))
        err[2] = err[0] + err[1]
        tc.send(few, te[1], err.at[2], err.at[3], (g.d, g.ty))
    acc2[...] = jnp.zeros_like(acc2)
    middle[0:c] = jnp.zeros((c, g.D), F32)

    @pl.loop(0, g.n_t)
    def _(i):
        @pl.when(i == 1)
        def _():
            zscat[0].relay(2)
            rows1[...] = turned(rows1[...])
            if g.square:
                tc.recv(te[1], err.at[3], (g.d, g.ty))
                err[base] = err[2] + err[3]
            else:
                total = err[0]
                for k in range(1, g.n_t):
                    tc.recv(te[k - 1], err.at[k], (g.d, (g.t + g.n_t - k) % g.n_t))
                    total = total + err[k]
                err[base] = total
            zc.send(gec, ec, err.at[base], err.at[base + 1], (g.sib, g.t))

        @pl.when(i == 2)
        def _():
            zc.recv(ec, err.at[base + 1], (g.sib, g.t))
            err[base + 2] = err[base] + err[base + 1]
            for k in range(1, C):
                zc.send(gez, ez[k - 1], err.at[base + 2], err.at[base + 2 + k], (g.zto(k), g.t))

        for k in range(1, g.n_t):
            pl.when(i == k)(functools.partial(ag.wait, k))
        blk = g.arrive_at(i)
        at = g.rows(blk)
        middle[0:c] += dot(mixt[blk], ga[at])

        @pl.when(i == g.n_t - 1)
        def _():
            zo.sent()
            wa[3] = turned(middle[0:c].astype(BF))
            zscat[3].start()

        go_t = dot(wo_t[...], ga[at], NT).astype(BF).astype(F32)
        mix_t = mixt[blk].astype(F32)
        scaled, dots = [], []
        for h in range(H):
            one_head = go_t[h * HD : (h + 1) * HD] * rinv[blk, h : h + 1, :]
            scaled.append(one_head)
            dots.append(jnp.sum(one_head * mix_t[h * HD : (h + 1) * HD], axis=0, keepdims=True))
        go = jnp.concatenate(scaled, axis=0).T.astype(BF)
        q_blk = q[at]
        for h in range(H):
            gom[h * R : (h + 1) * R] = head_lanes(go, h)
            qm[h * R : (h + 1) * R] = head_lanes(q_blk, h)

        @in_slot(g, n_pic, blk)
        def _(p, index, hi):
            dq = attend_back(g, hi, v, turn, probs[p].at[index], gom, qm, dots, dk, dv).T * HD**-0.5
            q[at] = rotated(dq, cosine[at], -sine[at]).astype(BF)

        pl.when(i == 0)(ag.relay)

        @pl.when(i == 2)
        def _():
            zscat[1].relay(0)
            zscat[1].relay(1)

    @pl.loop(0, g.n_t)
    def _(i):
        at = g.rows(g.leave_at(i))
        kk[at] = rotated(dk[at], cosine[at], -sine[at]).astype(BF)
        v[at] = dv[at].astype(BF)
        partial = dot(q[at], wa[0], NT) + dot(kk[at], wa[1], NT) + dot(v[at], wa[2], NT)

        @pl.when(i < g.n_t - 1)
        def _():
            rs.give(i, partial)

        @pl.when(i == g.n_t - 1)
        def _():
            grad_inputs[...] = partial


    zscat[3].pass_on()
    zscat[1].relay(2)
    zscat[2].relay(0)
    zscat[2].relay(1)
    za.sent()
    for j in range(3):
        wa[j] = dot(rows1[...], qkv[j]).astype(BF)
        zscat[4 + j].start()
    for j in (4, 5, 6):
        zscat[j].meet()
        zscat[j].part(0)
    rs.relay()
    for k in (1, 2):
        for j in (4, 5, 6):
            zscat[j].part(k)
    zscat[2].relay(2)
    zscat[3].relay(0)
    zscat[3].relay(1)
    one, inv = normed(x[...])

    for j, to in enumerate((o_d, o_g, o_u)):
        total_m(j)[...] = zscat[j].total().T if j else zscat[j].total()
        store(total_m(j), to)
    for j in (4, 5, 6):
        zscat[j].relay(0)
    zscat[3].relay(2)
    for j, k in ((4, 2), (5, 2), (4, 1), (6, 2), (5, 1)):
        zscat[j].relay(k)
    for i in range(2):
        for rows, back in rs.take(i, grad_inputs):
            grad_inputs[rows] = cot[rows] + normed_back(one[rows], inv[rows], back)
    store(grad_inputs, o_in)
    zscat[6].relay(1)
    dout_at = acc2.at[1, 0:c, Dn : 2 * Dn] if packed else dout
    dout_at[...] = zscat[3].total().T
    store(dout_at, o_o)
    total = err[base + 2]
    for k in range(1, C):
        zc.recv(ez[k - 1], err.at[base + 2 + k], (g.zfrom(k), g.t))
        total = total + err[base + 2 + k]
    stats[...] = (total * (1.0 / g.D) / tokens)[0:1, 0:1]
    store(stats, o_loss)
    for j, to in enumerate((o_q, o_k, o_v)):
        dattn[j] = zscat[4 + j].total()
        store(dattn.at[j], to)
    for copy in stores:
        copy.wait()
    ag.sent()
    for scat in zscat:
        scat.sent()
    tc.sent(few, err.at[0 : len(te)], (g.sib, g.t))
    for group, n in ((gsib, 1), (gz, C - 1), (gec, 1), (gez, C - 1)):
        zc.sent(group, cnt.at[0:n], (g.sib, g.t))
    assert tc.n <= tr.shape[0] and zc.n <= zr.shape[0] and tc.groups <= ts.shape[0] and zc.groups <= zs.shape[0]


def layer(g, n_pic, args):
    S, R, D, c, f, H, C, Dn = g.S, g.R, g.D, g.c, g.f, g.H, g.C, g.Dn
    sds, V = jax.ShapeDtypeStruct, pltpu.VMEM
    shapes = [(R, D), (R, D), (Dn, c), (Dn, c), (Dn, c), (c, Dn), (f, Dn), (f, Dn), (f, Dn), (1, 1)]
    outs = [sds(s, F32) for s in shapes]
    base = 4 if g.square else g.n_t
    scratch = [V((S, D), BF)] * 4 + [
        V((4, D, c), BF), V((3, D, f), BF), V((3, S, c), BF), V((S, c), BF), V((g.n_t, c, R), BF), V((c, S), BF), V((c, D), BF),
        V((g.n_t // 2, S // 2, H * R), BF), V((g.n_t // 2, S, H * R), BF), V((2, S, max(R, c)), F32), V((H * R, c), BF), V((H * R, c), BF), V((3, S, f), BF),
        V((max(R, c), D), F32), V((R, D), F32), V((8, S), jnp.int32), V((S, 128), jnp.int32), V((g.n_t, 8, R), F32),
        V((2 + C, 8, 128), F32), V((base + 2 + C, 8, 128), F32),
    ]
    scratch += scatter_scratch(g)
    m = weight_scatter_scratch(g, 2, Dn, f)
    d = weight_scatter_scratch(g, 1, f, Dn)
    few = V((1, 16, 128), BF)
    scratch += [V((f, S), BF), V((g.n_dp, f, Dn), BF), d[0], few if in_lanes(g) else V((C - 1, f, Dn), BF), d[2]]
    scratch += [m[0], m[2]] + weight_scatter_scratch(g, 4, Dn, c)
    scratch += [V((R, D), F32), V((R, D), F32), V((3, Dn, c), F32), few if in_lanes(g) else V((c, Dn), F32), few if in_lanes(g) else V((3, f, Dn), F32), V((1, 1), F32)]
    nt = 20 if g.square else 3 * (g.n_t - 1)
    nz = 4 * (2 * C - 1) + 7 * (6 if g.line else C) + 2 * C
    sem = pltpu.SemaphoreType.DMA
    scratch += [V(a.shape, a.dtype) for a in args[8:14]]
    scratch += [sem((3,)), sem((nt,)), sem((15,)), sem((nz,)), sem((20,))]
    whole = pl.BlockSpec(memory_space=pltpu.VMEM)
    specs = [whole] * len(args)
    for k in (1, *range(5, 14)):
        specs[k] = pl.BlockSpec(memory_space=pl.ANY)
    return pl.pallas_call(
        functools.partial(layer_body, g, n_pic),
        name="layer",
        out_shape=outs,
        in_specs=specs,
        out_specs=[pl.BlockSpec(memory_space=pl.ANY)] * len(outs),
        scratch_shapes=scratch,
        compiler_params=pltpu.CompilerParams(collective_id=1, has_side_effects=True, vmem_limit_bytes=VMEM_BYTES),
    )(*args)


def finish_body(n, *refs):
    parts, outs, bufs, come, go = refs[:n], refs[n : 2 * n], refs[2 * n : 3 * n], refs[3 * n], refs[3 * n + 1]
    loads = [pltpu.make_async_copy(a, b, come.at[k]) for k, (a, b) in enumerate(zip(parts, bufs))]
    stores = [pltpu.make_async_copy(a, b, go.at[k]) for k, (a, b) in enumerate(zip(bufs, outs))]
    for copy in loads:
        copy.start()
    for load, store in zip(loads, stores):
        load.wait()
        store.start()
    for copy in stores:
        copy.wait()


def finish(parts):
    anywhere, n = pl.BlockSpec(memory_space=pl.ANY), len(parts)
    return pl.pallas_call(
        functools.partial(finish_body, n),
        name="finish",
        out_shape=[jax.ShapeDtypeStruct(p.shape, F32) for p in parts],
        in_specs=[anywhere] * n,
        out_specs=[anywhere] * n,
        scratch_shapes=[pltpu.VMEM(p.shape, F32) for p in parts] + [pltpu.SemaphoreType.DMA((n,))] * 2,
    )(*parts)


def per_device(n_dp, n_t, inputs, teacher, valid_mask, documents, picture_starts,
               w_query, w_key, w_value, w_out, w_gate, w_up, w_down):
    R, D = inputs.shape
    c, f = w_query.shape[1], w_gate.shape[1]
    g = Geo(n_dp, n_t, R, D, c, f)
    args = (inputs, teacher, valid_mask, documents, picture_starts, w_query, w_key, w_value, w_out, w_gate.T, w_up.T, w_down)
    parts = layer(g, picture_starts.shape[1], (*args, *rotary(g.S, c)))
    out, *grads, gate, up, down, loss = finish(parts)
    return (out, loss.reshape(()), *grads, gate.T, up.T, down)


def solution(mesh):
    rows, pair = P(("dp", "tensor"), None), P("dp", None)
    cut, across = P("dp", "tensor"), P("tensor", "dp")
    return jax.shard_map(
        functools.partial(per_device, mesh.shape["dp"], mesh.shape["tensor"]),
        mesh=mesh,
        in_specs=(rows, rows, pair, pair, pair, cut, cut, cut, across, cut, cut, across),
        out_specs=(rows, P(), rows, cut, cut, cut, across, cut, cut, across),
        check_vma=False,
    )
```
